32 devices in a mesh: rows: 8 (over z, x), lev: 4 (over y, core).
Axes of the slice: x: 2, y: 2, z: 4, core: 2. Of those that a mesh axis runs over, the one named last changes fastest.
Arguments:
- source: float32 [2048, 16, 2048], P('rows', 'lev'), may hold values from -40 to 40
- solid: int32 [256, 16, 32], P('rows', 'lev'), may hold values 0 or 1
- couplings: float32 [17], replicated, may hold values from 2 to 8
Outputs:
- pressure: float32 [2048, 16, 2048], P('rows', 'lev')
The draws below stay inside these ranges and needn't reach their ends.
Inputs may be any that keep to these rules, and one draw needn't show every extreme that they name: Each entry is 0 or 1; 1 marks a block of 8 x 64 cells of one level inside a solid.
All inputs are finite; a program needn't handle non-finite values.
Results may differ from the reference program's by a relative error of at most 0.0001.
Values sent between devices are 32-bit elements; how exact they have to be, the bound alone decides.
A program may use at most 192 MiB of HBM per device.

```python
import math
import jax
import jax.numpy as jnp
from jax import lax

NX = 2048
NY = 2048
BY = 8
BX = 64
NZ = 16


def touch_ends(values, key, low, largest):
    extent = values.shape
    place = [jax.random.randint(jax.random.fold_in(key, axis), (), 0, extent[axis]) for axis in range(len(extent))]
    values = values.at[tuple(place)].set(low)
    longest = extent.index(max(extent))
    place[longest] = (place[longest] + 1) % extent[longest]
    return values.at[tuple(place)].set(largest)


def steps_of(own_key, dims, split, smallest, largest):
    level, own = 1.0, jax.random.fold_in(own_key, 6)
    for axis_at, shards_of in split:
        steps = jnp.exp(jax.random.uniform(jax.random.fold_in(own, axis_at), (shards_of,), jnp.float32, smallest / len(split), largest / len(split)))
        level = level * jnp.repeat(steps, dims[axis_at] // shards_of).reshape([-1 if axis == axis_at else 1 for axis in range(len(dims))])
    return level


def normal_values(key, extent, spread, limit, cuts=(), kind=jnp.bfloat16):
    entries = jax.random.normal(key, extent, jnp.float32) * spread
    if len(cuts) > 0:
        entries = steps_of(key, extent, cuts, -0.22, 0.18) * entries
    return jnp.clip(entries, min=-limit, max=limit).astype(kind)


def setup_inputs(seed: int = 0) -> dict:
    key_of = jax.random.split(jax.random.key(seed), 4)
    return {
        "source": normal_values(key_of[0], (NY, NZ, NX), 8.0, 40.0, ((0, 8), (1, 4)), jnp.float32),
        "solid": touch_ends((jax.random.randint(key_of[1], (NY // BY, NZ, NX // BX), 0, 4) < 1).astype(jnp.int32), jax.random.fold_in(key_of[1], 1), 0, 1),
        "couplings": jnp.clip(jnp.exp(jax.random.uniform(key_of[2], (NZ + 1,), jnp.float32, math.log(2.0), math.log(8.0))), 2.0, 8.0),
    }


full_turn = 2.0 * math.pi

def eigenvalue(length):
    slots = jnp.arange(length, dtype=jnp.int32)
    frequency = jnp.where(slots <= length // 2, slots, slots - length // 2)
    return 2.0 - 2.0 * jnp.cos(frequency.astype(jnp.float32) * (full_turn / length))

def weights_for(length):
    slots = jnp.arange(length, dtype=jnp.int32)
    edge = (slots == 0) | (slots == length // 2)
    return jnp.where(edge, math.sqrt(1.0 / length), math.sqrt(2.0 / length)).astype(jnp.float32)

def forward_last(values):
    length = values.shape[-1]
    half_len = length // 2
    spectral = jnp.fft.rfft(values, axis=-1)
    real_part = jnp.real(spectral)
    imag_part = jnp.imag(spectral)
    packed = jnp.concatenate([real_part[..., :half_len + 1], -imag_part[..., 1:half_len]], -1)
    return (packed * weights_for(length)).astype(jnp.float32)

def inverse_last(packed):
    length = packed.shape[-1]
    half_len = length // 2
    scaled = packed / weights_for(length)
    real_part = scaled[..., :half_len + 1]
    blank = jnp.zeros(packed.shape[:-1] + (1,), jnp.float32)
    imag_part = jnp.concatenate([blank, -scaled[..., half_len + 1:], blank], -1)
    return jnp.fft.irfft(lax.complex(real_part, imag_part), n=length, axis=-1).astype(jnp.float32)

def reference(source, solid, couplings):
    keep_cells = (1 - solid).astype(jnp.float32)
    horizontal = eigenvalue(NY)[:, None] + eigenvalue(NX)[None, :]
    zero_plane = jnp.zeros((NY, NX), jnp.float32)

    def forward(carry, level):
        ratio_prev, partial_prev = carry
        cells = lax.dynamic_index_in_dim(source, level, 1, keepdims=False)
        keep_level = lax.dynamic_index_in_dim(keep_cells, level, 1, keepdims=False)
        cells = (cells.reshape(NY // BY, BY, NX // BX, BX) * keep_level[:, None, :, None]).reshape(NY, NX)
        spectral = forward_last(forward_last(cells).T).T
        lower_w = couplings[level]
        upper_w = couplings[level + 1]
        inverse = 1.0 / (horizontal + lower_w + upper_w - lower_w * ratio_prev)
        ratio = upper_w * inverse
        partial_value = (spectral + lower_w * partial_prev) * inverse
        return ((ratio, partial_value), (ratio, partial_value))
    unused, (ratios, partials) = lax.scan(forward, (zero_plane, zero_plane), jnp.arange(NZ, dtype=jnp.int32))

    def backward(upper_values, slices):
        ratio, partial_value = slices
        current = partial_value + ratio * upper_values
        cells = inverse_last(inverse_last(current.T).T)
        return (current, cells)
    unused, levels = lax.scan(backward, zero_plane, (ratios, partials), reverse=True)
    return jnp.moveaxis(levels, 0, 1)
```

```python
import functools
import math

import numpy as np

import jax
import jax.numpy as jnp
from jax import lax
from jax.experimental import pallas as pl
from jax.experimental.pallas import tpu as pltpu
from jax.sharding import PartitionSpec as P

BY = 8
BX = 64
PARTS = 16
VMEM_BYTES = 48 * 1024 * 1024

f32 = jnp.float32
bf16 = jnp.bfloat16


def split_host(table):
    high = table.astype(np.float32).astype(jnp.bfloat16)
    low = (table - high.astype(np.float64)).astype(np.float32).astype(jnp.bfloat16)
    return high, low


def split(values):
    high = values.astype(bf16)
    low = (values - high.astype(f32)).astype(bf16)
    return high, low


def split_outside(values):
    high = lax.reduce_precision(values, 8, 7)
    return high.astype(bf16), (values - high).astype(bf16)


def dot3(left, right):
    dot = functools.partial(jnp.dot, preferred_element_type=f32)
    return dot(left[0], right[0]) + (dot(left[0], right[1]) + dot(left[1], right[0]))


@functools.lru_cache(None)
def x_tables(length):
    width = length // PARTS
    half = PARTS // 2
    place = np.arange(width)
    blocks = np.zeros((half, 2 * width, 2 * width))
    slots = np.zeros((half, 2 * width))
    inner = math.sqrt(2.0 / length)
    edge = math.sqrt(1.0 / length)

    def angle(freq):
        return 2.0 * math.pi * (np.outer(place, freq) % length) / length

    low = PARTS * np.arange(width // 2 + 1)
    weight = np.where((low == 0) | (low == length // 2), edge, inner)
    cosines = np.cos(angle(low)) * weight
    sines = np.sin(angle(low[1:-1])) * inner
    blocks[0, :width, :width] = np.concatenate([cosines, sines], 1)
    slots[0, :width] = np.concatenate([low, low[1:-1]])
    middle = half + PARTS * np.arange(width // 2)
    blocks[0, width:, width:] = np.concatenate([np.cos(angle(middle)), np.sin(angle(middle))], 1) * inner
    slots[0, width:] = np.concatenate([middle, middle])
    for first in range(1, half):
        freq = first + PARTS * np.arange(width)
        turn = angle(freq)
        cosines, sines = np.cos(turn) * inner, np.sin(turn) * inner
        blocks[first] = np.block([[cosines, -sines], [sines, cosines]])
        slots[first] = np.concatenate([freq, freq])
    eigen = 4.0 * np.sin(math.pi * slots.reshape(-1) / length) ** 2
    return blocks, eigen.astype(np.float32)


def turn(index):
    return math.cos(2.0 * math.pi * index / PARTS), math.sin(2.0 * math.pi * index / PARTS)


def stage(x):
    s = [x[b] + x[b + 8] for b in range(8)]
    d = [x[b] - x[b + 8] for b in range(8)]
    out = [None] * 8
    minus = [d[b] - d[8 - b] for b in range(1, 4)]
    plus = [d[b] + d[8 - b] for b in range(1, 4)]
    for first in (1, 3, 5, 7):
        real = d[0]
        imag = d[4] * (-turn(4 * first)[1])
        for b in (1, 2, 3):
            cosine, sine = turn(b * first)
            real = real + minus[b - 1] * cosine
            imag = imag - plus[b - 1] * sine
        out[first] = (real, imag)
    ss = [s[b] + s[b + 4] for b in range(4)]
    sd = [s[b] - s[b + 4] for b in range(4)]
    root = math.sqrt(0.5)
    m = (sd[1] - sd[3]) * root
    p = (sd[1] + sd[3]) * root
    out[2] = (sd[0] + m, -p - sd[2])
    out[6] = (sd[0] - m, sd[2] - p)
    out[4] = (ss[0] - ss[2], ss[3] - ss[1])
    even, odd = ss[0] + ss[2], ss[1] + ss[3]
    out[0] = (even + odd, even - odd)
    return out


def unstage(y):
    root = math.sqrt(0.5)
    even, odd = y[0][0] + y[0][1], y[0][0] - y[0][1]
    ss = [even + y[4][0], odd - y[4][1], even - y[4][0], odd + y[4][1]]
    m = (y[2][0] - y[6][0]) * root
    p = (y[2][1] + y[6][1]) * root
    sd = [y[2][0] + y[6][0], m - p, y[6][1] - y[2][1], -m - p]
    s = [ss[b] + sd[b] for b in range(4)] + [ss[b] - sd[b] for b in range(4)]
    d = [None] * 8
    d[0] = (y[1][0] + y[3][0]) + (y[5][0] + y[7][0])
    d[4] = (y[3][1] - y[1][1]) + (y[7][1] - y[5][1])
    for b in (1, 2, 3):
        real = None
        imag = None
        for first in (1, 3, 5, 7):
            cosine, sine = turn(b * first)
            term, other = y[first][0] * cosine, y[first][1] * sine
            real = term if real is None else real + term
            imag = other if imag is None else imag + other
        d[b] = real - imag
        d[8 - b] = -real - imag
    return [s[b] + d[b] for b in range(8)] + [s[b] - d[b] for b in range(8)]


def half_place():
    group = lax.axis_size("lev") // 2
    me = lax.axis_index("lev")
    return me // group, me % group


def block_of(index, share, length):
    blocks = PARTS // 2
    _, own = half_place()
    return lax.rem(index + own * (share * blocks // length), blocks)


def forward_kernel(x_ref, keep_ref, spread_ref, high_ref, low_ref, *rest):
    out_refs, (kept, mixed) = rest[:-2], rest[-2:]
    rows, levels, length = x_ref.shape
    width = length // PARTS
    share = out_refs[0].shape[2]
    kept[...] = jnp.dot(keep_ref[...], spread_ref[...], preferred_element_type=f32)

    def group(index, unused):
        row = pl.multiple_of(index * BY, BY)
        for level in range(levels):
            mask = kept[pl.ds(index * levels + level, 1), :]
            x = [
                x_ref[pl.ds(row, BY), level, pl.ds(b * width, width)] * mask[:, b * width : (b + 1) * width]
                for b in range(PARTS)
            ]
            base = pl.multiple_of(level * rows + row, BY)
            for block, (real, imag) in enumerate(stage(x)):
                mixed[block, pl.ds(base, BY), :width] = real
                mixed[block, pl.ds(base, BY), width:] = imag
        return unused

    lax.fori_loop(0, rows // BY, group, 0)
    for index in range(PARTS // 2):
        block = block_of(index, share, length)
        product = dot3(split(mixed[block]), (high_ref[block], low_ref[block]))
        target, offset = divmod(2 * index * width, share)
        out_refs[target][:, :, offset : offset + 2 * width] = product.reshape(levels, rows, 2 * width)


def backward_kernel(*refs):
    x_refs, (high_ref, low_ref, out_ref, mixed) = refs[:-4], refs[-4:]
    rows, levels, length = out_ref.shape
    width = length // PARTS
    share = x_refs[0].shape[2]
    for index in range(PARTS // 2):
        block = block_of(index, share, length)
        source, offset = divmod(2 * index * width, share)
        values = split(x_refs[source][:, :, offset : offset + 2 * width].reshape(levels * rows, 2 * width))
        mixed[block] = dot3(values, (high_ref[block], low_ref[block]))

    def group(index, unused):
        row = pl.multiple_of(index * BY, BY)
        for level in range(levels):
            base = pl.multiple_of(level * rows + row, BY)
            y = [
                (mixed[block, pl.ds(base, BY), :width], mixed[block, pl.ds(base, BY), width:])
                for block in range(PARTS // 2)
            ]
            for b, value in enumerate(unstage(y)):
                out_ref[pl.ds(row, BY), level, pl.ds(b * width, width)] = value
        return unused

    lax.fori_loop(0, rows // BY, group, 0)


def eigen_kernel(start_ref, out_ref, *, sizes, top):
    lanes = start_ref.shape[1]
    lane = lax.broadcasted_iota(jnp.int32, (1, lanes), 1)
    in_first = lane < sizes[0]
    local = jnp.where(in_first, lane, lane - sizes[0])
    count = jnp.where(in_first, sizes[0], sizes[1])

    def rotate(values, parity):
        is_left = local % 2 == parity
        alone = (lane >= sum(sizes)) | (is_left & (local == count - 1)) | (jnp.logical_not(is_left) & (local == 0))
        partner = jnp.where(is_left, pltpu.roll(values, lanes - 1, 1), pltpu.roll(values, 1, 1))
        head = values[:top]
        head_partner = partner[:top]
        own = jnp.sum(head * head, axis=0, keepdims=True)
        other = jnp.sum(head_partner * head_partner, axis=0, keepdims=True)
        cross = jnp.sum(head * head_partner, axis=0, keepdims=True)
        delta = other - own
        sign = jnp.where((delta > 0) | ((delta == 0) & is_left), 1.0, -1.0)
        bottom = jnp.abs(delta) + jnp.sqrt(delta * delta + 4.0 * cross * cross)
        tangent = 2.0 * cross * sign / jnp.maximum(bottom, 1e-30)
        cosine = 1.0 / jnp.sqrt(1.0 + tangent * tangent)
        sine = cosine * tangent
        angle = jnp.where(alone, 0.0, jnp.abs(cross) * lax.rsqrt(jnp.maximum(own * other, 1e-30)))
        return jnp.where(alone, values, cosine * partner + sine * values), angle

    def sweep(carry):
        values, done, unused = carry
        worst = jnp.zeros((1, lanes), f32)
        for step in range(max(sizes)):
            values, angle = rotate(values, step % 2)
            worst = jnp.maximum(worst, angle)
        return values, done + 1, jnp.max(worst)

    def going(carry):
        return (carry[2] > 1e-6) & (carry[1] < 20)

    values, _, _ = lax.while_loop(going, sweep, (start_ref[...], jnp.int32(0), jnp.float32(1.0)))
    out_ref[...] = values


def eigen(weights):
    sizes = tuple(weight.shape[0] - 1 for weight in weights)
    top = -(-(sizes[0] + 1) // 8) * 8
    low = -(-sizes[0] // 8) * 8
    lanes = 128
    columns = []
    turns = []
    for size, weight in zip(sizes, weights):
        differences = np.zeros((top, size), np.float32)
        differences[np.arange(size), np.arange(size)] = 1.0
        differences[np.arange(size) + 1, np.arange(size)] = -1.0
        columns.append(differences * jnp.pad(jnp.sqrt(weight), (0, top - size - 1))[:, None])
        turns.append(np.eye(low, size, dtype=np.float32))
    start = jnp.concatenate([jnp.concatenate(columns, 1), jnp.asarray(np.concatenate(turns, 1))], 0)
    start = jnp.pad(start, ((0, 0), (0, lanes - sum(sizes))))
    turned = pl.pallas_call(
        functools.partial(eigen_kernel, sizes=sizes, top=top),
        out_shape=jax.ShapeDtypeStruct(start.shape, f32),
        name="eigen",
    )(start)
    found = []
    first = 0
    for size in sizes:
        part = turned[:, first : first + size]
        found.append((jnp.sum(part[:top] ** 2, axis=0), part[top : top + size]))
        first += size
    return found


def to_modes_kernel(*refs):
    x_refs, (high_ref, low_ref, ratio_ref, modes_ref, ends_ref, power) = refs[:-6], refs[-6:]
    modes, share = ratio_ref.shape

    @pl.when(pl.program_id(0) == 0)
    def _():
        ends_ref[...] = jnp.zeros(ends_ref.shape, f32)
        power[...] = jnp.ones(power.shape, f32)

    values = jnp.concatenate([x_ref[...].reshape(-1, share) for x_ref in x_refs], 0)
    modes_ref[...] = dot3((high_ref[...], low_ref[...]), split(values))
    ratio = ratio_ref[...]
    first, last, scale = ends_ref[0], ends_ref[1], power[...]
    for row in range(modes_ref.shape[0] // modes):
        current = modes_ref[row * modes : (row + 1) * modes, :]
        first = first * ratio + current
        last = last + scale * current
        scale = scale * ratio
    ends_ref[0] = first
    ends_ref[1] = last
    power[...] = scale


def two_way(rows, ratio_ref, edge_ref, held, chunk, carry, source, finish):
    step = pl.program_id(0)
    steps = pl.num_programs(0) // 2
    modes = ratio_ref.shape[0]
    ratio = ratio_ref[...]

    @pl.when(step == 0)
    def _():
        carry[...] = edge_ref[0]

    @pl.when(step == steps)
    def _():
        carry[...] = edge_ref[1]

    @pl.when(step < steps)
    def _():
        base = pl.multiple_of(step * rows * modes, rows * modes)
        value = carry[...]
        for row in range(rows):
            value = value * ratio + source(row)
            held[pl.ds(base + row * modes, modes), :] = value
        carry[...] = value

    @pl.when(step >= steps)
    def _():
        base = pl.multiple_of((2 * steps - 1 - step) * rows * modes, rows * modes)
        value = carry[...]
        for row in reversed(range(rows)):
            value = (value + held[pl.ds(base + row * modes, modes), :]) * ratio
            chunk[row * modes : (row + 1) * modes, :] = value
        carry[...] = value
        finish(split(chunk[...]))


def interface_kernel(modes_ref, high_ref, low_ref, ratio_ref, edge_ref, keep_ref, send_ref, held, chunk, carry, line):
    modes = ratio_ref.shape[0]
    piece = keep_ref.shape[1]
    half, _ = half_place()

    def finish(values):
        line[...] = dot3((high_ref[...], low_ref[...]), values)
        keep_ref[...] = line[:, pl.ds(pl.multiple_of(half * piece, piece), piece)]
        send_ref[...] = line[:, pl.ds(pl.multiple_of((1 - half) * piece, piece), piece)]

    two_way(
        keep_ref.shape[0], ratio_ref, edge_ref, held, chunk, carry,
        lambda row: modes_ref[row * modes : (row + 1) * modes, :], finish,
    )


def plane_ends(plane_ref, ratio_ref, ends_ref, weight):
    rows = plane_ref.shape[0]
    shape = ratio_ref.shape
    ratio = ratio_ref[...]

    def group(index, carry):
        first, last, scale = carry
        lines = plane_ref[pl.ds(pl.multiple_of(index * BY, BY), BY), :]
        for row in range(BY):
            current = jnp.broadcast_to(lines[row : row + 1], shape)
            first = first * ratio + current
            last = last + scale * current
            scale = scale * ratio
        return first, last, scale

    zero = jnp.zeros(shape, f32)
    first, last, _ = lax.fori_loop(0, rows // BY, group, (zero, zero, jnp.ones(shape, f32)))
    ends_ref[0] = first if weight is None else first * weight
    ends_ref[1] = last if weight is None else last * weight


def sum_kernel(own_ref, other_ref, ratio_ref, plane_ref, ends_ref):
    plane_ref[...] = own_ref[...] + other_ref[...]
    plane_ends(plane_ref, ratio_ref, ends_ref, None)


def join_kernel(own_ref, other_ref, ratio_ref, weight_ref, plane_ref, ends_ref):
    half, _ = half_place()
    piece = own_ref.shape[1]
    plane_ref[:, pl.ds(pl.multiple_of(half * piece, piece), piece)] = own_ref[...]
    plane_ref[:, pl.ds(pl.multiple_of((1 - half) * piece, piece), piece)] = other_ref[...]
    plane_ends(plane_ref, ratio_ref, ends_ref, weight_ref[...])


def couple_kernel(
    plane_ref, again_ref, high_ref, low_ref, ratio_ref, edge_ref, strength_ref, out_ref, held, chunk, carry
):
    shape = ratio_ref.shape

    def finish(values):
        out_ref[...] = dot3((high_ref[...], low_ref[...]), values) + again_ref[...] * strength_ref[...]

    two_way(
        out_ref.shape[0], ratio_ref, edge_ref, held, chunk, carry,
        lambda row: jnp.broadcast_to(plane_ref[row : row + 1, :], shape), finish,
    )


def from_modes_kernel(modes_ref, plane_ref, weight_ref, high_ref, low_ref, ratio_ref, edge_ref, *rest):
    out_refs, (held, chunk, carry) = rest[:-3], rest[-3:]
    modes, share = ratio_ref.shape
    levels, rows, _ = out_refs[0].shape
    weight = weight_ref[...]

    def finish(values):
        result = dot3((high_ref[...], low_ref[...]), values).reshape(len(out_refs), levels, rows, share)
        for index, out_ref in enumerate(out_refs):
            out_ref[...] = result[index]

    two_way(
        rows, ratio_ref, edge_ref, held, chunk, carry,
        lambda row: modes_ref[row * modes : (row + 1) * modes, :] + weight * plane_ref[row : row + 1, :], finish,
    )


def params():
    return pltpu.CompilerParams(vmem_limit_bytes=VMEM_BYTES)


def cost(flops, moved):
    return pl.CostEstimate(flops=int(flops), bytes_accessed=int(moved), transcendentals=0)


def whole(shape):
    return pl.BlockSpec(shape, lambda *index: (0,) * len(shape))


def struct(*shape):
    return jax.ShapeDtypeStruct(shape, f32)


def decay(values, eigen_x):
    sigma = values[:, None] + eigen_x[None, :]
    return 1.0 / (1.0 + 0.5 * sigma + jnp.sqrt(sigma + 0.25 * sigma * sigma))


def edges(ends, ratio, row_count):
    row_devices = lax.axis_size("rows")
    everyone = lax.all_gather(ends, "rows")
    me = lax.axis_index("rows")
    across = ratio**row_count
    closing = 1.0 / (1.0 - across**row_devices)

    def around(which, direction):
        total = jnp.zeros(ratio.shape, f32)
        for hop in range(row_devices, 0, -1):
            place = jnp.mod(me + direction * hop, row_devices)
            total = total * across + lax.dynamic_index_in_dim(everyone, place, 0, keepdims=False)[which]
        return total * closing

    before = around(0, -1)
    after = around(1, 1)
    last = ends[0] + across * before
    above = ratio * (ratio * last + after) / (1.0 - ratio * ratio)
    return jnp.stack([before, above])


def body(source, solid, couplings):
    row_count, levels, length = source.shape
    lev_devices = lax.axis_size("lev")
    group = lev_devices // 2
    half, own = half_place()
    share = length // group
    piece = share // 2
    width = length // PARTS
    half_levels = levels * group
    all_levels = 2 * half_levels
    tile = 64 if row_count % 64 == 0 else BY
    size = source.size

    def passed(value, shift):
        pairs = [
            (side * group + place, side * group + (place + shift) % group) for side in range(2) for place in range(group)
        ]
        return lax.ppermute(value, "lev", pairs)

    def across_halves(value):
        return lax.ppermute(value, "lev", [(place, (place + group) % lev_devices) for place in range(lev_devices)])

    blocks, eigen_x = x_tables(length)
    high, low = split_host(blocks)
    back_high, back_low = split_host(np.swapaxes(blocks, 1, 2))
    keep = (1 - solid).astype(bf16).reshape(-1, length // BX)
    spread = (np.arange(length)[None, :] // BX == np.arange(length // BX)[:, None]).astype(jnp.bfloat16)
    groups = tile // BY * levels
    table = whole(blocks.shape)
    part_spec = pl.BlockSpec((levels, tile, share), lambda i: (0, i, 0))
    field_spec = pl.BlockSpec((tile, levels, length), lambda i: (i, 0, 0))
    mixed = pltpu.VMEM((PARTS // 2, levels * tile, 2 * width), f32)
    spectral = pl.pallas_call(
        forward_kernel,
        grid=(row_count // tile,),
        in_specs=[field_spec, pl.BlockSpec((groups, length // BX), lambda i: (i, 0)), whole(spread.shape), table, table],
        out_specs=[part_spec] * group,
        out_shape=[struct(levels, row_count, share)] * group,
        scratch_shapes=[pltpu.VMEM((groups, length), f32), mixed],
        compiler_params=params(),
        cost_estimate=cost(6 * size * 2 * width, 8 * size),
        name="forward_x",
    )(source, keep, spread, high, low)
    sections = [spectral[0]] + [passed(spectral[shift], shift) for shift in range(1, group)]

    middle = couplings[half_levels]
    edge_at = jnp.where(half == 0, half_levels, 0)
    mine = lax.dynamic_slice_in_dim(couplings, half * half_levels, half_levels + 1)
    mine = jnp.where(jnp.arange(half_levels + 1) == edge_at, 2.0 * middle, mine)
    (full_values, full_vectors), (values, vectors) = eigen([couplings, mine])
    edge_weight = jnp.where(half == 0, vectors[half_levels - 1], vectors[0])
    jump = middle * (full_vectors[half_levels - 1] + full_vectors[half_levels])
    eigen_x = lax.dynamic_slice_in_dim(jnp.asarray(eigen_x), own * share, share)
    ratio = decay(values, eigen_x)
    full_ratio = decay(full_values, lax.dynamic_slice_in_dim(eigen_x, half * piece, piece))

    chunk = max(BY, 256 // half_levels)
    thin = max(BY, 256 // all_levels)
    rows = chunk * half_levels
    plane_rows = thin * all_levels
    order = jnp.mod(own - jnp.arange(group), group)
    turned = vectors.reshape(group, levels, half_levels)[order].reshape(half_levels, half_levels)
    eye = jnp.eye(chunk, dtype=f32)
    to_modes = (eye[:, None, None, :] * turned.T[None, :, :, None]).reshape(rows, rows)
    from_modes = (eye[None, :, :, None] * turned[:, None, None, :]).reshape(rows, rows)
    to_edge = (eye[:, :, None] * edge_weight).reshape(chunk, rows)
    to_jump = (jnp.eye(thin, dtype=f32)[:, :, None] * (jump * jump)).reshape(thin, plane_rows)

    steps = row_count // chunk
    plane_steps = row_count // thin
    shape = (half_levels, share)
    plane_shape = (all_levels, piece)
    modes_shape = struct(row_count * half_levels, share)
    section_spec = pl.BlockSpec((levels, chunk, share), lambda i: (0, i, 0))

    def ahead(count):
        return lambda i: (jnp.minimum(i, count - 1), 0)

    def behind(count):
        return lambda i: (jnp.minimum(2 * count - 1 - i, count - 1), 0)

    def scratch(rows, shape):
        return [pltpu.VMEM((row_count * shape[0], shape[1]), f32), pltpu.VMEM((rows, shape[1]), f32), pltpu.VMEM(shape, f32)]

    modes, ends = pl.pallas_call(
        to_modes_kernel,
        grid=(steps,),
        in_specs=[section_spec] * group + [whole((rows, rows))] * 2 + [whole(shape)],
        out_specs=[pl.BlockSpec((rows, share), lambda i: (i, 0)), whole((2,) + shape)],
        out_shape=[modes_shape, struct(2, *shape)],
        scratch_shapes=[pltpu.VMEM(shape, f32)],
        compiler_params=params(),
        cost_estimate=cost(6 * size * rows, 8 * size),
        name="to_modes",
    )(*sections, *split_outside(to_modes), ratio)
    edge = edges(ends, ratio, row_count)

    kept, sent = pl.pallas_call(
        interface_kernel,
        grid=(2 * steps,),
        in_specs=[pl.BlockSpec((rows, share), ahead(steps))] + [whole((chunk, rows))] * 2 + [whole(shape), whole((2,) + shape)],
        out_specs=[pl.BlockSpec((chunk, piece), behind(steps))] * 2,
        out_shape=[struct(row_count, piece)] * 2,
        scratch_shapes=scratch(rows, shape) + [pltpu.VMEM((chunk, share), f32)],
        compiler_params=params(),
        cost_estimate=cost(6 * size * chunk, 5 * size),
        name="interface",
    )(modes, *split_outside(to_edge), ratio, edge)

    plane, plane_ends = pl.pallas_call(
        sum_kernel,
        out_shape=[struct(row_count, piece), struct(2, *plane_shape)],
        compiler_params=params(),
        name="plane_sum",
    )(kept, across_halves(sent), full_ratio)
    plane_edge = edges(plane_ends, full_ratio, row_count)

    moved = pl.pallas_call(
        couple_kernel,
        grid=(2 * plane_steps,),
        in_specs=[
            pl.BlockSpec((thin, piece), ahead(plane_steps)),
            pl.BlockSpec((thin, piece), behind(plane_steps)),
            whole((thin, plane_rows)),
            whole((thin, plane_rows)),
            whole(plane_shape),
            whole((2,) + plane_shape),
            whole((1, piece)),
        ],
        out_specs=pl.BlockSpec((thin, piece), behind(plane_steps)),
        out_shape=struct(row_count, piece),
        scratch_shapes=scratch(plane_rows, plane_shape),
        compiler_params=params(),
        cost_estimate=cost(6 * size * thin, 2 * size),
        name="couple",
    )(plane, plane, *split_outside(to_jump), full_ratio, plane_edge, jnp.full((1, piece), middle))

    weight = jnp.broadcast_to(edge_weight[:, None], shape)
    joined, joined_ends = pl.pallas_call(
        join_kernel,
        out_shape=[struct(row_count, share), struct(2, *shape)],
        compiler_params=params(),
        name="plane_join",
    )(moved, across_halves(moved), ratio, weight)
    edge = edge + edges(joined_ends, ratio, row_count)

    solved = pl.pallas_call(
        from_modes_kernel,
        grid=(2 * steps,),
        in_specs=[pl.BlockSpec((rows, share), ahead(steps)), pl.BlockSpec((chunk, share), ahead(steps)), whole(shape)]
        + [whole((rows, rows))] * 2
        + [whole(shape), whole((2,) + shape)],
        out_specs=[pl.BlockSpec((levels, chunk, share), lambda i: (0,) + behind(steps)(i))] * group,
        out_shape=[struct(levels, row_count, share)] * group,
        scratch_shapes=scratch(rows, shape),
        compiler_params=params(),
        cost_estimate=cost(6 * size * rows, 8 * size),
        name="from_modes",
    )(modes, joined, weight, *split_outside(from_modes), ratio, edge)
    returned = [solved[0]] + [passed(solved[shift], group - shift) for shift in range(1, group)]
    return pl.pallas_call(
        backward_kernel,
        grid=(row_count // tile,),
        in_specs=[part_spec] * group + [table, table],
        out_specs=field_spec,
        out_shape=struct(*source.shape),
        scratch_shapes=[mixed],
        compiler_params=params(),
        cost_estimate=cost(6 * size * 2 * width, 8 * size),
        name="backward_x",
    )(*returned, back_high, back_low)


def solution(mesh):
    return jax.shard_map(
        body,
        mesh=mesh,
        in_specs=(P("rows", "lev", None), P("rows", "lev", None), P()),
        out_specs=P("rows", "lev", None),
        check_vma=False,
    )
```

```python
import functools
import math

import numpy as np

import jax
import jax.numpy as jnp
from jax import lax
from jax.experimental import pallas as pl
from jax.experimental.pallas import tpu as pltpu
from jax.sharding import PartitionSpec as P

BY = 8
BX = 64
PARTS = 16
VMEM_BYTES = 48 * 1024 * 1024

f32 = jnp.float32
bf16 = jnp.bfloat16


def split(values):
    high = values.astype(bf16)
    low = (values - high.astype(f32)).astype(bf16)
    return high, low


def split_outside(values):
    high = lax.reduce_precision(values, 8, 7)
    return high.astype(bf16), (values - high).astype(bf16)


def dot3(left, right):
    dot = functools.partial(jnp.dot, preferred_element_type=f32)
    return dot(left[0], right[0]) + (dot(left[0], right[1]) + dot(left[1], right[0]))


@functools.lru_cache(None)
def x_tables(length):
    width = length // PARTS
    half = PARTS // 2
    place = np.arange(width)
    blocks = np.zeros((half, 2 * width, 2 * width))
    slots = np.zeros((half, 2 * width))
    inner = math.sqrt(2.0 / length)
    edge = math.sqrt(1.0 / length)

    def angle(freq):
        return 2.0 * math.pi * (np.outer(place, freq) % length) / length

    low = PARTS * np.arange(width // 2 + 1)
    weight = np.where((low == 0) | (low == length // 2), edge, inner)
    cosines = np.cos(angle(low)) * weight
    sines = np.sin(angle(low[1:-1])) * inner
    blocks[0, :width, :width] = np.concatenate([cosines, sines], 1)
    slots[0, :width] = np.concatenate([low, low[1:-1]])
    middle = half + PARTS * np.arange(width // 2)
    blocks[0, width:, width:] = np.concatenate([np.cos(angle(middle)), np.sin(angle(middle))], 1) * inner
    slots[0, width:] = np.concatenate([middle, middle])
    for first in range(1, half):
        freq = first + PARTS * np.arange(width)
        turn = angle(freq)
        cosines, sines = np.cos(turn) * inner, np.sin(turn) * inner
        blocks[first] = np.block([[cosines, -sines], [sines, cosines]])
        slots[first] = np.concatenate([freq, freq])
    eigen = 4.0 * np.sin(math.pi * slots.reshape(-1) / length) ** 2
    return blocks, eigen.astype(np.float32)


def turn(index):
    return math.cos(2.0 * math.pi * index / PARTS), math.sin(2.0 * math.pi * index / PARTS)


def stage(x):
    s = [x[b] + x[b + 8] for b in range(8)]
    d = [x[b] - x[b + 8] for b in range(8)]
    out = [None] * 8
    minus = [d[b] - d[8 - b] for b in range(1, 4)]
    plus = [d[b] + d[8 - b] for b in range(1, 4)]
    for first in (1, 3, 5, 7):
        real = d[0]
        imag = d[4] * (-turn(4 * first)[1])
        for b in (1, 2, 3):
            cosine, sine = turn(b * first)
            real = real + minus[b - 1] * cosine
            imag = imag - plus[b - 1] * sine
        out[first] = (real, imag)
    ss = [s[b] + s[b + 4] for b in range(4)]
    sd = [s[b] - s[b + 4] for b in range(4)]
    root = math.sqrt(0.5)
    m = (sd[1] - sd[3]) * root
    p = (sd[1] + sd[3]) * root
    out[2] = (sd[0] + m, -p - sd[2])
    out[6] = (sd[0] - m, sd[2] - p)
    out[4] = (ss[0] - ss[2], ss[3] - ss[1])
    even, odd = ss[0] + ss[2], ss[1] + ss[3]
    out[0] = (even + odd, even - odd)
    return out


def unstage(y):
    root = math.sqrt(0.5)
    even, odd = y[0][0] + y[0][1], y[0][0] - y[0][1]
    ss = [even + y[4][0], odd - y[4][1], even - y[4][0], odd + y[4][1]]
    m = (y[2][0] - y[6][0]) * root
    p = (y[2][1] + y[6][1]) * root
    sd = [y[2][0] + y[6][0], m - p, y[6][1] - y[2][1], -m - p]
    s = [ss[b] + sd[b] for b in range(4)] + [ss[b] - sd[b] for b in range(4)]
    d = [None] * 8
    d[0] = (y[1][0] + y[3][0]) + (y[5][0] + y[7][0])
    d[4] = (y[3][1] - y[1][1]) + (y[7][1] - y[5][1])
    for b in (1, 2, 3):
        real = None
        imag = None
        for first in (1, 3, 5, 7):
            cosine, sine = turn(b * first)
            term, other = y[first][0] * cosine, y[first][1] * sine
            real = term if real is None else real + term
            imag = other if imag is None else imag + other
        d[b] = real - imag
        d[8 - b] = -real - imag
    return [s[b] + d[b] for b in range(8)] + [s[b] - d[b] for b in range(8)]


def half_place():
    group = lax.axis_size("lev") // 2
    me = lax.axis_index("lev")
    return me // group, me % group


def block_of(index, share, length):
    blocks = PARTS // 2
    _, own = half_place()
    return lax.rem(index + own * (share * blocks // length), blocks)


def keep_split(table_ref, high_ref, low_ref):
    @pl.when(pl.program_id(0) == 0)
    def _():
        for block in range(table_ref.shape[0]):
            high_ref[block], low_ref[block] = split(table_ref[block])


def forward_kernel(x_ref, keep_ref, table_ref, *rest):
    out_refs, (kept, mixed, high_ref, low_ref) = rest[:-4], rest[-4:]
    rows, levels, length = x_ref.shape
    width = length // PARTS
    share = out_refs[0].shape[1]
    pair = 8 // levels
    keep_split(table_ref, high_ref, low_ref)
    shape = (length // BX, length)
    first = lax.broadcasted_iota(jnp.int32, shape, 0) * BX
    lane = lax.broadcasted_iota(jnp.int32, shape, 1)
    spread = jnp.where((lane >= first) & (lane < first + BX), 1.0, 0.0).astype(bf16)
    kept[...] = jnp.dot(keep_ref[...], spread, preferred_element_type=f32)

    def group(index, unused):
        mask = kept[pl.ds(pl.multiple_of(index * 8, 8), 8), :]
        for part in range(BY // pair):
            row = index * BY + part * pair
            x = [
                x_ref[pl.ds(row, pair), :, pl.ds(b * width, width)].reshape(8, width)
                * mask[:, b * width : (b + 1) * width]
                for b in range(PARTS)
            ]
            base = pl.multiple_of(row * levels, 8)
            for block, (real, imag) in enumerate(stage(x)):
                mixed[block, pl.ds(base, 8), :width] = real
                mixed[block, pl.ds(base, 8), width:] = imag
        return unused

    lax.fori_loop(0, rows // BY, group, 0)
    for index in range(PARTS // 2):
        block = block_of(index, share, length)
        product = dot3(split(mixed[block]), (high_ref[block], low_ref[block]))
        target, offset = divmod(2 * index * width, share)
        out_refs[target][:, offset : offset + 2 * width] = product


def backward_kernel(*refs):
    x_refs, (table_ref, out_ref, mixed, high_ref, low_ref) = refs[:-5], refs[-5:]
    rows, levels, length = out_ref.shape
    width = length // PARTS
    share = x_refs[0].shape[1]
    pair = 8 // levels
    keep_split(table_ref, high_ref, low_ref)
    for index in range(PARTS // 2):
        block = block_of(index, share, length)
        source, offset = divmod(2 * index * width, share)
        values = split(x_refs[source][:, offset : offset + 2 * width])
        mixed[block] = dot3(values, (high_ref[block], low_ref[block]))

    def group(index, unused):
        row = index * pair
        base = pl.multiple_of(index * 8, 8)
        y = [
            (mixed[block, pl.ds(base, 8), :width], mixed[block, pl.ds(base, 8), width:])
            for block in range(PARTS // 2)
        ]
        for b, value in enumerate(unstage(y)):
            out_ref[pl.ds(row, pair), :, pl.ds(b * width, width)] = value.reshape(pair, levels, width)
        return unused

    lax.fori_loop(0, rows // pair, group, 0, unroll=4)


def eigen_kernel(start_ref, out_ref, *, sizes, top):
    lanes = start_ref.shape[1]
    lane = lax.broadcasted_iota(jnp.int32, (1, lanes), 1)
    in_first = lane < sizes[0]
    local = jnp.where(in_first, lane, lane - sizes[0])
    count = jnp.where(in_first, sizes[0], sizes[1])

    def rotate(values, parity):
        is_left = local % 2 == parity
        alone = (lane >= sum(sizes)) | (is_left & (local == count - 1)) | (jnp.logical_not(is_left) & (local == 0))
        partner = jnp.where(is_left, pltpu.roll(values, lanes - 1, 1), pltpu.roll(values, 1, 1))
        head = values[:top]
        head_partner = partner[:top]
        own = jnp.sum(head * head, axis=0, keepdims=True)
        other = jnp.sum(head_partner * head_partner, axis=0, keepdims=True)
        cross = jnp.sum(head * head_partner, axis=0, keepdims=True)
        delta = other - own
        sign = jnp.where((delta > 0) | ((delta == 0) & is_left), 1.0, -1.0)
        bottom = jnp.abs(delta) + jnp.sqrt(delta * delta + 4.0 * cross * cross)
        tangent = 2.0 * cross * sign / jnp.maximum(bottom, 1e-30)
        cosine = 1.0 / jnp.sqrt(1.0 + tangent * tangent)
        sine = cosine * tangent
        angle = jnp.where(alone, 0.0, jnp.abs(cross) * lax.rsqrt(jnp.maximum(own * other, 1e-30)))
        return jnp.where(alone, values, cosine * partner + sine * values), angle

    def sweep(carry):
        values, done, unused = carry
        worst = jnp.zeros((1, lanes), f32)
        for step in range(max(sizes)):
            values, angle = rotate(values, step % 2)
            worst = jnp.maximum(worst, angle)
        return values, done + 1, jnp.max(worst)

    def going(carry):
        return (carry[2] > 1e-4) & (carry[1] < 20)

    values, _, _ = lax.while_loop(going, sweep, (start_ref[...], jnp.int32(0), jnp.float32(1.0)))
    out_ref[...] = values


def eigen(weights):
    sizes = tuple(weight.shape[0] - 1 for weight in weights)
    top = -(-(sizes[0] + 1) // 8) * 8
    low = -(-sizes[0] // 8) * 8
    lanes = 128
    columns = []
    turns = []
    for size, weight in zip(sizes, weights):
        differences = np.zeros((top, size), np.float32)
        differences[np.arange(size), np.arange(size)] = 1.0
        differences[np.arange(size) + 1, np.arange(size)] = -1.0
        columns.append(differences * jnp.pad(jnp.sqrt(weight), (0, top - size - 1))[:, None])
        turns.append(np.eye(low, size, dtype=np.float32))
    start = jnp.concatenate([jnp.concatenate(columns, 1), jnp.asarray(np.concatenate(turns, 1))], 0)
    start = jnp.pad(start, ((0, 0), (0, lanes - sum(sizes))))
    turned = pl.pallas_call(
        functools.partial(eigen_kernel, sizes=sizes, top=top),
        out_shape=jax.ShapeDtypeStruct(start.shape, f32),
        name="eigen",
    )(start)
    found = []
    first = 0
    for size in sizes:
        part = turned[:, first : first + size]
        found.append((jnp.sum(part[:top] ** 2, axis=0), part[top : top + size]))
        first += size
    return found


def power(value, exponent):
    result = None
    while exponent:
        if exponent % 2:
            result = value if result is None else result * value
        value = value * value
        exponent //= 2
    return result


def rows_place():
    me = lax.axis_index("rows")
    return me // 2, lax.rem(me, 2), lax.axis_size("rows") // 2


def partners():
    pair, place, pairs = rows_place()
    return [2 * pair + 1 - place] + [2 * lax.rem(pair + hop, pairs) + place for hop in range(1, pairs)]


def greet():
    barrier = pltpu.get_barrier_semaphore()
    for partner in partners():
        pl.semaphore_signal(barrier, inc=1, device_id={"rows": partner}, device_id_type=pl.DeviceIdType.MESH)


def exchange(row_count, ratio, ends, mate, total, others, send_sem, recv_sem):
    pair, place, pairs = rows_place()
    targets = partners()
    pl.semaphore_wait(pltpu.get_barrier_semaphore(), pairs)

    def copy(index, source, target):
        return pltpu.make_async_remote_copy(
            src_ref=source,
            dst_ref=target,
            send_sem=send_sem.at[index],
            recv_sem=recv_sem.at[index],
            device_id={"rows": targets[index]},
            device_id_type=pl.DeviceIdType.MESH,
        )

    near = copy(0, ends, mate)
    near.start()
    across = power(ratio, row_count)
    twice = across * across
    closing = 1.0 / (1.0 - power(twice, pairs))
    near.wait()
    is_first = place == 0
    first_f, last_f = jnp.where(is_first, ends[0], mate[0]), jnp.where(is_first, mate[0], ends[0])
    first_b, last_b = jnp.where(is_first, ends[1], mate[1]), jnp.where(is_first, mate[1], ends[1])
    total[0] = last_f + across * first_f
    total[1] = first_b + across * last_b
    far = [copy(hop, total, others.at[hop - 1]) for hop in range(1, pairs)]
    for one in far:
        one.start()
    for one in far:
        one.wait()
    before, after = total[0], total[1]
    for hop in range(pairs - 1, 0, -1):
        before = before * twice + others[hop - 1, 0]
        after = after * twice + others[pairs - hop - 1, 1]
    before, after = before * closing, after * closing
    before = jnp.where(is_first, before, first_f + across * before)
    after = jnp.where(is_first, last_b + across * after, after)
    last = ends[0] + across * before
    above = ratio * (ratio * last + after) / (1.0 - ratio * ratio)
    return before, above


def to_modes_kernel(*refs):
    x_refs = refs[:-12]
    high_ref, low_ref, ratio_ref, modes_ref, edge_ref, scale_ref, ends, mate, total, others, send_sem, recv_sem = refs[-12:]
    modes, share = ratio_ref.shape
    step = pl.program_id(0)

    @pl.when(step == 0)
    def _():
        greet()
        ends[...] = jnp.zeros(ends.shape, f32)
        scale_ref[...] = jnp.ones(scale_ref.shape, f32)

    values = jnp.concatenate([x_ref[...] for x_ref in x_refs], 0)
    modes_ref[...] = dot3((high_ref[...], low_ref[...]), split(values))
    ratio = ratio_ref[...]
    first, last, scale = ends[0], ends[1], scale_ref[...]
    rows = modes_ref.shape[0] // modes
    for row in range(rows):
        current = modes_ref[row * modes : (row + 1) * modes, :]
        first = first * ratio + current
        last = last + scale * current
        scale = scale * ratio
    ends[0] = first
    ends[1] = last
    scale_ref[...] = scale

    @pl.when(step == pl.num_programs(0) - 1)
    def _():
        count = rows * pl.num_programs(0)
        edge_ref[0], edge_ref[1] = exchange(count, ratio_ref[...], ends, mate, total, others, send_sem, recv_sem)


def two_way(rows, ratio_ref, edge_ref, held, chunk, carry, source, finish):
    step = pl.program_id(0)
    steps = pl.num_programs(0) // 2
    modes = ratio_ref.shape[0]
    ratio = ratio_ref[...]

    @pl.when(step == 0)
    def _():
        carry[...] = edge_ref[0]

    @pl.when(step == steps)
    def _():
        carry[...] = edge_ref[1]

    @pl.when(step < steps)
    def _():
        base = pl.multiple_of(step * rows * modes, rows * modes)
        value = carry[...]
        for row in range(rows):
            value = value * ratio + source(row)
            held[pl.ds(base + row * modes, modes), :] = value
        carry[...] = value

    @pl.when(step >= steps)
    def _():
        base = pl.multiple_of((2 * steps - 1 - step) * rows * modes, rows * modes)
        value = carry[...]
        for row in reversed(range(rows)):
            value = (value + held[pl.ds(base + row * modes, modes), :]) * ratio
            chunk[row * modes : (row + 1) * modes, :] = value
        carry[...] = value
        finish(split(chunk[...]))


def interface_kernel(modes_ref, high_ref, low_ref, ratio_ref, edge_ref, keep_ref, send_ref, held, chunk, carry, line):
    modes = ratio_ref.shape[0]
    piece = keep_ref.shape[1]
    half, _ = half_place()

    def finish(values):
        line[...] = dot3((high_ref[...], low_ref[...]), values)
        keep_ref[...] = line[:, pl.ds(pl.multiple_of(half * piece, piece), piece)]
        send_ref[...] = line[:, pl.ds(pl.multiple_of((1 - half) * piece, piece), piece)]

    two_way(
        keep_ref.shape[0], ratio_ref, edge_ref, held, chunk, carry,
        lambda row: modes_ref[row * modes : (row + 1) * modes, :], finish,
    )


def plane_ends(plane_ref, ratio_ref, ends, weight):
    rows = plane_ref.shape[0]
    shape = ratio_ref.shape
    ratio = ratio_ref[...]

    def group(index, carry):
        first, last, scale = carry
        lines = plane_ref[pl.ds(pl.multiple_of(index * BY, BY), BY), :]
        for row in range(BY):
            current = jnp.broadcast_to(lines[row : row + 1], shape)
            first = first * ratio + current
            last = last + scale * current
            scale = scale * ratio
        return first, last, scale

    zero = jnp.zeros(shape, f32)
    first, last, _ = lax.fori_loop(0, rows // BY, group, (zero, zero, jnp.ones(shape, f32)))
    ends[0] = first if weight is None else first * weight
    ends[1] = last if weight is None else last * weight


def sum_kernel(own_ref, other_ref, ratio_ref, plane_ref, edge_ref, ends, *rest):
    greet()
    plane_ref[...] = own_ref[...] + other_ref[...]
    plane_ends(plane_ref, ratio_ref, ends, None)
    edge_ref[0], edge_ref[1] = exchange(plane_ref.shape[0], ratio_ref[...], ends, *rest)


def join_kernel(own_ref, other_ref, ratio_ref, weight_ref, known_ref, plane_ref, edge_ref, ends, *rest):
    greet()
    half, _ = half_place()
    piece = own_ref.shape[1]
    plane_ref[:, pl.ds(pl.multiple_of(half * piece, piece), piece)] = own_ref[...]
    plane_ref[:, pl.ds(pl.multiple_of((1 - half) * piece, piece), piece)] = other_ref[...]
    plane_ends(plane_ref, ratio_ref, ends, weight_ref[...])
    before, above = exchange(plane_ref.shape[0], ratio_ref[...], ends, *rest)
    edge_ref[0] = known_ref[0] + before
    edge_ref[1] = known_ref[1] + above


def couple_kernel(
    plane_ref, again_ref, high_ref, low_ref, ratio_ref, edge_ref, strength_ref, out_ref, held, chunk, carry
):
    shape = ratio_ref.shape

    def finish(values):
        out_ref[...] = dot3((high_ref[...], low_ref[...]), values) + again_ref[...] * strength_ref[...]

    two_way(
        out_ref.shape[0], ratio_ref, edge_ref, held, chunk, carry,
        lambda row: jnp.broadcast_to(plane_ref[row : row + 1, :], shape), finish,
    )


def from_modes_kernel(modes_ref, plane_ref, weight_ref, high_ref, low_ref, ratio_ref, edge_ref, *rest):
    out_refs, (held, chunk, carry) = rest[:-3], rest[-3:]
    modes, share = ratio_ref.shape
    rows = plane_ref.shape[0]
    weight = weight_ref[...]

    def finish(values):
        result = dot3((high_ref[...], low_ref[...]), values)
        each = out_refs[0].shape[0]
        for index, out_ref in enumerate(out_refs):
            out_ref[...] = result[index * each : (index + 1) * each]

    two_way(
        rows, ratio_ref, edge_ref, held, chunk, carry,
        lambda row: modes_ref[row * modes : (row + 1) * modes, :] + weight * plane_ref[row : row + 1, :], finish,
    )


def params(collective_id=None):
    if collective_id is None:
        return pltpu.CompilerParams(vmem_limit_bytes=VMEM_BYTES)
    return pltpu.CompilerParams(vmem_limit_bytes=VMEM_BYTES, collective_id=collective_id, has_side_effects=True)


def exchange_scratch(shape, row_devices):
    pairs = row_devices // 2
    two = (2,) + shape
    return [pltpu.VMEM(two, f32)] * 3 + [
        pltpu.VMEM((pairs - 1,) + two, f32),
        pltpu.SemaphoreType.DMA((pairs,)),
        pltpu.SemaphoreType.DMA((pairs,)),
    ]


def cost(flops, moved):
    return pl.CostEstimate(flops=int(flops), bytes_accessed=int(moved), transcendentals=0)


def whole(shape):
    return pl.BlockSpec(shape, lambda *index: (0,) * len(shape))


def struct(*shape):
    return jax.ShapeDtypeStruct(shape, f32)


def decay(values, eigen_x):
    sigma = values[:, None] + eigen_x[None, :]
    return 1.0 / (1.0 + 0.5 * sigma + jnp.sqrt(sigma + 0.25 * sigma * sigma))


def body(source, solid, couplings):
    row_count, levels, length = source.shape
    lev_devices = lax.axis_size("lev")
    row_devices = lax.axis_size("rows")
    group = lev_devices // 2
    half, own = half_place()
    share = length // group
    piece = share // 2
    width = length // PARTS
    half_levels = levels * group
    all_levels = 2 * half_levels
    tile = 64 if row_count % 64 == 0 else BY
    size = source.size

    def passed(value, shift):
        pairs = [
            (side * group + place, side * group + (place + shift) % group) for side in range(2) for place in range(group)
        ]
        return lax.ppermute(value, "lev", pairs)

    def across_halves(value):
        return lax.ppermute(value, "lev", [(place, (place + group) % lev_devices) for place in range(lev_devices)])

    blocks, eigen_x = x_tables(length)
    forward_table = blocks.astype(np.float32)
    backward_table = np.swapaxes(blocks, 1, 2).astype(np.float32)
    keep = (1 - solid).astype(bf16)[:, None]
    keep = jnp.broadcast_to(keep, (keep.shape[0], 8 // levels) + keep.shape[2:]).reshape(-1, length // BX)
    groups = tile // BY * 8
    table = whole(blocks.shape)
    part_spec = pl.BlockSpec((tile * levels, share), lambda i: (i, 0))
    field_spec = pl.BlockSpec((tile, levels, length), lambda i: (i, 0, 0))
    mixed = pltpu.VMEM((PARTS // 2, levels * tile, 2 * width), f32)
    halves = [pltpu.VMEM(blocks.shape, bf16)] * 2
    spectral = pl.pallas_call(
        forward_kernel,
        grid=(row_count // tile,),
        in_specs=[field_spec, pl.BlockSpec((groups, length // BX), lambda i: (i, 0)), table],
        out_specs=[part_spec] * group,
        out_shape=[struct(row_count * levels, share)] * group,
        scratch_shapes=[pltpu.VMEM((groups, length), f32), mixed] + halves,
        compiler_params=params(),
        cost_estimate=cost(6 * size * 2 * width, 8 * size),
        name="forward_x",
    )(source, keep, forward_table)
    sections = [spectral[0]] + [passed(spectral[shift], shift) for shift in range(1, group)]

    middle = couplings[half_levels]
    edge_at = jnp.where(half == 0, half_levels, 0)
    mine = lax.dynamic_slice_in_dim(couplings, half * half_levels, half_levels + 1)
    mine = jnp.where(jnp.arange(half_levels + 1) == edge_at, 2.0 * middle, mine)
    (full_values, full_vectors), (values, vectors) = eigen([couplings, mine])
    edge_weight = jnp.where(half == 0, vectors[half_levels - 1], vectors[0])
    jump = middle * (full_vectors[half_levels - 1] + full_vectors[half_levels])
    eigen_x = lax.dynamic_slice_in_dim(jnp.asarray(eigen_x), own * share, share)
    ratio = decay(values, eigen_x)
    full_ratio = decay(full_values, lax.dynamic_slice_in_dim(eigen_x, half * piece, piece))

    chunk = max(BY, 256 // half_levels)
    thin = max(BY, 256 // all_levels)
    rows = chunk * half_levels
    plane_rows = thin * all_levels
    order = jnp.mod(own - jnp.arange(group), group)
    turned = vectors.reshape(group, levels, half_levels)[order]
    eye = jnp.eye(chunk, dtype=f32)
    to_modes = (eye[:, None, None, :, None] * turned.transpose(2, 0, 1)[None, :, :, None, :]).reshape(rows, rows)
    from_modes = (eye[None, :, None, :, None] * turned[:, None, :, None, :]).reshape(rows, rows)
    to_edge = (eye[:, :, None] * edge_weight).reshape(chunk, rows)
    to_jump = (jnp.eye(thin, dtype=f32)[:, :, None] * (jump * jump)).reshape(thin, plane_rows)

    steps = row_count // chunk
    plane_steps = row_count // thin
    shape = (half_levels, share)
    plane_shape = (all_levels, piece)
    modes_shape = struct(row_count * half_levels, share)
    section_spec = pl.BlockSpec((chunk * levels, share), lambda i: (i, 0))

    def ahead(count):
        return lambda i: (jnp.minimum(i, count - 1), 0)

    def behind(count):
        return lambda i: (jnp.minimum(2 * count - 1 - i, count - 1), 0)

    def scratch(rows, shape):
        return [pltpu.VMEM((row_count * shape[0], shape[1]), f32), pltpu.VMEM((rows, shape[1]), f32), pltpu.VMEM(shape, f32)]

    modes, edge = pl.pallas_call(
        to_modes_kernel,
        grid=(steps,),
        in_specs=[section_spec] * group + [whole((rows, rows))] * 2 + [whole(shape)],
        out_specs=[pl.BlockSpec((rows, share), lambda i: (i, 0)), whole((2,) + shape)],
        out_shape=[modes_shape, struct(2, *shape)],
        scratch_shapes=[pltpu.VMEM(shape, f32)] + exchange_scratch(shape, row_devices),
        compiler_params=params(0),
        cost_estimate=cost(6 * size * rows, 8 * size),
        name="to_modes",
    )(*sections, *split_outside(to_modes), ratio)

    kept, sent = pl.pallas_call(
        interface_kernel,
        grid=(2 * steps,),
        in_specs=[pl.BlockSpec((rows, share), ahead(steps))] + [whole((chunk, rows))] * 2 + [whole(shape), whole((2,) + shape)],
        out_specs=[pl.BlockSpec((chunk, piece), behind(steps))] * 2,
        out_shape=[struct(row_count, piece)] * 2,
        scratch_shapes=scratch(rows, shape) + [pltpu.VMEM((chunk, share), f32)],
        compiler_params=params(),
        cost_estimate=cost(6 * size * chunk, 5 * size),
        name="interface",
    )(modes, *split_outside(to_edge), ratio, edge)

    plane, plane_edge = pl.pallas_call(
        sum_kernel,
        out_shape=[struct(row_count, piece), struct(2, *plane_shape)],
        scratch_shapes=exchange_scratch(plane_shape, row_devices),
        compiler_params=params(1),
        name="plane_sum",
    )(kept, across_halves(sent), full_ratio)

    moved = pl.pallas_call(
        couple_kernel,
        grid=(2 * plane_steps,),
        in_specs=[
            pl.BlockSpec((thin, piece), ahead(plane_steps)),
            pl.BlockSpec((thin, piece), behind(plane_steps)),
            whole((thin, plane_rows)),
            whole((thin, plane_rows)),
            whole(plane_shape),
            whole((2,) + plane_shape),
            whole((1, piece)),
        ],
        out_specs=pl.BlockSpec((thin, piece), behind(plane_steps)),
        out_shape=struct(row_count, piece),
        scratch_shapes=scratch(plane_rows, plane_shape),
        compiler_params=params(),
        cost_estimate=cost(6 * size * thin, 2 * size),
        name="couple",
    )(plane, plane, *split_outside(to_jump), full_ratio, plane_edge, jnp.full((1, piece), middle))

    weight = jnp.broadcast_to(edge_weight[:, None], shape)
    joined, edge = pl.pallas_call(
        join_kernel,
        out_shape=[struct(row_count, share), struct(2, *shape)],
        scratch_shapes=exchange_scratch(shape, row_devices),
        compiler_params=params(2),
        name="plane_join",
    )(moved, across_halves(moved), ratio, weight, edge)

    solved = pl.pallas_call(
        from_modes_kernel,
        grid=(2 * steps,),
        in_specs=[pl.BlockSpec((rows, share), ahead(steps)), pl.BlockSpec((chunk, share), ahead(steps)), whole(shape)]
        + [whole((rows, rows))] * 2
        + [whole(shape), whole((2,) + shape)],
        out_specs=[pl.BlockSpec((chunk * levels, share), behind(steps))] * group,
        out_shape=[struct(row_count * levels, share)] * group,
        scratch_shapes=scratch(rows, shape),
        compiler_params=params(),
        cost_estimate=cost(6 * size * rows, 8 * size),
        name="from_modes",
    )(modes, joined, weight, *split_outside(from_modes), ratio, edge)
    returned = [solved[0]] + [passed(solved[shift], group - shift) for shift in range(1, group)]
    return pl.pallas_call(
        backward_kernel,
        grid=(row_count // tile,),
        in_specs=[part_spec] * group + [table],
        out_specs=field_spec,
        out_shape=struct(*source.shape),
        scratch_shapes=[mixed] + halves,
        compiler_params=params(),
        cost_estimate=cost(6 * size * 2 * width, 8 * size),
        name="backward_x",
    )(*returned, backward_table)


def solution(mesh):
    return jax.shard_map(
        body,
        mesh=mesh,
        in_specs=(P("rows", "lev", None), P("rows", "lev", None), P()),
        out_specs=P("rows", "lev", None),
        check_vma=False,
    )
```

```python
import functools
import math

import numpy as np

import jax
import jax.numpy as jnp
from jax import lax
from jax.experimental import pallas as pl
from jax.experimental.pallas import tpu as pltpu
from jax.sharding import PartitionSpec as P

BY = 8
BX = 64
PARTS = 16
VMEM_BYTES = 48 * 1024 * 1024

f32 = jnp.float32
highest = lax.Precision.HIGHEST
bf16 = jnp.bfloat16


def split(values):
    high = values.astype(bf16)
    low = (values - high.astype(f32)).astype(bf16)
    return high, low


def dot3(left, right):
    dot = functools.partial(jnp.dot, preferred_element_type=f32)
    return dot(left[0], right[0]) + (dot(left[0], right[1]) + dot(left[1], right[0]))


@functools.lru_cache(None)
def x_tables(length):
    width = length // PARTS
    half = PARTS // 2
    place = np.arange(width)
    blocks = np.zeros((half, 2 * width, 2 * width))
    slots = np.zeros((half, 2 * width))
    inner = math.sqrt(2.0 / length)
    edge = math.sqrt(1.0 / length)

    def angle(freq):
        return 2.0 * math.pi * (np.outer(place, freq) % length) / length

    low = PARTS * np.arange(width // 2 + 1)
    weight = np.where((low == 0) | (low == length // 2), edge, inner)
    cosines = np.cos(angle(low)) * weight
    sines = np.sin(angle(low[1:-1])) * inner
    blocks[0, :width, :width] = np.concatenate([cosines, sines], 1)
    slots[0, :width] = np.concatenate([low, low[1:-1]])
    middle = half + PARTS * np.arange(width // 2)
    blocks[0, width:, width:] = np.concatenate([np.cos(angle(middle)), np.sin(angle(middle))], 1) * inner
    slots[0, width:] = np.concatenate([middle, middle])
    for first in range(1, half):
        freq = first + PARTS * np.arange(width)
        turn = angle(freq)
        cosines, sines = np.cos(turn) * inner, np.sin(turn) * inner
        blocks[first] = np.block([[cosines, -sines], [sines, cosines]])
        slots[first] = np.concatenate([freq, freq])
    eigen = 4.0 * np.sin(math.pi * slots.reshape(-1) / length) ** 2
    return blocks, eigen.astype(np.float32)


def turn(index):
    return math.cos(2.0 * math.pi * index / PARTS), math.sin(2.0 * math.pi * index / PARTS)


def stage(x):
    s = [x[b] + x[b + 8] for b in range(8)]
    d = [x[b] - x[b + 8] for b in range(8)]
    out = [None] * 8
    minus = [d[b] - d[8 - b] for b in range(1, 4)]
    plus = [d[b] + d[8 - b] for b in range(1, 4)]
    for first in (1, 3, 5, 7):
        real = d[0]
        imag = d[4] * (-turn(4 * first)[1])
        for b in (1, 2, 3):
            cosine, sine = turn(b * first)
            real = real + minus[b - 1] * cosine
            imag = imag - plus[b - 1] * sine
        out[first] = (real, imag)
    ss = [s[b] + s[b + 4] for b in range(4)]
    sd = [s[b] - s[b + 4] for b in range(4)]
    root = math.sqrt(0.5)
    m = (sd[1] - sd[3]) * root
    p = (sd[1] + sd[3]) * root
    out[2] = (sd[0] + m, -p - sd[2])
    out[6] = (sd[0] - m, sd[2] - p)
    out[4] = (ss[0] - ss[2], ss[3] - ss[1])
    even, odd = ss[0] + ss[2], ss[1] + ss[3]
    out[0] = (even + odd, even - odd)
    return out


def unstage(y):
    root = math.sqrt(0.5)
    even, odd = y[0][0] + y[0][1], y[0][0] - y[0][1]
    ss = [even + y[4][0], odd - y[4][1], even - y[4][0], odd + y[4][1]]
    m = (y[2][0] - y[6][0]) * root
    p = (y[2][1] + y[6][1]) * root
    sd = [y[2][0] + y[6][0], m - p, y[6][1] - y[2][1], -m - p]
    s = [ss[b] + sd[b] for b in range(4)] + [ss[b] - sd[b] for b in range(4)]
    d = [None] * 8
    d[0] = (y[1][0] + y[3][0]) + (y[5][0] + y[7][0])
    d[4] = (y[3][1] - y[1][1]) + (y[7][1] - y[5][1])
    for b in (1, 2, 3):
        real = None
        imag = None
        for first in (1, 3, 5, 7):
            cosine, sine = turn(b * first)
            term, other = y[first][0] * cosine, y[first][1] * sine
            real = term if real is None else real + term
            imag = other if imag is None else imag + other
        d[b] = real - imag
        d[8 - b] = -real - imag
    return [s[b] + d[b] for b in range(8)] + [s[b] - d[b] for b in range(8)]


def half_place():
    group = lax.axis_size("lev") // 2
    me = lax.axis_index("lev")
    return me // group, me % group


def block_of(index, share, length):
    blocks = PARTS // 2
    _, own = half_place()
    return lax.rem(index + own * (share * blocks // length), blocks)


def keep_split(table_ref, high_ref, low_ref):
    @pl.when(pl.program_id(0) == 0)
    def _():
        for block in range(table_ref.shape[0]):
            high_ref[block], low_ref[block] = split(table_ref[block])


def forward_kernel(x_ref, keep_ref, table_ref, *rest):
    out_refs, (kept, mixed, high_ref, low_ref) = rest[:-4], rest[-4:]
    rows, levels, length = x_ref.shape
    width = length // PARTS
    share = out_refs[0].shape[1]
    pair = 8 // levels
    keep_split(table_ref, high_ref, low_ref)
    shape = (length // BX, length)
    first = lax.broadcasted_iota(jnp.int32, shape, 0) * BX
    lane = lax.broadcasted_iota(jnp.int32, shape, 1)
    spread = jnp.where((lane >= first) & (lane < first + BX), 1.0, 0.0).astype(bf16)
    kept[...] = jnp.dot(keep_ref[...], spread, preferred_element_type=f32)

    def group(index, unused):
        mask = kept[pl.ds(pl.multiple_of(index * 8, 8), 8), :]
        for part in range(BY // pair):
            row = index * BY + part * pair
            x = [
                x_ref[pl.ds(row, pair), :, pl.ds(b * width, width)].reshape(8, width)
                * mask[:, b * width : (b + 1) * width]
                for b in range(PARTS)
            ]
            base = pl.multiple_of(row * levels, 8)
            for block, (real, imag) in enumerate(stage(x)):
                mixed[block, pl.ds(base, 8), :width] = real
                mixed[block, pl.ds(base, 8), width:] = imag
        return unused

    lax.fori_loop(0, rows // BY, group, 0)
    for index in range(PARTS // 2):
        block = block_of(index, share, length)
        product = dot3(split(mixed[block]), (high_ref[block], low_ref[block]))
        target, offset = divmod(2 * index * width, share)
        out_refs[target][:, offset : offset + 2 * width] = product


def backward_kernel(*refs):
    x_refs, (table_ref, out_ref, mixed, high_ref, low_ref) = refs[:-5], refs[-5:]
    rows, levels, length = out_ref.shape
    width = length // PARTS
    share = x_refs[0].shape[1]
    pair = 8 // levels
    keep_split(table_ref, high_ref, low_ref)
    for index in range(PARTS // 2):
        block = block_of(index, share, length)
        source, offset = divmod(2 * index * width, share)
        values = split(x_refs[source][:, offset : offset + 2 * width])
        mixed[block] = dot3(values, (high_ref[block], low_ref[block]))

    def group(index, unused):
        row = index * pair
        base = pl.multiple_of(index * 8, 8)
        y = [
            (mixed[block, pl.ds(base, 8), :width], mixed[block, pl.ds(base, 8), width:])
            for block in range(PARTS // 2)
        ]
        for b, value in enumerate(unstage(y)):
            out_ref[pl.ds(row, pair), :, pl.ds(b * width, width)] = value.reshape(pair, levels, width)
        return unused

    lax.fori_loop(0, rows // pair, group, 0, unroll=4)


def jacobi(start, sizes, top):
    lanes = start.shape[1]
    lane = lax.broadcasted_iota(jnp.int32, (1, lanes), 1)
    in_first = lane < sizes[0]
    local = jnp.where(in_first, lane, lane - sizes[0])
    count = jnp.where(in_first, sizes[0], sizes[1])

    def rotate(values, parity):
        is_left = local % 2 == parity
        alone = (lane >= sum(sizes)) | (is_left & (local == count - 1)) | (jnp.logical_not(is_left) & (local == 0))
        partner = jnp.where(is_left, pltpu.roll(values, lanes - 1, 1), pltpu.roll(values, 1, 1))
        head = values[:top]
        head_partner = partner[:top]
        own = jnp.sum(head * head, axis=0, keepdims=True)
        other = jnp.sum(head_partner * head_partner, axis=0, keepdims=True)
        cross = jnp.sum(head * head_partner, axis=0, keepdims=True)
        delta = other - own
        sign = jnp.where((delta > 0) | ((delta == 0) & is_left), 1.0, -1.0)
        bottom = jnp.abs(delta) + jnp.sqrt(delta * delta + 4.0 * cross * cross)
        tangent = 2.0 * cross * sign / jnp.maximum(bottom, 1e-30)
        cosine = 1.0 / jnp.sqrt(1.0 + tangent * tangent)
        sine = cosine * tangent
        angle = jnp.where(alone, 0.0, jnp.abs(cross) * lax.rsqrt(jnp.maximum(own * other, 1e-30)))
        return jnp.where(alone, values, cosine * partner + sine * values), angle

    def sweep(carry):
        values, done, unused = carry
        worst = jnp.zeros((1, lanes), f32)
        for step in range(max(sizes)):
            values, angle = rotate(values, step % 2)
            worst = jnp.maximum(worst, angle)
        return values, done + 1, jnp.max(worst)

    def going(carry):
        return (carry[2] > 1e-4) & (carry[1] < 20)

    return lax.while_loop(going, sweep, (start, jnp.int32(0), jnp.float32(1.0)))[0]


def levels_kernel(
    couplings_ref, eigen_ref, to_high, to_low, from_high, from_low, edge_high, edge_low, jump_high, jump_low,
    ratio_ref, full_ref, weight_ref, *, group,
):
    modes, share = ratio_ref.shape
    all_modes, piece = full_ref.shape
    lanes = 128
    rows = to_high.shape[0]
    chunk = edge_high.shape[0]
    levels = modes // group
    top = -(-(all_modes + 1) // 8) * 8
    low = -(-all_modes // 8) * 8
    half, own = half_place()
    exact = functools.partial(jnp.dot, precision=highest, preferred_element_type=f32)

    def iota(shape, axis):
        return lax.broadcasted_iota(jnp.int32, shape, axis)

    def spot(condition):
        return jnp.where(condition, 1.0, 0.0)

    row, lane = iota((top, lanes), 0), iota((top, lanes), 1)
    in_first = lane < all_modes
    local = jnp.where(in_first, lane, lane - all_modes)
    used = lane < all_modes + modes
    weights = jnp.zeros((top, lanes), f32)
    for place in range(all_modes + 1):
        weights = jnp.where(in_first & (row == place), couplings_ref[place], weights)
    cut = jnp.where(half == 0, modes, 0)
    for place in range(modes + 1):
        value = couplings_ref[half * modes + place] * jnp.where(cut == place, 2.0, 1.0)
        weights = jnp.where(jnp.logical_not(in_first) & (row == place), value, weights)
    head = jnp.sqrt(weights) * (spot(used & (row == local)) - spot(used & (row == local + 1)))
    tail = spot(used & (row == local))[:low]
    turned = jacobi(jnp.concatenate([head, tail], 0), (all_modes, modes), top)
    head, vectors = turned[:top], turned[top : top + low]
    values = jnp.sum(head * head, axis=0, keepdims=True)

    at, to = iota((rows, low), 0), iota((rows, low), 1)
    section = at // (chunk * levels)
    level = lax.rem(own - section + group, group) * levels + lax.rem(at, levels)
    pick = spot(to == level)
    column = iota((lanes, rows), 1)
    place = spot(iota((lanes, rows), 0) == all_modes + lax.rem(column, modes))
    spread = exact(exact(pick, vectors), place)
    at, to = iota((rows, rows), 0), iota((rows, rows), 1)
    spread = jnp.where(lax.rem(at // levels, chunk) == to // modes, spread, 0.0)
    from_high[...], from_low[...] = split(spread)
    to_high[...], to_low[...] = split(spread.T)

    edge = jnp.where(half == 0, vectors[modes - 1 : modes], vectors[0:1])
    line = exact(jnp.broadcast_to(edge, (8, lanes)), place)[0:1]
    at, to = iota((chunk, rows), 0), iota((chunk, rows), 1)
    edge_high[...], edge_low[...] = split(jnp.where(at == to // modes, line, 0.0))
    jump = couplings_ref[modes] * (vectors[modes - 1 : modes] + vectors[modes : modes + 1])
    thin, plane_rows = jump_high.shape
    column = iota((lanes, plane_rows), 1)
    place = spot(iota((lanes, plane_rows), 0) == lax.rem(column, all_modes))
    line = exact(jnp.broadcast_to(jump * jump, (8, lanes)), place)[0:1]
    at, to = iota((thin, plane_rows), 0), iota((thin, plane_rows), 1)
    jump_high[...], jump_low[...] = split(jnp.where(at == to // all_modes, line, 0.0))

    def decay(count, first, mine):
        at, to = iota((count, lanes), 0), iota((count, lanes), 1)
        own_values = jnp.sum(jnp.where(to == at + first, values, 0.0), axis=1, keepdims=True)
        sigma = own_values + mine
        return 1.0 / (1.0 + 0.5 * sigma + jnp.sqrt(sigma + 0.25 * sigma * sigma))

    start = pl.multiple_of(own * share, share)
    ratio_ref[...] = decay(modes, all_modes, eigen_ref[:, pl.ds(start, share)])
    full_ref[...] = decay(all_modes, 0, eigen_ref[:, pl.ds(pl.multiple_of(start + half * piece, piece), piece)])
    at, to = iota((modes, lanes), 0), iota((modes, lanes), 1)
    weight = jnp.sum(jnp.where(to == at + all_modes, edge, 0.0), axis=1, keepdims=True)
    weight_ref[...] = jnp.broadcast_to(weight, (modes, share))


def power(value, exponent):
    result = None
    while exponent:
        if exponent % 2:
            result = value if result is None else result * value
        value = value * value
        exponent //= 2
    return result


def rows_place():
    me = lax.axis_index("rows")
    return me // 2, lax.rem(me, 2), lax.axis_size("rows") // 2


def partners():
    pair, place, pairs = rows_place()
    return [2 * pair + 1 - place] + [2 * lax.rem(pair + hop, pairs) + place for hop in range(1, pairs)]


def greet():
    barrier = pltpu.get_barrier_semaphore()
    for partner in partners():
        pl.semaphore_signal(barrier, inc=1, device_id={"rows": partner}, device_id_type=pl.DeviceIdType.MESH)


def exchange(row_count, ratio, ends, mate, total, others, send_sem, recv_sem):
    pair, place, pairs = rows_place()
    targets = partners()
    pl.semaphore_wait(pltpu.get_barrier_semaphore(), pairs)

    def copy(index, source, target):
        return pltpu.make_async_remote_copy(
            src_ref=source,
            dst_ref=target,
            send_sem=send_sem.at[index],
            recv_sem=recv_sem.at[index],
            device_id={"rows": targets[index]},
            device_id_type=pl.DeviceIdType.MESH,
        )

    near = copy(0, ends, mate)
    near.start()
    across = power(ratio, row_count)
    twice = across * across
    closing = 1.0 / (1.0 - power(twice, pairs))
    near.wait()
    is_first = place == 0
    first_f, last_f = jnp.where(is_first, ends[0], mate[0]), jnp.where(is_first, mate[0], ends[0])
    first_b, last_b = jnp.where(is_first, ends[1], mate[1]), jnp.where(is_first, mate[1], ends[1])
    total[0] = last_f + across * first_f
    total[1] = first_b + across * last_b
    far = [copy(hop, total, others.at[hop - 1]) for hop in range(1, pairs)]
    for one in far:
        one.start()
    for one in far:
        one.wait()
    before, after = total[0], total[1]
    for hop in range(pairs - 1, 0, -1):
        before = before * twice + others[hop - 1, 0]
        after = after * twice + others[pairs - hop - 1, 1]
    before, after = before * closing, after * closing
    before = jnp.where(is_first, before, first_f + across * before)
    after = jnp.where(is_first, last_b + across * after, after)
    last = ends[0] + across * before
    above = ratio * (ratio * last + after) / (1.0 - ratio * ratio)
    return before, above


def to_modes_kernel(*refs):
    x_refs = refs[:-12]
    high_ref, low_ref, ratio_ref, modes_ref, edge_ref, scale_ref, ends, mate, total, others, send_sem, recv_sem = refs[-12:]
    modes, share = ratio_ref.shape
    step = pl.program_id(0)

    @pl.when(step == 0)
    def _():
        greet()
        ends[...] = jnp.zeros(ends.shape, f32)
        scale_ref[...] = jnp.ones(scale_ref.shape, f32)

    values = jnp.concatenate([x_ref[...] for x_ref in x_refs], 0)
    modes_ref[...] = dot3((high_ref[...], low_ref[...]), split(values))
    ratio = ratio_ref[...]
    first, last, scale = ends[0], ends[1], scale_ref[...]
    rows = modes_ref.shape[0] // modes
    for row in range(rows):
        current = modes_ref[row * modes : (row + 1) * modes, :]
        first = first * ratio + current
        last = last + scale * current
        scale = scale * ratio
    ends[0] = first
    ends[1] = last
    scale_ref[...] = scale

    @pl.when(step == pl.num_programs(0) - 1)
    def _():
        count = rows * pl.num_programs(0)
        edge_ref[0], edge_ref[1] = exchange(count, ratio_ref[...], ends, mate, total, others, send_sem, recv_sem)


def two_way(rows, ratio_ref, edge_ref, held, chunk, carry, source, finish):
    step = pl.program_id(0)
    steps = pl.num_programs(0) // 2
    modes = ratio_ref.shape[0]
    ratio = ratio_ref[...]

    @pl.when(step == 0)
    def _():
        carry[...] = edge_ref[0]

    @pl.when(step == steps)
    def _():
        carry[...] = edge_ref[1]

    @pl.when(step < steps)
    def _():
        base = pl.multiple_of(step * rows * modes, rows * modes)
        value = carry[...]
        for row in range(rows):
            value = value * ratio + source(row)
            held[pl.ds(base + row * modes, modes), :] = value
        carry[...] = value

    @pl.when(step >= steps)
    def _():
        base = pl.multiple_of((2 * steps - 1 - step) * rows * modes, rows * modes)
        value = carry[...]
        for row in reversed(range(rows)):
            value = (value + held[pl.ds(base + row * modes, modes), :]) * ratio
            chunk[row * modes : (row + 1) * modes, :] = value
        carry[...] = value
        finish(split(chunk[...]))


def interface_kernel(modes_ref, high_ref, low_ref, ratio_ref, edge_ref, keep_ref, send_ref, held, chunk, carry, line):
    modes = ratio_ref.shape[0]
    piece = keep_ref.shape[1]
    half, _ = half_place()

    def finish(values):
        line[...] = dot3((high_ref[...], low_ref[...]), values)
        keep_ref[...] = line[:, pl.ds(pl.multiple_of(half * piece, piece), piece)]
        send_ref[...] = line[:, pl.ds(pl.multiple_of((1 - half) * piece, piece), piece)]

    two_way(
        keep_ref.shape[0], ratio_ref, edge_ref, held, chunk, carry,
        lambda row: modes_ref[row * modes : (row + 1) * modes, :], finish,
    )


def plane_ends(plane_ref, ratio_ref, ends, weight):
    rows = plane_ref.shape[0]
    shape = ratio_ref.shape
    ratio = ratio_ref[...]

    def group(index, carry):
        first, last, scale = carry
        lines = plane_ref[pl.ds(pl.multiple_of(index * BY, BY), BY), :]
        for row in range(BY):
            current = jnp.broadcast_to(lines[row : row + 1], shape)
            first = first * ratio + current
            last = last + scale * current
            scale = scale * ratio
        return first, last, scale

    zero = jnp.zeros(shape, f32)
    first, last, _ = lax.fori_loop(0, rows // BY, group, (zero, zero, jnp.ones(shape, f32)))
    ends[0] = first if weight is None else first * weight
    ends[1] = last if weight is None else last * weight


def sum_kernel(own_ref, other_ref, ratio_ref, plane_ref, edge_ref, ends, *rest):
    greet()
    plane_ref[...] = own_ref[...] + other_ref[...]
    plane_ends(plane_ref, ratio_ref, ends, None)
    edge_ref[0], edge_ref[1] = exchange(plane_ref.shape[0], ratio_ref[...], ends, *rest)


def join_kernel(own_ref, other_ref, ratio_ref, weight_ref, known_ref, plane_ref, edge_ref, ends, *rest):
    greet()
    half, _ = half_place()
    piece = own_ref.shape[1]
    plane_ref[:, pl.ds(pl.multiple_of(half * piece, piece), piece)] = own_ref[...]
    plane_ref[:, pl.ds(pl.multiple_of((1 - half) * piece, piece), piece)] = other_ref[...]
    plane_ends(plane_ref, ratio_ref, ends, weight_ref[...])
    before, above = exchange(plane_ref.shape[0], ratio_ref[...], ends, *rest)
    edge_ref[0] = known_ref[0] + before
    edge_ref[1] = known_ref[1] + above


def couple_kernel(
    plane_ref, again_ref, high_ref, low_ref, ratio_ref, edge_ref, couplings_ref, out_ref, held, chunk, carry
):
    shape = ratio_ref.shape
    strength = couplings_ref[shape[0] // 2]

    def finish(values):
        out_ref[...] = dot3((high_ref[...], low_ref[...]), values) + again_ref[...] * strength

    two_way(
        out_ref.shape[0], ratio_ref, edge_ref, held, chunk, carry,
        lambda row: jnp.broadcast_to(plane_ref[row : row + 1, :], shape), finish,
    )


def from_modes_kernel(modes_ref, plane_ref, weight_ref, high_ref, low_ref, ratio_ref, edge_ref, *rest, group):
    out_refs, (held, chunk, carry, *remote) = rest[:group], rest[group:]
    modes, share = ratio_ref.shape
    rows = plane_ref.shape[0]
    weight = weight_ref[...]
    step = pl.program_id(0)
    steps = pl.num_programs(0) // 2
    half, own = half_place()
    each = out_refs[0].shape[0]
    targets = [half * group + lax.rem(own + group - hop, group) for hop in range(1, group)]

    def copy(hop, index):
        outgoing, send_sem, recv_sem = remote
        place = pl.ds(pl.multiple_of(index * each, each), each)
        return pltpu.make_async_remote_copy(
            src_ref=outgoing.at[hop - 1, place],
            dst_ref=out_refs[hop].at[place],
            send_sem=send_sem.at[hop - 1, index],
            recv_sem=recv_sem.at[hop - 1, index],
            device_id={"lev": targets[hop - 1]},
            device_id_type=pl.DeviceIdType.MESH,
        )

    if group > 1:

        @pl.when(step == 0)
        def _():
            barrier = pltpu.get_barrier_semaphore()
            for target in targets:
                pl.semaphore_signal(barrier, inc=1, device_id={"lev": target}, device_id_type=pl.DeviceIdType.MESH)

        @pl.when(step == steps)
        def _():
            pl.semaphore_wait(pltpu.get_barrier_semaphore(), group - 1)

    def finish(values):
        result = dot3((high_ref[...], low_ref[...]), values)
        out_refs[0][...] = result[:each]
        index = 2 * steps - 1 - step
        for hop in range(1, group):
            remote[0][hop - 1, pl.ds(pl.multiple_of(index * each, each), each), :] = result[hop * each : (hop + 1) * each]
            copy(hop, index).start()

    two_way(
        rows, ratio_ref, edge_ref, held, chunk, carry,
        lambda row: modes_ref[row * modes : (row + 1) * modes, :] + weight * plane_ref[row : row + 1, :], finish,
    )

    if group > 1:

        @pl.when(step == 2 * steps - 1)
        def _():
            def settle(index, unused):
                for hop in range(1, group):
                    copy(hop, index).wait()
                return unused

            lax.fori_loop(0, steps, settle, 0)


def params(collective_id=None):
    if collective_id is None:
        return pltpu.CompilerParams(vmem_limit_bytes=VMEM_BYTES)
    return pltpu.CompilerParams(vmem_limit_bytes=VMEM_BYTES, collective_id=collective_id, has_side_effects=True)


def exchange_scratch(shape, row_devices):
    pairs = row_devices // 2
    two = (2,) + shape
    return [pltpu.VMEM(two, f32)] * 3 + [
        pltpu.VMEM((pairs - 1,) + two, f32),
        pltpu.SemaphoreType.DMA((pairs,)),
        pltpu.SemaphoreType.DMA((pairs,)),
    ]


def cost(flops, moved):
    return pl.CostEstimate(flops=int(flops), bytes_accessed=int(moved), transcendentals=0)


def whole(shape):
    return pl.BlockSpec(shape, lambda *index: (0,) * len(shape))


def struct(*shape):
    return jax.ShapeDtypeStruct(shape, f32)


def body(source, solid, couplings):
    row_count, levels, length = source.shape
    lev_devices = lax.axis_size("lev")
    row_devices = lax.axis_size("rows")
    group = lev_devices // 2
    share = length // group
    piece = share // 2
    width = length // PARTS
    half_levels = levels * group
    all_levels = 2 * half_levels
    tile = 64 if row_count % 64 == 0 else BY
    size = source.size

    def passed(value, shift):
        pairs = [
            (side * group + place, side * group + (place + shift) % group) for side in range(2) for place in range(group)
        ]
        return lax.ppermute(value, "lev", pairs)

    def across_halves(value):
        return lax.ppermute(value, "lev", [(place, (place + group) % lev_devices) for place in range(lev_devices)])

    blocks, eigen_x = x_tables(length)
    forward_table = blocks.astype(np.float32)
    backward_table = np.swapaxes(blocks, 1, 2).astype(np.float32)
    keep = (1 - solid).astype(bf16)[:, None]
    keep = jnp.broadcast_to(keep, (keep.shape[0], 8 // levels) + keep.shape[2:]).reshape(-1, length // BX)
    groups = tile // BY * 8
    table = whole(blocks.shape)
    part_spec = pl.BlockSpec((tile * levels, share), lambda i: (i, 0))
    field_spec = pl.BlockSpec((tile, levels, length), lambda i: (i, 0, 0))
    mixed = pltpu.VMEM((PARTS // 2, levels * tile, 2 * width), f32)
    halves = [pltpu.VMEM(blocks.shape, bf16)] * 2
    spectral = pl.pallas_call(
        forward_kernel,
        grid=(row_count // tile,),
        in_specs=[field_spec, pl.BlockSpec((groups, length // BX), lambda i: (i, 0)), table],
        out_specs=[part_spec] * group,
        out_shape=[struct(row_count * levels, share)] * group,
        scratch_shapes=[pltpu.VMEM((groups, length), f32), mixed] + halves,
        compiler_params=params(),
        cost_estimate=cost(6 * size * 2 * width, 8 * size),
        name="forward_x",
    )(source, keep, forward_table)
    sections = [spectral[0]] + [passed(spectral[shift], shift) for shift in range(1, group)]

    chunk = max(BY, 256 // half_levels)
    thin = max(BY, 256 // all_levels)
    rows = chunk * half_levels
    plane_rows = thin * all_levels
    in_smem = pl.BlockSpec(memory_space=pltpu.SMEM)
    built = [(rows, rows)] * 4 + [(chunk, rows)] * 2 + [(thin, plane_rows)] * 2
    *matrices, ratio, full_ratio, weight = pl.pallas_call(
        functools.partial(levels_kernel, group=group),
        in_specs=[in_smem, pl.BlockSpec(memory_space=pltpu.VMEM)],
        out_shape=[jax.ShapeDtypeStruct(each, bf16) for each in built]
        + [struct(half_levels, share), struct(all_levels, piece), struct(half_levels, share)],
        compiler_params=params(),
        name="levels",
    )(couplings, eigen_x[None, :])
    to_modes, from_modes, to_edge, to_jump = (matrices[2 * index : 2 * index + 2] for index in range(4))

    steps = row_count // chunk
    plane_steps = row_count // thin
    shape = (half_levels, share)
    plane_shape = (all_levels, piece)
    modes_shape = struct(row_count * half_levels, share)
    section_spec = pl.BlockSpec((chunk * levels, share), lambda i: (i, 0))

    def ahead(count):
        return lambda i: (jnp.minimum(i, count - 1), 0)

    def behind(count):
        return lambda i: (jnp.minimum(2 * count - 1 - i, count - 1), 0)

    def scratch(rows, shape):
        return [pltpu.VMEM((row_count * shape[0], shape[1]), f32), pltpu.VMEM((rows, shape[1]), f32), pltpu.VMEM(shape, f32)]

    modes, edge = pl.pallas_call(
        to_modes_kernel,
        grid=(steps,),
        in_specs=[section_spec] * group + [whole((rows, rows))] * 2 + [whole(shape)],
        out_specs=[pl.BlockSpec((rows, share), lambda i: (i, 0)), whole((2,) + shape)],
        out_shape=[modes_shape, struct(2, *shape)],
        scratch_shapes=[pltpu.VMEM(shape, f32)] + exchange_scratch(shape, row_devices),
        compiler_params=params(0),
        cost_estimate=cost(6 * size * rows, 8 * size),
        name="to_modes",
    )(*sections, *to_modes, ratio)

    kept, sent = pl.pallas_call(
        interface_kernel,
        grid=(2 * steps,),
        in_specs=[pl.BlockSpec((rows, share), ahead(steps))] + [whole((chunk, rows))] * 2 + [whole(shape), whole((2,) + shape)],
        out_specs=[pl.BlockSpec((chunk, piece), behind(steps))] * 2,
        out_shape=[struct(row_count, piece)] * 2,
        scratch_shapes=scratch(rows, shape) + [pltpu.VMEM((chunk, share), f32)],
        compiler_params=params(),
        cost_estimate=cost(6 * size * chunk, 5 * size),
        name="interface",
    )(modes, *to_edge, ratio, edge)

    plane, plane_edge = pl.pallas_call(
        sum_kernel,
        out_shape=[struct(row_count, piece), struct(2, *plane_shape)],
        scratch_shapes=exchange_scratch(plane_shape, row_devices),
        compiler_params=params(1),
        name="plane_sum",
    )(kept, across_halves(sent), full_ratio)

    moved = pl.pallas_call(
        couple_kernel,
        grid=(2 * plane_steps,),
        in_specs=[
            pl.BlockSpec((thin, piece), ahead(plane_steps)),
            pl.BlockSpec((thin, piece), behind(plane_steps)),
            whole((thin, plane_rows)),
            whole((thin, plane_rows)),
            whole(plane_shape),
            whole((2,) + plane_shape),
            in_smem,
        ],
        out_specs=pl.BlockSpec((thin, piece), behind(plane_steps)),
        out_shape=struct(row_count, piece),
        scratch_shapes=scratch(plane_rows, plane_shape),
        compiler_params=params(),
        cost_estimate=cost(6 * size * thin, 2 * size),
        name="couple",
    )(plane, plane, *to_jump, full_ratio, plane_edge, couplings)

    joined, edge = pl.pallas_call(
        join_kernel,
        out_shape=[struct(row_count, share), struct(2, *shape)],
        scratch_shapes=exchange_scratch(shape, row_devices),
        compiler_params=params(2),
        name="plane_join",
    )(moved, across_halves(moved), ratio, weight, edge)

    outgoing = [
        pltpu.VMEM((group - 1, row_count * levels, share), f32),
        pltpu.SemaphoreType.DMA((group - 1, steps)),
        pltpu.SemaphoreType.DMA((group - 1, steps)),
    ]
    returned = pl.pallas_call(
        functools.partial(from_modes_kernel, group=group),
        grid=(2 * steps,),
        in_specs=[pl.BlockSpec((rows, share), ahead(steps)), pl.BlockSpec((chunk, share), ahead(steps)), whole(shape)]
        + [whole((rows, rows))] * 2
        + [whole(shape), whole((2,) + shape)],
        out_specs=[pl.BlockSpec((chunk * levels, share), behind(steps))] + [pl.BlockSpec(memory_space=pl.ANY)] * (group - 1),
        out_shape=[struct(row_count * levels, share)] * group,
        scratch_shapes=scratch(rows, shape) + (outgoing if group > 1 else []),
        compiler_params=params(3 if group > 1 else None),
        cost_estimate=cost(6 * size * rows, 8 * size),
        name="from_modes",
    )(modes, joined, weight, *from_modes, ratio, edge)
    return pl.pallas_call(
        backward_kernel,
        grid=(row_count // tile,),
        in_specs=[part_spec] * group + [table],
        out_specs=field_spec,
        out_shape=struct(*source.shape),
        scratch_shapes=[mixed] + halves,
        compiler_params=params(),
        cost_estimate=cost(6 * size * 2 * width, 8 * size),
        name="backward_x",
    )(*returned, backward_table)


def solution(mesh):
    return jax.shard_map(
        body,
        mesh=mesh,
        in_specs=(P("rows", "lev", None), P("rows", "lev", None), P()),
        out_specs=P("rows", "lev", None),
        check_vma=False,
    )
```

```python
import functools
import math

import numpy as np

import jax
import jax.numpy as jnp
from jax import lax
from jax.experimental import pallas as pl
from jax.experimental.pallas import tpu as pltpu
from jax.sharding import PartitionSpec as P

BY = 8
BX = 64
PARTS = 16
VMEM_BYTES = 60 * 1024 * 1024

f32 = jnp.float32
highest = lax.Precision.HIGHEST
bf16 = jnp.bfloat16


def split(values):
    high = values.astype(bf16)
    low = (values - high.astype(f32)).astype(bf16)
    return high, low


def dot3(left, right):
    dot = functools.partial(jnp.dot, preferred_element_type=f32)
    return dot(left[0], right[0]) + (dot(left[0], right[1]) + dot(left[1], right[0]))


@functools.lru_cache(None)
def x_tables(length):
    width = length // PARTS
    half = PARTS // 2
    place = np.arange(width)
    blocks = np.zeros((half, 2 * width, 2 * width))
    slots = np.zeros((half, 2 * width))
    inner = math.sqrt(2.0 / length)
    edge = math.sqrt(1.0 / length)

    def angle(freq):
        return 2.0 * math.pi * (np.outer(place, freq) % length) / length

    low = PARTS * np.arange(width // 2 + 1)
    weight = np.where((low == 0) | (low == length // 2), edge, inner)
    cosines = np.cos(angle(low)) * weight
    sines = np.sin(angle(low[1:-1])) * inner
    blocks[0, :width, :width] = np.concatenate([cosines, sines], 1)
    slots[0, :width] = np.concatenate([low, low[1:-1]])
    middle = half + PARTS * np.arange(width // 2)
    blocks[0, width:, width:] = np.concatenate([np.cos(angle(middle)), np.sin(angle(middle))], 1) * inner
    slots[0, width:] = np.concatenate([middle, middle])
    for first in range(1, half):
        freq = first + PARTS * np.arange(width)
        turn = angle(freq)
        cosines, sines = np.cos(turn) * inner, np.sin(turn) * inner
        blocks[first] = np.block([[cosines, -sines], [sines, cosines]])
        slots[first] = np.concatenate([freq, freq])
    eigen = 4.0 * np.sin(math.pi * slots.reshape(-1) / length) ** 2
    return blocks, eigen.astype(np.float32)


def turn(index):
    return math.cos(2.0 * math.pi * index / PARTS), math.sin(2.0 * math.pi * index / PARTS)


def stage(x):
    s = [x[b] + x[b + 8] for b in range(8)]
    d = [x[b] - x[b + 8] for b in range(8)]
    out = [None] * 8
    minus = [d[b] - d[8 - b] for b in range(1, 4)]
    plus = [d[b] + d[8 - b] for b in range(1, 4)]
    for first in (1, 3, 5, 7):
        real = d[0]
        imag = d[4] * (-turn(4 * first)[1])
        for b in (1, 2, 3):
            cosine, sine = turn(b * first)
            real = real + minus[b - 1] * cosine
            imag = imag - plus[b - 1] * sine
        out[first] = (real, imag)
    ss = [s[b] + s[b + 4] for b in range(4)]
    sd = [s[b] - s[b + 4] for b in range(4)]
    root = math.sqrt(0.5)
    m = (sd[1] - sd[3]) * root
    p = (sd[1] + sd[3]) * root
    out[2] = (sd[0] + m, -p - sd[2])
    out[6] = (sd[0] - m, sd[2] - p)
    out[4] = (ss[0] - ss[2], ss[3] - ss[1])
    even, odd = ss[0] + ss[2], ss[1] + ss[3]
    out[0] = (even + odd, even - odd)
    return out


def unstage(y):
    root = math.sqrt(0.5)
    even, odd = y[0][0] + y[0][1], y[0][0] - y[0][1]
    ss = [even + y[4][0], odd - y[4][1], even - y[4][0], odd + y[4][1]]
    m = (y[2][0] - y[6][0]) * root
    p = (y[2][1] + y[6][1]) * root
    sd = [y[2][0] + y[6][0], m - p, y[6][1] - y[2][1], -m - p]
    s = [ss[b] + sd[b] for b in range(4)] + [ss[b] - sd[b] for b in range(4)]
    d = [None] * 8
    d[0] = (y[1][0] + y[3][0]) + (y[5][0] + y[7][0])
    d[4] = (y[3][1] - y[1][1]) + (y[7][1] - y[5][1])
    for b in (1, 2, 3):
        real = None
        imag = None
        for first in (1, 3, 5, 7):
            cosine, sine = turn(b * first)
            term, other = y[first][0] * cosine, y[first][1] * sine
            real = term if real is None else real + term
            imag = other if imag is None else imag + other
        d[b] = real - imag
        d[8 - b] = -real - imag
    return [s[b] + d[b] for b in range(8)] + [s[b] - d[b] for b in range(8)]


def half_place():
    group = lax.axis_size("lev") // 2
    me = lax.axis_index("lev")
    return me // group, me % group


def block_of(index, share, length):
    blocks = PARTS // 2
    _, own = half_place()
    return lax.rem(index + own * (share * blocks // length), blocks)


def keep_split(table_ref, high_ref, low_ref):
    @pl.when(pl.program_id(0) == 0)
    def _():
        for block in range(table_ref.shape[0]):
            high_ref[block], low_ref[block] = split(table_ref[block])


def forward_kernel(x_ref, solid_ref, table_ref, *rest):
    out_refs, (kept, mixed, high_ref, low_ref) = rest[:-4], rest[-4:]
    rows, levels, length = x_ref.shape
    width = length // PARTS
    share = out_refs[0].shape[1]
    pair = 8 // levels
    keep_split(table_ref, high_ref, low_ref)
    shape = (length // BX, length)
    first = lax.broadcasted_iota(jnp.int32, shape, 0) * BX
    lane = lax.broadcasted_iota(jnp.int32, shape, 1)
    spread = jnp.where((lane >= first) & (lane < first + BX), 1.0, 0.0).astype(bf16)
    keep = (1 - solid_ref[...]).astype(f32)
    keep = jnp.concatenate([keep] * pair, 1).reshape(kept.shape[0], length // BX)
    kept[...] = jnp.dot(keep.astype(bf16), spread, preferred_element_type=f32)

    def group(index, unused):
        mask = kept[pl.ds(pl.multiple_of(index * 8, 8), 8), :]
        for part in range(BY // pair):
            row = index * BY + part * pair
            x = [
                x_ref[pl.ds(row, pair), :, pl.ds(b * width, width)].reshape(8, width)
                * mask[:, b * width : (b + 1) * width]
                for b in range(PARTS)
            ]
            base = pl.multiple_of(row * levels, 8)
            for block, (real, imag) in enumerate(stage(x)):
                mixed[block, pl.ds(base, 8), :width] = real
                mixed[block, pl.ds(base, 8), width:] = imag
        return unused

    lax.fori_loop(0, rows // BY, group, 0)
    for index in range(PARTS // 2):
        block = block_of(index, share, length)
        product = dot3(split(mixed[block]), (high_ref[block], low_ref[block]))
        target, offset = divmod(2 * index * width, share)
        out_refs[target][:, offset : offset + 2 * width] = product


def backward_kernel(*refs):
    x_refs, (table_ref, out_ref, mixed, high_ref, low_ref) = refs[:-5], refs[-5:]
    rows, levels, length = out_ref.shape
    width = length // PARTS
    share = x_refs[0].shape[1]
    pair = 8 // levels
    keep_split(table_ref, high_ref, low_ref)
    for index in range(PARTS // 2):
        block = block_of(index, share, length)
        source, offset = divmod(2 * index * width, share)
        values = split(x_refs[source][:, offset : offset + 2 * width])
        mixed[block] = dot3(values, (high_ref[block], low_ref[block]))

    def group(index, unused):
        row = index * pair
        base = pl.multiple_of(index * 8, 8)
        y = [
            (mixed[block, pl.ds(base, 8), :width], mixed[block, pl.ds(base, 8), width:])
            for block in range(PARTS // 2)
        ]
        for b, value in enumerate(unstage(y)):
            out_ref[pl.ds(row, pair), :, pl.ds(b * width, width)] = value.reshape(pair, levels, width)
        return unused

    lax.fori_loop(0, rows // pair, group, 0, unroll=4)


def jacobi(start, sizes, top):
    lanes = start.shape[1]
    lane = lax.broadcasted_iota(jnp.int32, (1, lanes), 1)
    in_first = lane < sizes[0]
    local = jnp.where(in_first, lane, lane - sizes[0])
    count = jnp.where(in_first, sizes[0], sizes[1])

    def rotate(values, parity):
        is_left = local % 2 == parity
        alone = (lane >= sum(sizes)) | (is_left & (local == count - 1)) | (jnp.logical_not(is_left) & (local == 0))
        partner = jnp.where(is_left, pltpu.roll(values, lanes - 1, 1), pltpu.roll(values, 1, 1))
        head = values[:top]
        head_partner = partner[:top]
        own = jnp.sum(head * head, axis=0, keepdims=True)
        other = jnp.sum(head_partner * head_partner, axis=0, keepdims=True)
        cross = jnp.sum(head * head_partner, axis=0, keepdims=True)
        delta = other - own
        sign = jnp.where((delta > 0) | ((delta == 0) & is_left), 1.0, -1.0)
        bottom = jnp.abs(delta) + jnp.sqrt(delta * delta + 4.0 * cross * cross)
        tangent = 2.0 * cross * sign / jnp.maximum(bottom, 1e-30)
        cosine = 1.0 / jnp.sqrt(1.0 + tangent * tangent)
        sine = cosine * tangent
        angle = jnp.where(alone, 0.0, jnp.abs(cross) * lax.rsqrt(jnp.maximum(own * other, 1e-30)))
        return jnp.where(alone, values, cosine * partner + sine * values), angle

    def sweep(carry):
        values, done, unused = carry
        worst = jnp.zeros((1, lanes), f32)
        for step in range(max(sizes)):
            values, angle = rotate(values, step % 2)
            worst = jnp.maximum(worst, angle)
        return values, done + 1, jnp.max(worst)

    def going(carry):
        return (carry[2] > 1e-5) & (carry[1] < 20)

    return lax.while_loop(going, sweep, (start, jnp.int32(0), jnp.float32(1.0)))[0]


def levels_kernel(
    couplings_ref, eigen_ref, to_high, to_low, from_high, from_low, edge_high, edge_low, jump_high, jump_low,
    ratio_ref, full_ref, weight_ref, *, group,
):
    modes, share = ratio_ref.shape
    all_modes, piece = full_ref.shape
    lanes = 128
    rows = to_high.shape[0]
    chunk = edge_high.shape[0]
    levels = modes // group
    top = -(-(all_modes + 1) // 8) * 8
    low = -(-all_modes // 8) * 8
    half, own = half_place()
    exact = functools.partial(jnp.dot, precision=highest, preferred_element_type=f32)

    def iota(shape, axis):
        return lax.broadcasted_iota(jnp.int32, shape, axis)

    def spot(condition):
        return jnp.where(condition, 1.0, 0.0)

    row, lane = iota((top, lanes), 0), iota((top, lanes), 1)
    in_first = lane < all_modes
    local = jnp.where(in_first, lane, lane - all_modes)
    used = lane < all_modes + modes
    weights = jnp.zeros((top, lanes), f32)
    for place in range(all_modes + 1):
        weights = jnp.where(in_first & (row == place), couplings_ref[place], weights)
    cut = jnp.where(half == 0, modes, 0)
    for place in range(modes + 1):
        value = couplings_ref[half * modes + place] * jnp.where(cut == place, 2.0, 1.0)
        weights = jnp.where(jnp.logical_not(in_first) & (row == place), value, weights)
    head = jnp.sqrt(weights) * (spot(used & (row == local)) - spot(used & (row == local + 1)))
    tail = spot(used & (row == local))[:low]
    turned = jacobi(jnp.concatenate([head, tail], 0), (all_modes, modes), top)
    head, vectors = turned[:top], turned[top : top + low]
    values = jnp.sum(head * head, axis=0, keepdims=True)

    at, to = iota((rows, low), 0), iota((rows, low), 1)
    section = at // (chunk * levels)
    level = lax.rem(own - section + group, group) * levels + lax.rem(at, levels)
    pick = spot(to == level)
    column = iota((lanes, rows), 1)
    place = spot(iota((lanes, rows), 0) == all_modes + lax.rem(column, modes))
    spread = exact(exact(pick, vectors), place)
    at, to = iota((rows, rows), 0), iota((rows, rows), 1)
    spread = jnp.where(lax.rem(at // levels, chunk) == to // modes, spread, 0.0)
    from_high[...], from_low[...] = split(spread)
    to_high[...], to_low[...] = split(spread.T)

    edge = jnp.where(half == 0, vectors[modes - 1 : modes], vectors[0:1])
    line = exact(jnp.broadcast_to(edge, (8, lanes)), place)[0:1]
    at, to = iota((chunk, rows), 0), iota((chunk, rows), 1)
    edge_high[...], edge_low[...] = split(jnp.where(at == to // modes, line, 0.0))
    jump = couplings_ref[modes] * (vectors[modes - 1 : modes] + vectors[modes : modes + 1])
    thin, plane_rows = jump_high.shape
    column = iota((lanes, plane_rows), 1)
    place = spot(iota((lanes, plane_rows), 0) == lax.rem(column, all_modes))
    line = exact(jnp.broadcast_to(jump * jump, (8, lanes)), place)[0:1]
    at, to = iota((thin, plane_rows), 0), iota((thin, plane_rows), 1)
    jump_high[...], jump_low[...] = split(jnp.where(at == to // all_modes, line, 0.0))

    def decay(count, first, mine):
        at, to = iota((count, lanes), 0), iota((count, lanes), 1)
        own_values = jnp.sum(jnp.where(to == at + first, values, 0.0), axis=1, keepdims=True)
        sigma = own_values + mine
        return 1.0 / (1.0 + 0.5 * sigma + jnp.sqrt(sigma + 0.25 * sigma * sigma))

    start = pl.multiple_of(own * share, share)
    ratio_ref[...] = decay(modes, all_modes, eigen_ref[:, pl.ds(start, share)])
    full_ref[...] = decay(all_modes, 0, eigen_ref[:, pl.ds(pl.multiple_of(start + half * piece, piece), piece)])
    at, to = iota((modes, lanes), 0), iota((modes, lanes), 1)
    weight = jnp.sum(jnp.where(to == at + all_modes, edge, 0.0), axis=1, keepdims=True)
    weight_ref[...] = jnp.broadcast_to(weight, (modes, share))


def power(value, exponent):
    result = None
    while exponent:
        if exponent % 2:
            result = value if result is None else result * value
        value = value * value
        exponent //= 2
    return result


def rows_place():
    me = lax.axis_index("rows")
    return me // 2, lax.rem(me, 2), lax.axis_size("rows") // 2


def partners():
    pair, place, pairs = rows_place()
    return [2 * pair + 1 - place] + [2 * lax.rem(pair + hop, pairs) + place for hop in range(1, pairs)]


def greet():
    barrier = pltpu.get_barrier_semaphore()
    for partner in partners():
        pl.semaphore_signal(barrier, inc=1, device_id={"rows": partner}, device_id_type=pl.DeviceIdType.MESH)


def exchange(row_count, ratio, ends, mate, total, others, send_sem, recv_sem):
    pair, place, pairs = rows_place()
    targets = partners()
    pl.semaphore_wait(pltpu.get_barrier_semaphore(), pairs)

    def copy(index, source, target):
        return pltpu.make_async_remote_copy(
            src_ref=source,
            dst_ref=target,
            send_sem=send_sem.at[index],
            recv_sem=recv_sem.at[index],
            device_id={"rows": targets[index]},
            device_id_type=pl.DeviceIdType.MESH,
        )

    near = copy(0, ends, mate)
    near.start()
    across = power(ratio, row_count)
    twice = across * across
    closing = 1.0 / (1.0 - power(twice, pairs))
    near.wait()
    is_first = place == 0
    first_f, last_f = jnp.where(is_first, ends[0], mate[0]), jnp.where(is_first, mate[0], ends[0])
    first_b, last_b = jnp.where(is_first, ends[1], mate[1]), jnp.where(is_first, mate[1], ends[1])
    total[0] = last_f + across * first_f
    total[1] = first_b + across * last_b
    far = [copy(hop, total, others.at[hop - 1]) for hop in range(1, pairs)]
    for one in far:
        one.start()
    for one in far:
        one.wait()
    before, after = total[0], total[1]
    for hop in range(pairs - 1, 0, -1):
        before = before * twice + others[hop - 1, 0]
        after = after * twice + others[pairs - hop - 1, 1]
    before, after = before * closing, after * closing
    before = jnp.where(is_first, before, first_f + across * before)
    after = jnp.where(is_first, last_b + across * after, after)
    last = ends[0] + across * before
    above = ratio * (ratio * last + after) / (1.0 - ratio * ratio)
    return before, above


def to_modes_kernel(*refs):
    x_refs = refs[:-12]
    high_ref, low_ref, ratio_ref, modes_ref, edge_ref, scale_ref, ends, mate, total, others, send_sem, recv_sem = refs[-12:]
    modes, share = ratio_ref.shape
    step = pl.program_id(0)

    @pl.when(step == 0)
    def _():
        greet()
        ends[...] = jnp.zeros(ends.shape, f32)
        scale_ref[...] = jnp.ones(scale_ref.shape, f32)

    values = jnp.concatenate([x_ref[...] for x_ref in x_refs], 0)
    modes_ref[...] = dot3((high_ref[...], low_ref[...]), split(values))
    ratio = ratio_ref[...]
    first, last, scale = ends[0], ends[1], scale_ref[...]
    rows = modes_ref.shape[0] // modes
    for row in range(rows):
        current = modes_ref[row * modes : (row + 1) * modes, :]
        first = first * ratio + current
        last = last + scale * current
        scale = scale * ratio
    ends[0] = first
    ends[1] = last
    scale_ref[...] = scale

    @pl.when(step == pl.num_programs(0) - 1)
    def _():
        count = rows * pl.num_programs(0)
        edge_ref[0], edge_ref[1] = exchange(count, ratio_ref[...], ends, mate, total, others, send_sem, recv_sem)


def two_way(rows, ratio_ref, edge_ref, held, chunk, carry, source, finish):
    step = pl.program_id(0)
    steps = pl.num_programs(0) // 2
    modes = ratio_ref.shape[0]
    ratio = ratio_ref[...]

    @pl.when(step == 0)
    def _():
        carry[...] = edge_ref[0]

    @pl.when(step == steps)
    def _():
        carry[...] = edge_ref[1]

    @pl.when(step < steps)
    def _():
        base = pl.multiple_of(step * rows * modes, rows * modes)
        value = carry[...]
        for row in range(rows):
            value = value * ratio + source(row)
            held[pl.ds(base + row * modes, modes), :] = value
        carry[...] = value

    @pl.when(step >= steps)
    def _():
        base = pl.multiple_of((2 * steps - 1 - step) * rows * modes, rows * modes)
        value = carry[...]
        for row in reversed(range(rows)):
            value = (value + held[pl.ds(base + row * modes, modes), :]) * ratio
            chunk[row * modes : (row + 1) * modes, :] = value
        carry[...] = value
        finish(split(chunk[...]))


class Mirror:
    def __init__(self, received, outgoing, send_sem, recv_sem):
        half, own = half_place()
        self.target = (1 - half) * (lax.axis_size("lev") // 2) + own
        self.refs = received, outgoing, send_sem, recv_sem
        self.step = pl.program_id(0)
        self.steps = pl.num_programs(0) // 2
        self.rows = outgoing.shape[0]

    def copy(self, index, rows):
        received, outgoing, send_sem, recv_sem = self.refs
        place = pl.ds(pl.multiple_of(index * rows, rows), rows)
        return pltpu.make_async_remote_copy(
            src_ref=outgoing.at[place],
            dst_ref=received.at[place],
            send_sem=send_sem.at[index],
            recv_sem=recv_sem.at[index],
            device_id={"lev": self.target},
            device_id_type=pl.DeviceIdType.MESH,
        )

    def greet(self):
        @pl.when(self.step == 0)
        def _():
            pl.semaphore_signal(
                pltpu.get_barrier_semaphore(), inc=1, device_id={"lev": self.target}, device_id_type=pl.DeviceIdType.MESH
            )

        @pl.when(self.step == self.steps)
        def _():
            pl.semaphore_wait(pltpu.get_barrier_semaphore(), 1)

    def send(self, values):
        rows = values.shape[0]
        index = 2 * self.steps - 1 - self.step
        self.refs[1][pl.ds(pl.multiple_of(index * rows, rows), rows), :] = values
        self.copy(index, rows).start()

    def settle(self, rows):
        @pl.when(self.step == 2 * self.steps - 1)
        def _():
            def one(index, unused):
                self.copy(index, rows).wait()
                return unused

            lax.fori_loop(0, self.steps, one, 0)


def interface_kernel(
    modes_ref, high_ref, low_ref, ratio_ref, edge_ref, keep_ref, received, held, chunk, carry, line, *remote
):
    modes = ratio_ref.shape[0]
    piece = keep_ref.shape[1]
    half, _ = half_place()
    mirror = Mirror(received, *remote)
    mirror.greet()

    def finish(values):
        line[...] = dot3((high_ref[...], low_ref[...]), values)
        keep_ref[...] = line[:, pl.ds(pl.multiple_of(half * piece, piece), piece)]
        mirror.send(line[:, pl.ds(pl.multiple_of((1 - half) * piece, piece), piece)])

    two_way(
        keep_ref.shape[0], ratio_ref, edge_ref, held, chunk, carry,
        lambda row: modes_ref[row * modes : (row + 1) * modes, :], finish,
    )
    mirror.settle(keep_ref.shape[0])


def plane_ends(plane_ref, ratio_ref, ends, weight):
    rows = plane_ref.shape[0]
    shape = ratio_ref.shape
    ratio = ratio_ref[...]

    def group(index, carry):
        first, last, scale = carry
        lines = plane_ref[pl.ds(pl.multiple_of(index * BY, BY), BY), :]
        for row in range(BY):
            current = jnp.broadcast_to(lines[row : row + 1], shape)
            first = first * ratio + current
            last = last + scale * current
            scale = scale * ratio
        return first, last, scale

    zero = jnp.zeros(shape, f32)
    first, last, _ = lax.fori_loop(0, rows // BY, group, (zero, zero, jnp.ones(shape, f32)))
    ends[0] = first if weight is None else first * weight
    ends[1] = last if weight is None else last * weight


def sum_kernel(own_ref, other_ref, ratio_ref, plane_ref, edge_ref, ends, *rest):
    greet()
    plane_ref[...] = own_ref[...] + other_ref[...]
    plane_ends(plane_ref, ratio_ref, ends, None)
    edge_ref[0], edge_ref[1] = exchange(plane_ref.shape[0], ratio_ref[...], ends, *rest)


def join_kernel(own_ref, other_ref, ratio_ref, weight_ref, known_ref, plane_ref, edge_ref, ends, *rest):
    greet()
    half, _ = half_place()
    piece = own_ref.shape[1]
    plane_ref[:, pl.ds(pl.multiple_of(half * piece, piece), piece)] = own_ref[...]
    plane_ref[:, pl.ds(pl.multiple_of((1 - half) * piece, piece), piece)] = other_ref[...]
    plane_ends(plane_ref, ratio_ref, ends, weight_ref[...])
    before, above = exchange(plane_ref.shape[0], ratio_ref[...], ends, *rest)
    edge_ref[0] = known_ref[0] + before
    edge_ref[1] = known_ref[1] + above


def couple_kernel(
    plane_ref, again_ref, high_ref, low_ref, ratio_ref, edge_ref, couplings_ref, out_ref, received, held, chunk, carry,
    *remote,
):
    shape = ratio_ref.shape
    strength = couplings_ref[shape[0] // 2]
    mirror = Mirror(received, *remote)
    mirror.greet()

    def finish(values):
        result = dot3((high_ref[...], low_ref[...]), values) + again_ref[...] * strength
        out_ref[...] = result
        mirror.send(result)

    two_way(
        out_ref.shape[0], ratio_ref, edge_ref, held, chunk, carry,
        lambda row: jnp.broadcast_to(plane_ref[row : row + 1, :], shape), finish,
    )
    mirror.settle(out_ref.shape[0])


def from_modes_kernel(modes_ref, plane_ref, weight_ref, high_ref, low_ref, ratio_ref, edge_ref, *rest, group):
    out_refs, (held, chunk, carry, *remote) = rest[:group], rest[group:]
    modes, share = ratio_ref.shape
    rows = plane_ref.shape[0]
    weight = weight_ref[...]
    step = pl.program_id(0)
    steps = pl.num_programs(0) // 2
    half, own = half_place()
    each = out_refs[0].shape[0]
    targets = [half * group + lax.rem(own + group - hop, group) for hop in range(1, group)]

    def copy(hop, index):
        outgoing, send_sem, recv_sem = remote
        place = pl.ds(pl.multiple_of(index * each, each), each)
        return pltpu.make_async_remote_copy(
            src_ref=outgoing.at[hop - 1, place],
            dst_ref=out_refs[hop].at[place],
            send_sem=send_sem.at[hop - 1, index],
            recv_sem=recv_sem.at[hop - 1, index],
            device_id={"lev": targets[hop - 1]},
            device_id_type=pl.DeviceIdType.MESH,
        )

    if group > 1:

        @pl.when(step == 0)
        def _():
            barrier = pltpu.get_barrier_semaphore()
            for target in targets:
                pl.semaphore_signal(barrier, inc=1, device_id={"lev": target}, device_id_type=pl.DeviceIdType.MESH)

        @pl.when(step == steps)
        def _():
            pl.semaphore_wait(pltpu.get_barrier_semaphore(), group - 1)

    def finish(values):
        result = dot3((high_ref[...], low_ref[...]), values)
        out_refs[0][...] = result[:each]
        index = 2 * steps - 1 - step
        for hop in range(1, group):
            remote[0][hop - 1, pl.ds(pl.multiple_of(index * each, each), each), :] = result[hop * each : (hop + 1) * each]
            copy(hop, index).start()

    two_way(
        rows, ratio_ref, edge_ref, held, chunk, carry,
        lambda row: modes_ref[row * modes : (row + 1) * modes, :] + weight * plane_ref[row : row + 1, :], finish,
    )

    if group > 1:

        @pl.when(step == 2 * steps - 1)
        def _():
            def settle(index, unused):
                for hop in range(1, group):
                    copy(hop, index).wait()
                return unused

            lax.fori_loop(0, steps, settle, 0)


def params(collective_id=None):
    if collective_id is None:
        return pltpu.CompilerParams(vmem_limit_bytes=VMEM_BYTES)
    return pltpu.CompilerParams(vmem_limit_bytes=VMEM_BYTES, collective_id=collective_id, has_side_effects=True)


def exchange_scratch(shape, row_devices):
    pairs = row_devices // 2
    two = (2,) + shape
    return [pltpu.VMEM(two, f32)] * 3 + [
        pltpu.VMEM((pairs - 1,) + two, f32),
        pltpu.SemaphoreType.DMA((pairs,)),
        pltpu.SemaphoreType.DMA((pairs,)),
    ]


def cost(flops, moved):
    return pl.CostEstimate(flops=int(flops), bytes_accessed=int(moved), transcendentals=0)


def whole(shape):
    return pl.BlockSpec(shape, lambda *index: (0,) * len(shape))


def struct(*shape):
    return jax.ShapeDtypeStruct(shape, f32)


def body(source, solid, couplings):
    row_count, levels, length = source.shape
    lev_devices = lax.axis_size("lev")
    row_devices = lax.axis_size("rows")
    group = lev_devices // 2
    share = length // group
    piece = share // 2
    width = length // PARTS
    half_levels = levels * group
    all_levels = 2 * half_levels
    tile = 64 if row_count % 64 == 0 else BY
    size = source.size

    def passed(value, shift):
        pairs = [
            (side * group + place, side * group + (place + shift) % group) for side in range(2) for place in range(group)
        ]
        return lax.ppermute(value, "lev", pairs)

    blocks, eigen_x = x_tables(length)
    forward_table = blocks.astype(np.float32)
    backward_table = np.swapaxes(blocks, 1, 2).astype(np.float32)
    groups = tile // BY * 8
    table = whole(blocks.shape)
    part_spec = pl.BlockSpec((tile * levels, share), lambda i: (i, 0))
    field_spec = pl.BlockSpec((tile, levels, length), lambda i: (i, 0, 0))
    mixed = pltpu.VMEM((PARTS // 2, levels * tile, 2 * width), f32)
    halves = [pltpu.VMEM(blocks.shape, bf16)] * 2
    spectral = pl.pallas_call(
        forward_kernel,
        grid=(row_count // tile,),
        in_specs=[field_spec, pl.BlockSpec((tile // BY, levels, length // BX), lambda i: (i, 0, 0)), table],
        out_specs=[part_spec] * group,
        out_shape=[struct(row_count * levels, share)] * group,
        scratch_shapes=[pltpu.VMEM((groups, length), f32), mixed] + halves,
        compiler_params=params(),
        cost_estimate=cost(6 * size * 2 * width, 8 * size),
        name="forward_x",
    )(source, solid, forward_table)
    sections = [spectral[0]] + [passed(spectral[shift], shift) for shift in range(1, group)]

    chunk = max(BY, 256 // half_levels)
    thin = max(BY, 256 // all_levels)
    rows = chunk * half_levels
    plane_rows = thin * all_levels
    in_smem = pl.BlockSpec(memory_space=pltpu.SMEM)
    built = [(rows, rows)] * 4 + [(chunk, rows)] * 2 + [(thin, plane_rows)] * 2
    *matrices, ratio, full_ratio, weight = pl.pallas_call(
        functools.partial(levels_kernel, group=group),
        in_specs=[in_smem, pl.BlockSpec(memory_space=pltpu.VMEM)],
        out_shape=[jax.ShapeDtypeStruct(each, bf16) for each in built]
        + [struct(half_levels, share), struct(all_levels, piece), struct(half_levels, share)],
        compiler_params=params(),
        name="levels",
    )(couplings, eigen_x[None, :])
    to_modes, from_modes, to_edge, to_jump = (matrices[2 * index : 2 * index + 2] for index in range(4))

    steps = row_count // chunk
    plane_steps = row_count // thin
    shape = (half_levels, share)
    plane_shape = (all_levels, piece)
    modes_shape = struct(row_count * half_levels, share)
    section_spec = pl.BlockSpec((chunk * levels, share), lambda i: (i, 0))

    def ahead(count):
        return lambda i: (jnp.minimum(i, count - 1), 0)

    def behind(count):
        return lambda i: (jnp.minimum(2 * count - 1 - i, count - 1), 0)

    def scratch(rows, shape):
        return [pltpu.VMEM((row_count * shape[0], shape[1]), f32), pltpu.VMEM((rows, shape[1]), f32), pltpu.VMEM(shape, f32)]

    modes, edge = pl.pallas_call(
        to_modes_kernel,
        grid=(steps,),
        in_specs=[section_spec] * group + [whole((rows, rows))] * 2 + [whole(shape)],
        out_specs=[pl.BlockSpec((rows, share), lambda i: (i, 0)), whole((2,) + shape)],
        out_shape=[modes_shape, struct(2, *shape)],
        scratch_shapes=[pltpu.VMEM(shape, f32)] + exchange_scratch(shape, row_devices),
        compiler_params=params(0),
        cost_estimate=cost(6 * size * rows, 8 * size),
        name="to_modes",
    )(*sections, *to_modes, ratio)

    def mirrored(count):
        return [
            pltpu.VMEM((row_count, piece), f32),
            pltpu.SemaphoreType.DMA((count,)),
            pltpu.SemaphoreType.DMA((count,)),
        ]

    kept, received = pl.pallas_call(
        interface_kernel,
        grid=(2 * steps,),
        in_specs=[pl.BlockSpec((rows, share), ahead(steps))] + [whole((chunk, rows))] * 2 + [whole(shape), whole((2,) + shape)],
        out_specs=[pl.BlockSpec((chunk, piece), behind(steps)), pl.BlockSpec(memory_space=pl.ANY)],
        out_shape=[struct(row_count, piece)] * 2,
        scratch_shapes=scratch(rows, shape) + [pltpu.VMEM((chunk, share), f32)] + mirrored(steps),
        compiler_params=params(4),
        cost_estimate=cost(6 * size * chunk, 5 * size),
        name="interface",
    )(modes, *to_edge, ratio, edge)

    plane, plane_edge = pl.pallas_call(
        sum_kernel,
        out_shape=[struct(row_count, piece), struct(2, *plane_shape)],
        scratch_shapes=exchange_scratch(plane_shape, row_devices),
        compiler_params=params(1),
        name="plane_sum",
    )(kept, received, full_ratio)

    moved, received = pl.pallas_call(
        couple_kernel,
        grid=(2 * plane_steps,),
        in_specs=[
            pl.BlockSpec((thin, piece), ahead(plane_steps)),
            pl.BlockSpec((thin, piece), behind(plane_steps)),
            whole((thin, plane_rows)),
            whole((thin, plane_rows)),
            whole(plane_shape),
            whole((2,) + plane_shape),
            in_smem,
        ],
        out_specs=[pl.BlockSpec((thin, piece), behind(plane_steps)), pl.BlockSpec(memory_space=pl.ANY)],
        out_shape=[struct(row_count, piece)] * 2,
        scratch_shapes=scratch(plane_rows, plane_shape) + mirrored(plane_steps),
        compiler_params=params(5),
        cost_estimate=cost(6 * size * thin, 2 * size),
        name="couple",
    )(plane, plane, *to_jump, full_ratio, plane_edge, couplings)

    joined, edge = pl.pallas_call(
        join_kernel,
        out_shape=[struct(row_count, share), struct(2, *shape)],
        scratch_shapes=exchange_scratch(shape, row_devices),
        compiler_params=params(2),
        name="plane_join",
    )(moved, received, ratio, weight, edge)

    outgoing = [
        pltpu.VMEM((group - 1, row_count * levels, share), f32),
        pltpu.SemaphoreType.DMA((group - 1, steps)),
        pltpu.SemaphoreType.DMA((group - 1, steps)),
    ]
    returned = pl.pallas_call(
        functools.partial(from_modes_kernel, group=group),
        grid=(2 * steps,),
        in_specs=[pl.BlockSpec((rows, share), ahead(steps)), pl.BlockSpec((chunk, share), ahead(steps)), whole(shape)]
        + [whole((rows, rows))] * 2
        + [whole(shape), whole((2,) + shape)],
        out_specs=[pl.BlockSpec((chunk * levels, share), behind(steps))] + [pl.BlockSpec(memory_space=pl.ANY)] * (group - 1),
        out_shape=[struct(row_count * levels, share)] * group,
        scratch_shapes=scratch(rows, shape) + (outgoing if group > 1 else []),
        compiler_params=params(3 if group > 1 else None),
        cost_estimate=cost(6 * size * rows, 8 * size),
        name="from_modes",
    )(modes, joined, weight, *from_modes, ratio, edge)
    return pl.pallas_call(
        backward_kernel,
        grid=(row_count // tile,),
        in_specs=[part_spec] * group + [table],
        out_specs=field_spec,
        out_shape=struct(*source.shape),
        scratch_shapes=[mixed] + halves,
        compiler_params=params(),
        cost_estimate=cost(6 * size * 2 * width, 8 * size),
        name="backward_x",
    )(*returned, backward_table)


def solution(mesh):
    return jax.shard_map(
        body,
        mesh=mesh,
        in_specs=(P("rows", "lev", None), P("rows", "lev", None), P()),
        out_specs=P("rows", "lev", None),
        check_vma=False,
    )
```

```python
import functools
import math

import numpy as np

import jax
import jax.numpy as jnp
from jax import lax
from jax.experimental import pallas as pl
from jax.experimental.pallas import tpu as pltpu
from jax.sharding import PartitionSpec as P

BY = 8
BX = 64
PARTS = 16
VMEM_BYTES = 48 * 1024 * 1024
ALL_VMEM_BYTES = 60 * 1024 * 1024

f32 = jnp.float32
highest = lax.Precision.HIGHEST
bf16 = jnp.bfloat16


def split(values):
    high = values.astype(bf16)
    low = (values - high.astype(f32)).astype(bf16)
    return high, low


def dot3(left, right):
    left = jnp.concatenate([left[0], left[0], left[1]], 1)
    right = jnp.concatenate([right[0], right[1], right[0]], 0)
    return jnp.dot(left, right, preferred_element_type=f32)


@functools.lru_cache(None)
def x_tables(length):
    width = length // PARTS
    half = PARTS // 2
    place = np.arange(width)
    blocks = np.zeros((half, 2 * width, 2 * width))
    slots = np.zeros((half, 2 * width))
    inner = math.sqrt(2.0 / length)
    edge = math.sqrt(1.0 / length)

    def angle(freq):
        return 2.0 * math.pi * (np.outer(place, freq) % length) / length

    low = PARTS * np.arange(width // 2 + 1)
    weight = np.where((low == 0) | (low == length // 2), edge, inner)
    cosines = np.cos(angle(low)) * weight
    sines = np.sin(angle(low[1:-1])) * inner
    blocks[0, :width, :width] = np.concatenate([cosines, sines], 1)
    slots[0, :width] = np.concatenate([low, low[1:-1]])
    middle = half + PARTS * np.arange(width // 2)
    blocks[0, width:, width:] = np.concatenate([np.cos(angle(middle)), np.sin(angle(middle))], 1) * inner
    slots[0, width:] = np.concatenate([middle, middle])
    for first in range(1, half):
        freq = first + PARTS * np.arange(width)
        turn = angle(freq)
        cosines, sines = np.cos(turn) * inner, np.sin(turn) * inner
        blocks[first] = np.block([[cosines, -sines], [sines, cosines]])
        slots[first] = np.concatenate([freq, freq])
    eigen = 4.0 * np.sin(math.pi * slots.reshape(-1) / length) ** 2
    return blocks, eigen.astype(np.float32)


def turn(index):
    return math.cos(2.0 * math.pi * index / PARTS), math.sin(2.0 * math.pi * index / PARTS)


def stage(x):
    s = [x[b] + x[b + 8] for b in range(8)]
    d = [x[b] - x[b + 8] for b in range(8)]
    out = [None] * 8
    minus = [d[b] - d[8 - b] for b in range(1, 4)]
    plus = [d[b] + d[8 - b] for b in range(1, 4)]
    for first in (1, 3, 5, 7):
        real = d[0]
        imag = d[4] * (-turn(4 * first)[1])
        for b in (1, 2, 3):
            cosine, sine = turn(b * first)
            real = real + minus[b - 1] * cosine
            imag = imag - plus[b - 1] * sine
        out[first] = (real, imag)
    ss = [s[b] + s[b + 4] for b in range(4)]
    sd = [s[b] - s[b + 4] for b in range(4)]
    root = math.sqrt(0.5)
    m = (sd[1] - sd[3]) * root
    p = (sd[1] + sd[3]) * root
    out[2] = (sd[0] + m, -p - sd[2])
    out[6] = (sd[0] - m, sd[2] - p)
    out[4] = (ss[0] - ss[2], ss[3] - ss[1])
    even, odd = ss[0] + ss[2], ss[1] + ss[3]
    out[0] = (even + odd, even - odd)
    return out


def unstage(y):
    root = math.sqrt(0.5)
    even, odd = y[0][0] + y[0][1], y[0][0] - y[0][1]
    ss = [even + y[4][0], odd - y[4][1], even - y[4][0], odd + y[4][1]]
    m = (y[2][0] - y[6][0]) * root
    p = (y[2][1] + y[6][1]) * root
    sd = [y[2][0] + y[6][0], m - p, y[6][1] - y[2][1], -m - p]
    s = [ss[b] + sd[b] for b in range(4)] + [ss[b] - sd[b] for b in range(4)]
    d = [None] * 8
    d[0] = (y[1][0] + y[3][0]) + (y[5][0] + y[7][0])
    d[4] = (y[3][1] - y[1][1]) + (y[7][1] - y[5][1])
    for b in (1, 2, 3):
        real = None
        imag = None
        for first in (1, 3, 5, 7):
            cosine, sine = turn(b * first)
            term, other = y[first][0] * cosine, y[first][1] * sine
            real = term if real is None else real + term
            imag = other if imag is None else imag + other
        d[b] = real - imag
        d[8 - b] = -real - imag
    return [s[b] + d[b] for b in range(8)] + [s[b] - d[b] for b in range(8)]


def half_place():
    group = lax.axis_size("lev") // 2
    me = lax.axis_index("lev")
    return me // group, me % group


def block_of(index, share, length):
    blocks = PARTS // 2
    _, own = half_place()
    return lax.rem(index + own * (share * blocks // length), blocks)


def keep_split(table_ref, high_ref, low_ref):
    @pl.when(pl.program_id(0) == 0)
    def _():
        for block in range(table_ref.shape[0]):
            high_ref[block], low_ref[block] = split(table_ref[block])


def forward_kernel(x_ref, solid_ref, table_ref, *rest):
    out_refs, (kept, mixed, high_ref, low_ref) = rest[:-4], rest[-4:]
    rows, levels, length = x_ref.shape
    width = length // PARTS
    share = out_refs[0].shape[1]
    pair = 8 // levels
    keep_split(table_ref, high_ref, low_ref)
    shape = (length // BX, length)
    first = lax.broadcasted_iota(jnp.int32, shape, 0) * BX
    lane = lax.broadcasted_iota(jnp.int32, shape, 1)
    spread = jnp.where((lane >= first) & (lane < first + BX), 1.0, 0.0).astype(bf16)
    keep = (1 - solid_ref[...]).astype(f32)
    keep = jnp.concatenate([keep] * pair, 1).reshape(kept.shape[0], length // BX)
    kept[...] = jnp.dot(keep.astype(bf16), spread, preferred_element_type=f32)

    def group(index, unused):
        mask = kept[pl.ds(pl.multiple_of(index * 8, 8), 8), :]
        for part in range(BY // pair):
            row = index * BY + part * pair
            x = [
                x_ref[pl.ds(row, pair), :, pl.ds(b * width, width)].reshape(8, width)
                * mask[:, b * width : (b + 1) * width]
                for b in range(PARTS)
            ]
            base = pl.multiple_of(row * levels, 8)
            for block, (real, imag) in enumerate(stage(x)):
                mixed[block, pl.ds(base, 8), :width] = real
                mixed[block, pl.ds(base, 8), width:] = imag
        return unused

    lax.fori_loop(0, rows // BY, group, 0)
    for index in range(PARTS // 2):
        block = block_of(index, share, length)
        product = dot3(split(mixed[block]), (high_ref[block], low_ref[block]))
        target, offset = divmod(2 * index * width, share)
        out_refs[target][:, offset : offset + 2 * width] = product


def backward_kernel(*refs):
    x_refs, (table_ref, out_ref, mixed, high_ref, low_ref) = refs[:-5], refs[-5:]
    rows, levels, length = out_ref.shape
    width = length // PARTS
    share = x_refs[0].shape[1]
    pair = 8 // levels
    keep_split(table_ref, high_ref, low_ref)
    for index in range(PARTS // 2):
        block = block_of(index, share, length)
        source, offset = divmod(2 * index * width, share)
        values = split(x_refs[source][:, offset : offset + 2 * width])
        mixed[block] = dot3(values, (high_ref[block], low_ref[block]))

    def group(index, unused):
        row = index * pair
        base = pl.multiple_of(index * 8, 8)
        y = [
            (mixed[block, pl.ds(base, 8), :width], mixed[block, pl.ds(base, 8), width:])
            for block in range(PARTS // 2)
        ]
        for b, value in enumerate(unstage(y)):
            out_ref[pl.ds(row, pair), :, pl.ds(b * width, width)] = value.reshape(pair, levels, width)
        return unused

    lax.fori_loop(0, rows // pair, group, 0, unroll=4)


def jacobi(start, sizes, top):
    lanes = start.shape[1]
    lane = lax.broadcasted_iota(jnp.int32, (1, lanes), 1)
    in_first = lane < sizes[0]
    local = jnp.where(in_first, lane, lane - sizes[0])
    count = jnp.where(in_first, sizes[0], sizes[1])

    def rotate(values, parity):
        is_left = local % 2 == parity
        alone = (lane >= sum(sizes)) | (is_left & (local == count - 1)) | (jnp.logical_not(is_left) & (local == 0))
        partner = jnp.where(is_left, pltpu.roll(values, lanes - 1, 1), pltpu.roll(values, 1, 1))
        head = values[:top]
        head_partner = partner[:top]
        own = jnp.sum(head * head, axis=0, keepdims=True)
        other = jnp.sum(head_partner * head_partner, axis=0, keepdims=True)
        cross = jnp.sum(head * head_partner, axis=0, keepdims=True)
        delta = other - own
        sign = jnp.where((delta > 0) | ((delta == 0) & is_left), 1.0, -1.0)
        bottom = jnp.abs(delta) + jnp.sqrt(delta * delta + 4.0 * cross * cross)
        tangent = 2.0 * cross * sign / jnp.maximum(bottom, 1e-30)
        cosine = 1.0 / jnp.sqrt(1.0 + tangent * tangent)
        sine = cosine * tangent
        angle = jnp.where(alone, 0.0, jnp.abs(cross) * lax.rsqrt(jnp.maximum(own * other, 1e-30)))
        return jnp.where(alone, values, cosine * partner + sine * values), angle

    def sweep(carry):
        values, done, unused = carry
        worst = jnp.zeros((1, lanes), f32)
        for step in range(max(sizes)):
            values, angle = rotate(values, step % 2)
            worst = jnp.maximum(worst, angle)
        return values, done + 1, jnp.max(worst)

    def going(carry):
        return (carry[2] > 1e-4) & (carry[1] < 20)

    return lax.while_loop(going, sweep, (start, jnp.int32(0), jnp.float32(1.0)))[0]


def levels_kernel(
    couplings_ref, eigen_ref, to_high, to_low, from_high, from_low, edge_high, edge_low, jump_high, jump_low,
    ratio_ref, full_ref, weight_ref, *, group,
):
    modes, share = ratio_ref.shape
    all_modes, piece = full_ref.shape
    lanes = 128
    rows = to_high.shape[0]
    chunk = edge_high.shape[0]
    levels = modes // group
    top = -(-(all_modes + 1) // 8) * 8
    low = -(-all_modes // 8) * 8
    half, own = half_place()
    exact = functools.partial(jnp.dot, precision=highest, preferred_element_type=f32)

    def iota(shape, axis):
        return lax.broadcasted_iota(jnp.int32, shape, axis)

    def spot(condition):
        return jnp.where(condition, 1.0, 0.0)

    row, lane = iota((top, lanes), 0), iota((top, lanes), 1)
    in_first = lane < all_modes
    local = jnp.where(in_first, lane, lane - all_modes)
    used = lane < all_modes + modes
    weights = jnp.zeros((top, lanes), f32)
    for place in range(all_modes + 1):
        weights = jnp.where(in_first & (row == place), couplings_ref[place], weights)
    cut = jnp.where(half == 0, modes, 0)
    for place in range(modes + 1):
        value = couplings_ref[half * modes + place] * jnp.where(cut == place, 2.0, 1.0)
        weights = jnp.where(jnp.logical_not(in_first) & (row == place), value, weights)
    head = jnp.sqrt(weights) * (spot(used & (row == local)) - spot(used & (row == local + 1)))
    tail = spot(used & (row == local))[:low]
    turned = jacobi(jnp.concatenate([head, tail], 0), (all_modes, modes), top)
    head, vectors = turned[:top], turned[top : top + low]
    values = jnp.sum(head * head, axis=0, keepdims=True)

    at, to = iota((rows, low), 0), iota((rows, low), 1)
    section = at // (chunk * levels)
    level = lax.rem(own - section + group, group) * levels + lax.rem(at, levels)
    pick = spot(to == level)
    column = iota((lanes, rows), 1)
    place = spot(iota((lanes, rows), 0) == all_modes + lax.rem(column, modes))
    spread = exact(exact(pick, vectors), place)
    at, to = iota((rows, rows), 0), iota((rows, rows), 1)
    spread = jnp.where(lax.rem(at // levels, chunk) == to // modes, spread, 0.0)
    from_high[...], from_low[...] = split(spread)
    to_high[...], to_low[...] = split(spread.T)

    edge = jnp.where(half == 0, vectors[modes - 1 : modes], vectors[0:1])
    line = exact(jnp.broadcast_to(edge, (8, lanes)), place)[0:1]
    at, to = iota((chunk, rows), 0), iota((chunk, rows), 1)
    edge_high[...], edge_low[...] = split(jnp.where(at == to // modes, line, 0.0))
    jump = couplings_ref[modes] * (vectors[modes - 1 : modes] + vectors[modes : modes + 1])
    thin, plane_rows = jump_high.shape
    column = iota((lanes, plane_rows), 1)
    place = spot(iota((lanes, plane_rows), 0) == lax.rem(column, all_modes))
    line = exact(jnp.broadcast_to(jump * jump, (8, lanes)), place)[0:1]
    at, to = iota((thin, plane_rows), 0), iota((thin, plane_rows), 1)
    jump_high[...], jump_low[...] = split(jnp.where(at == to // all_modes, line, 0.0))

    def decay(count, first, mine):
        at, to = iota((count, lanes), 0), iota((count, lanes), 1)
        own_values = jnp.sum(jnp.where(to == at + first, values, 0.0), axis=1, keepdims=True)
        sigma = own_values + mine
        return 1.0 / (1.0 + 0.5 * sigma + jnp.sqrt(sigma + 0.25 * sigma * sigma))

    start = pl.multiple_of(own * share, share)
    ratio_ref[...] = decay(modes, all_modes, eigen_ref[:, pl.ds(start, share)])
    full_ref[...] = decay(all_modes, 0, eigen_ref[:, pl.ds(pl.multiple_of(start + half * piece, piece), piece)])
    at, to = iota((modes, lanes), 0), iota((modes, lanes), 1)
    weight = jnp.sum(jnp.where(to == at + all_modes, edge, 0.0), axis=1, keepdims=True)
    weight_ref[...] = jnp.broadcast_to(weight, (modes, share))


def power(value, exponent):
    result = None
    while exponent:
        if exponent % 2:
            result = value if result is None else result * value
        value = value * value
        exponent //= 2
    return result


def rows_place():
    me = lax.axis_index("rows")
    return me // 2, lax.rem(me, 2), lax.axis_size("rows") // 2


def partners():
    pair, place, pairs = rows_place()
    return [2 * pair + 1 - place] + [2 * lax.rem(pair + hop, pairs) + place for hop in range(1, pairs)]


def greet():
    barrier = pltpu.get_barrier_semaphore()
    for partner in partners():
        pl.semaphore_signal(barrier, inc=1, device_id={"rows": partner}, device_id_type=pl.DeviceIdType.MESH)


def exchange(row_count, ratio, ends, mate, total, others, send_sem, recv_sem):
    pair, place, pairs = rows_place()
    targets = partners()
    pl.semaphore_wait(pltpu.get_barrier_semaphore(), pairs)

    def copy(index, source, target):
        return pltpu.make_async_remote_copy(
            src_ref=source,
            dst_ref=target,
            send_sem=send_sem.at[index],
            recv_sem=recv_sem.at[index],
            device_id={"rows": targets[index]},
            device_id_type=pl.DeviceIdType.MESH,
        )

    near = copy(0, ends, mate)
    near.start()
    across = power(ratio, row_count)
    twice = across * across
    closing = 1.0 / (1.0 - power(twice, pairs))
    near.wait()
    is_first = place == 0
    first_f, last_f = jnp.where(is_first, ends[0], mate[0]), jnp.where(is_first, mate[0], ends[0])
    first_b, last_b = jnp.where(is_first, ends[1], mate[1]), jnp.where(is_first, mate[1], ends[1])
    total[0] = last_f + across * first_f
    total[1] = first_b + across * last_b
    far = [copy(hop, total, others.at[hop - 1]) for hop in range(1, pairs)]
    for one in far:
        one.start()
    for one in far:
        one.wait()
    before, after = total[0], total[1]
    for hop in range(pairs - 1, 0, -1):
        before = before * twice + others[hop - 1, 0]
        after = after * twice + others[pairs - hop - 1, 1]
    before, after = before * closing, after * closing
    before = jnp.where(is_first, before, first_f + across * before)
    after = jnp.where(is_first, last_b + across * after, after)
    last = ends[0] + across * before
    above = ratio * (ratio * last + after) / (1.0 - ratio * ratio)
    return before, above


def to_modes_kernel(*refs):
    x_refs = refs[:-12]
    high_ref, low_ref, ratio_ref, modes_ref, edge_ref, scale_ref, ends, mate, total, others, send_sem, recv_sem = refs[-12:]
    modes, share = ratio_ref.shape
    step = pl.program_id(0)

    @pl.when(step == 0)
    def _():
        greet()
        ends[...] = jnp.zeros(ends.shape, f32)
        scale_ref[...] = jnp.ones(scale_ref.shape, f32)

    values = jnp.concatenate([x_ref[...] for x_ref in x_refs], 0)
    modes_ref[...] = dot3((high_ref[...], low_ref[...]), split(values))
    ratio = ratio_ref[...]
    first, last, scale = ends[0], ends[1], scale_ref[...]
    rows = modes_ref.shape[0] // modes
    for row in range(rows):
        current = modes_ref[row * modes : (row + 1) * modes, :]
        first = first * ratio + current
        last = last + scale * current
        scale = scale * ratio
    ends[0] = first
    ends[1] = last
    scale_ref[...] = scale

    @pl.when(step == pl.num_programs(0) - 1)
    def _():
        count = rows * pl.num_programs(0)
        edge_ref[0], edge_ref[1] = exchange(count, ratio_ref[...], ends, mate, total, others, send_sem, recv_sem)


def two_way(rows, ratio_ref, edge_ref, held, chunk, carry, source, finish):
    step = pl.program_id(0)
    steps = pl.num_programs(0) // 2
    modes = ratio_ref.shape[0]
    ratio = ratio_ref[...]

    @pl.when(step == 0)
    def _():
        carry[...] = edge_ref[0]

    @pl.when(step == steps)
    def _():
        carry[...] = edge_ref[1]

    @pl.when(step < steps)
    def _():
        base = pl.multiple_of(step * rows * modes, rows * modes)
        value = carry[...]
        for row in range(rows):
            value = value * ratio + source(row)
            held[pl.ds(base + row * modes, modes), :] = value
        carry[...] = value

    @pl.when(step >= steps)
    def _():
        base = pl.multiple_of((2 * steps - 1 - step) * rows * modes, rows * modes)
        value = carry[...]
        for row in reversed(range(rows)):
            value = (value + held[pl.ds(base + row * modes, modes), :]) * ratio
            chunk[row * modes : (row + 1) * modes, :] = value
        carry[...] = value
        finish(split(chunk[...]))


def interface_kernel(modes_ref, high_ref, low_ref, ratio_ref, edge_ref, keep_ref, send_ref, held, chunk, carry, line):
    modes = ratio_ref.shape[0]
    piece = keep_ref.shape[1]
    half, _ = half_place()

    def finish(values):
        line[...] = dot3((high_ref[...], low_ref[...]), values)
        keep_ref[...] = line[:, pl.ds(pl.multiple_of(half * piece, piece), piece)]
        send_ref[...] = line[:, pl.ds(pl.multiple_of((1 - half) * piece, piece), piece)]

    two_way(
        keep_ref.shape[0], ratio_ref, edge_ref, held, chunk, carry,
        lambda row: modes_ref[row * modes : (row + 1) * modes, :], finish,
    )


def plane_ends(plane_ref, ratio_ref, ends, weight):
    rows = plane_ref.shape[0]
    shape = ratio_ref.shape
    ratio = ratio_ref[...]

    def group(index, carry):
        first, last, scale = carry
        lines = plane_ref[pl.ds(pl.multiple_of(index * BY, BY), BY), :]
        for row in range(BY):
            current = jnp.broadcast_to(lines[row : row + 1], shape)
            first = first * ratio + current
            last = last + scale * current
            scale = scale * ratio
        return first, last, scale

    zero = jnp.zeros(shape, f32)
    first, last, _ = lax.fori_loop(0, rows // BY, group, (zero, zero, jnp.ones(shape, f32)))
    ends[0] = first if weight is None else first * weight
    ends[1] = last if weight is None else last * weight


def sum_kernel(own_ref, other_ref, ratio_ref, plane_ref, edge_ref, ends, *rest):
    greet()
    plane_ref[...] = own_ref[...] + other_ref[...]
    plane_ends(plane_ref, ratio_ref, ends, None)
    edge_ref[0], edge_ref[1] = exchange(plane_ref.shape[0], ratio_ref[...], ends, *rest)


def join_kernel(own_ref, other_ref, ratio_ref, weight_ref, known_ref, plane_ref, edge_ref, ends, *rest):
    greet()
    half, _ = half_place()
    piece = own_ref.shape[1]
    plane_ref[:, pl.ds(pl.multiple_of(half * piece, piece), piece)] = own_ref[...]
    plane_ref[:, pl.ds(pl.multiple_of((1 - half) * piece, piece), piece)] = other_ref[...]
    plane_ends(plane_ref, ratio_ref, ends, weight_ref[...])
    before, above = exchange(plane_ref.shape[0], ratio_ref[...], ends, *rest)
    edge_ref[0] = known_ref[0] + before
    edge_ref[1] = known_ref[1] + above


def couple_kernel(
    plane_ref, again_ref, high_ref, low_ref, ratio_ref, edge_ref, couplings_ref, out_ref, held, chunk, carry
):
    shape = ratio_ref.shape
    strength = couplings_ref[shape[0] // 2]

    def finish(values):
        out_ref[...] = dot3((high_ref[...], low_ref[...]), values) + again_ref[...] * strength

    two_way(
        out_ref.shape[0], ratio_ref, edge_ref, held, chunk, carry,
        lambda row: jnp.broadcast_to(plane_ref[row : row + 1, :], shape), finish,
    )


def from_modes_kernel(modes_ref, plane_ref, weight_ref, high_ref, low_ref, ratio_ref, edge_ref, *rest, group):
    out_refs, (held, chunk, carry, *remote) = rest[:group], rest[group:]
    modes, share = ratio_ref.shape
    rows = plane_ref.shape[0]
    weight = weight_ref[...]
    step = pl.program_id(0)
    steps = pl.num_programs(0) // 2
    half, own = half_place()
    each = out_refs[0].shape[0]
    targets = [half * group + lax.rem(own + group - hop, group) for hop in range(1, group)]

    def copy(hop, index):
        outgoing, send_sem, recv_sem = remote
        place = pl.ds(pl.multiple_of(index * each, each), each)
        return pltpu.make_async_remote_copy(
            src_ref=outgoing.at[hop - 1, place],
            dst_ref=out_refs[hop].at[place],
            send_sem=send_sem.at[hop - 1, index],
            recv_sem=recv_sem.at[hop - 1, index],
            device_id={"lev": targets[hop - 1]},
            device_id_type=pl.DeviceIdType.MESH,
        )

    if group > 1:

        @pl.when(step == 0)
        def _():
            barrier = pltpu.get_barrier_semaphore()
            for target in targets:
                pl.semaphore_signal(barrier, inc=1, device_id={"lev": target}, device_id_type=pl.DeviceIdType.MESH)

        @pl.when(step == steps)
        def _():
            pl.semaphore_wait(pltpu.get_barrier_semaphore(), group - 1)

    def finish(values):
        result = dot3((high_ref[...], low_ref[...]), values)
        out_refs[0][...] = result[:each]
        index = 2 * steps - 1 - step
        for hop in range(1, group):
            remote[0][hop - 1, pl.ds(pl.multiple_of(index * each, each), each), :] = result[hop * each : (hop + 1) * each]
            copy(hop, index).start()

    two_way(
        rows, ratio_ref, edge_ref, held, chunk, carry,
        lambda row: modes_ref[row * modes : (row + 1) * modes, :] + weight * plane_ref[row : row + 1, :], finish,
    )

    if group > 1:

        @pl.when(step == 2 * steps - 1)
        def _():
            def settle(index, unused):
                for hop in range(1, group):
                    copy(hop, index).wait()
                return unused

            lax.fori_loop(0, steps, settle, 0)


def params(collective_id=None, room=VMEM_BYTES):
    if collective_id is None:
        return pltpu.CompilerParams(vmem_limit_bytes=room)
    return pltpu.CompilerParams(vmem_limit_bytes=room, collective_id=collective_id, has_side_effects=True)


def exchange_scratch(shape, row_devices):
    pairs = row_devices // 2
    two = (2,) + shape
    return [pltpu.VMEM(two, f32)] * 3 + [
        pltpu.VMEM((pairs - 1,) + two, f32),
        pltpu.SemaphoreType.DMA((pairs,)),
        pltpu.SemaphoreType.DMA((pairs,)),
    ]


def cost(flops, moved):
    return pl.CostEstimate(flops=int(flops), bytes_accessed=int(moved), transcendentals=0)


def whole(shape):
    return pl.BlockSpec(shape, lambda *index: (0,) * len(shape))


def struct(*shape):
    return jax.ShapeDtypeStruct(shape, f32)


def body(source, solid, couplings):
    row_count, levels, length = source.shape
    lev_devices = lax.axis_size("lev")
    row_devices = lax.axis_size("rows")
    group = lev_devices // 2
    share = length // group
    piece = share // 2
    width = length // PARTS
    half_levels = levels * group
    all_levels = 2 * half_levels
    tile = 64 if row_count % 64 == 0 else BY
    size = source.size

    def passed(value, shift):
        pairs = [
            (side * group + place, side * group + (place + shift) % group) for side in range(2) for place in range(group)
        ]
        return lax.ppermute(value, "lev", pairs)

    def across_halves(value):
        return lax.ppermute(value, "lev", [(place, (place + group) % lev_devices) for place in range(lev_devices)])

    blocks, eigen_x = x_tables(length)
    forward_table = blocks.astype(np.float32)
    backward_table = np.swapaxes(blocks, 1, 2).astype(np.float32)
    groups = tile // BY * 8
    table = whole(blocks.shape)
    part_spec = pl.BlockSpec((tile * levels, share), lambda i: (i, 0))
    field_spec = pl.BlockSpec((tile, levels, length), lambda i: (i, 0, 0))
    mixed = pltpu.VMEM((PARTS // 2, levels * tile, 2 * width), f32)
    halves = [pltpu.VMEM(blocks.shape, bf16)] * 2
    spectral = pl.pallas_call(
        forward_kernel,
        grid=(row_count // tile,),
        in_specs=[field_spec, pl.BlockSpec((tile // BY, levels, length // BX), lambda i: (i, 0, 0)), table],
        out_specs=[part_spec] * group,
        out_shape=[struct(row_count * levels, share)] * group,
        scratch_shapes=[pltpu.VMEM((groups, length), f32), mixed] + halves,
        compiler_params=params(room=ALL_VMEM_BYTES),
        cost_estimate=cost(6 * size * 2 * width, 8 * size),
        name="forward_x",
    )(source, solid, forward_table)
    sections = [spectral[0]] + [passed(spectral[shift], shift) for shift in range(1, group)]

    chunk = max(BY, 256 // half_levels)
    thin = max(BY, 256 // all_levels)
    rows = chunk * half_levels
    plane_rows = thin * all_levels
    in_smem = pl.BlockSpec(memory_space=pltpu.SMEM)
    built = [(rows, rows)] * 4 + [(chunk, rows)] * 2 + [(thin, plane_rows)] * 2
    *matrices, ratio, full_ratio, weight = pl.pallas_call(
        functools.partial(levels_kernel, group=group),
        in_specs=[in_smem, pl.BlockSpec(memory_space=pltpu.VMEM)],
        out_shape=[jax.ShapeDtypeStruct(each, bf16) for each in built]
        + [struct(half_levels, share), struct(all_levels, piece), struct(half_levels, share)],
        compiler_params=params(),
        name="levels",
    )(couplings, eigen_x[None, :])
    to_modes, from_modes, to_edge, to_jump = (matrices[2 * index : 2 * index + 2] for index in range(4))

    steps = row_count // chunk
    plane_steps = row_count // thin
    shape = (half_levels, share)
    plane_shape = (all_levels, piece)
    modes_shape = struct(row_count * half_levels, share)
    section_spec = pl.BlockSpec((chunk * levels, share), lambda i: (i, 0))

    def ahead(count):
        return lambda i: (jnp.minimum(i, count - 1), 0)

    def behind(count):
        return lambda i: (jnp.minimum(2 * count - 1 - i, count - 1), 0)

    def scratch(rows, shape):
        return [pltpu.VMEM((row_count * shape[0], shape[1]), f32), pltpu.VMEM((rows, shape[1]), f32), pltpu.VMEM(shape, f32)]

    modes, edge = pl.pallas_call(
        to_modes_kernel,
        grid=(steps,),
        in_specs=[section_spec] * group + [whole((rows, rows))] * 2 + [whole(shape)],
        out_specs=[pl.BlockSpec((rows, share), lambda i: (i, 0)), whole((2,) + shape)],
        out_shape=[modes_shape, struct(2, *shape)],
        scratch_shapes=[pltpu.VMEM(shape, f32)] + exchange_scratch(shape, row_devices),
        compiler_params=params(0, ALL_VMEM_BYTES),
        cost_estimate=cost(6 * size * rows, 8 * size),
        name="to_modes",
    )(*sections, *to_modes, ratio)

    kept, sent = pl.pallas_call(
        interface_kernel,
        grid=(2 * steps,),
        in_specs=[pl.BlockSpec((rows, share), ahead(steps))] + [whole((chunk, rows))] * 2 + [whole(shape), whole((2,) + shape)],
        out_specs=[pl.BlockSpec((chunk, piece), behind(steps))] * 2,
        out_shape=[struct(row_count, piece)] * 2,
        scratch_shapes=scratch(rows, shape) + [pltpu.VMEM((chunk, share), f32)],
        compiler_params=params(),
        cost_estimate=cost(6 * size * chunk, 5 * size),
        name="interface",
    )(modes, *to_edge, ratio, edge)

    plane, plane_edge = pl.pallas_call(
        sum_kernel,
        out_shape=[struct(row_count, piece), struct(2, *plane_shape)],
        scratch_shapes=exchange_scratch(plane_shape, row_devices),
        compiler_params=params(1),
        name="plane_sum",
    )(kept, across_halves(sent), full_ratio)

    moved = pl.pallas_call(
        couple_kernel,
        grid=(2 * plane_steps,),
        in_specs=[
            pl.BlockSpec((thin, piece), ahead(plane_steps)),
            pl.BlockSpec((thin, piece), behind(plane_steps)),
            whole((thin, plane_rows)),
            whole((thin, plane_rows)),
            whole(plane_shape),
            whole((2,) + plane_shape),
            in_smem,
        ],
        out_specs=pl.BlockSpec((thin, piece), behind(plane_steps)),
        out_shape=struct(row_count, piece),
        scratch_shapes=scratch(plane_rows, plane_shape),
        compiler_params=params(),
        cost_estimate=cost(6 * size * thin, 2 * size),
        name="couple",
    )(plane, plane, *to_jump, full_ratio, plane_edge, couplings)

    joined, edge = pl.pallas_call(
        join_kernel,
        out_shape=[struct(row_count, share), struct(2, *shape)],
        scratch_shapes=exchange_scratch(shape, row_devices),
        compiler_params=params(2),
        name="plane_join",
    )(moved, across_halves(moved), ratio, weight, edge)

    outgoing = [
        pltpu.VMEM((group - 1, row_count * levels, share), f32),
        pltpu.SemaphoreType.DMA((group - 1, steps)),
        pltpu.SemaphoreType.DMA((group - 1, steps)),
    ]
    returned = pl.pallas_call(
        functools.partial(from_modes_kernel, group=group),
        grid=(2 * steps,),
        in_specs=[pl.BlockSpec((rows, share), ahead(steps)), pl.BlockSpec((chunk, share), ahead(steps)), whole(shape)]
        + [whole((rows, rows))] * 2
        + [whole(shape), whole((2,) + shape)],
        out_specs=[pl.BlockSpec((chunk * levels, share), behind(steps))] + [pl.BlockSpec(memory_space=pl.ANY)] * (group - 1),
        out_shape=[struct(row_count * levels, share)] * group,
        scratch_shapes=scratch(rows, shape) + (outgoing if group > 1 else []),
        compiler_params=params(3 if group > 1 else None),
        cost_estimate=cost(6 * size * rows, 8 * size),
        name="from_modes",
    )(modes, joined, weight, *from_modes, ratio, edge)
    return pl.pallas_call(
        backward_kernel,
        grid=(row_count // tile,),
        in_specs=[part_spec] * group + [table],
        out_specs=field_spec,
        out_shape=struct(*source.shape),
        scratch_shapes=[mixed] + halves,
        compiler_params=params(room=ALL_VMEM_BYTES),
        cost_estimate=cost(6 * size * 2 * width, 8 * size),
        name="backward_x",
    )(*returned, backward_table)


def solution(mesh):
    return jax.shard_map(
        body,
        mesh=mesh,
        in_specs=(P("rows", "lev", None), P("rows", "lev", None), P()),
        out_specs=P("rows", "lev", None),
        check_vma=False,
    )
```

```python
import functools
import math

import numpy as np

import jax
import jax.numpy as jnp
from jax import lax
from jax.experimental import pallas as pl
from jax.experimental.pallas import tpu as pltpu
from jax.sharding import PartitionSpec as P

BY = 8
BX = 64
PARTS = 16
VMEM_BYTES = 48 * 1024 * 1024
ALL_VMEM_BYTES = 60 * 1024 * 1024

f32 = jnp.float32
highest = lax.Precision.HIGHEST
bf16 = jnp.bfloat16


def split(values):
    high = values.astype(bf16)
    low = (values - high.astype(f32)).astype(bf16)
    return high, low


def dot3(left, right):
    dot = functools.partial(jnp.dot, preferred_element_type=f32)
    return dot(left[0], right[0]) + (dot(left[0], right[1]) + dot(left[1], right[0]))


@functools.lru_cache(None)
def x_tables(length):
    width = length // PARTS
    half = PARTS // 2
    place = np.arange(width)
    blocks = np.zeros((half, 2 * width, 2 * width))
    slots = np.zeros((half, 2 * width))
    inner = math.sqrt(2.0 / length)
    edge = math.sqrt(1.0 / length)

    def angle(freq):
        return 2.0 * math.pi * (np.outer(place, freq) % length) / length

    low = PARTS * np.arange(width // 2 + 1)
    weight = np.where((low == 0) | (low == length // 2), edge, inner)
    cosines = np.cos(angle(low)) * weight
    sines = np.sin(angle(low[1:-1])) * inner
    blocks[0, :width, :width] = np.concatenate([cosines, sines], 1)
    slots[0, :width] = np.concatenate([low, low[1:-1]])
    middle = half + PARTS * np.arange(width // 2)
    blocks[0, width:, width:] = np.concatenate([np.cos(angle(middle)), np.sin(angle(middle))], 1) * inner
    slots[0, width:] = np.concatenate([middle, middle])
    for first in range(1, half):
        freq = first + PARTS * np.arange(width)
        turn = angle(freq)
        cosines, sines = np.cos(turn) * inner, np.sin(turn) * inner
        blocks[first] = np.block([[cosines, -sines], [sines, cosines]])
        slots[first] = np.concatenate([freq, freq])
    eigen = 4.0 * np.sin(math.pi * slots.reshape(-1) / length) ** 2
    return blocks, eigen.astype(np.float32)


def turn(index):
    return math.cos(2.0 * math.pi * index / PARTS), math.sin(2.0 * math.pi * index / PARTS)


def stage(x):
    s = [x[b] + x[b + 8] for b in range(8)]
    d = [x[b] - x[b + 8] for b in range(8)]
    out = [None] * 8
    minus = [d[b] - d[8 - b] for b in range(1, 4)]
    plus = [d[b] + d[8 - b] for b in range(1, 4)]
    for first in (1, 3, 5, 7):
        real = d[0]
        imag = d[4] * (-turn(4 * first)[1])
        for b in (1, 2, 3):
            cosine, sine = turn(b * first)
            real = real + minus[b - 1] * cosine
            imag = imag - plus[b - 1] * sine
        out[first] = (real, imag)
    ss = [s[b] + s[b + 4] for b in range(4)]
    sd = [s[b] - s[b + 4] for b in range(4)]
    root = math.sqrt(0.5)
    m = (sd[1] - sd[3]) * root
    p = (sd[1] + sd[3]) * root
    out[2] = (sd[0] + m, -p - sd[2])
    out[6] = (sd[0] - m, sd[2] - p)
    out[4] = (ss[0] - ss[2], ss[3] - ss[1])
    even, odd = ss[0] + ss[2], ss[1] + ss[3]
    out[0] = (even + odd, even - odd)
    return out


def unstage(y):
    root = math.sqrt(0.5)
    even, odd = y[0][0] + y[0][1], y[0][0] - y[0][1]
    ss = [even + y[4][0], odd - y[4][1], even - y[4][0], odd + y[4][1]]
    m = (y[2][0] - y[6][0]) * root
    p = (y[2][1] + y[6][1]) * root
    sd = [y[2][0] + y[6][0], m - p, y[6][1] - y[2][1], -m - p]
    s = [ss[b] + sd[b] for b in range(4)] + [ss[b] - sd[b] for b in range(4)]
    d = [None] * 8
    d[0] = (y[1][0] + y[3][0]) + (y[5][0] + y[7][0])
    d[4] = (y[3][1] - y[1][1]) + (y[7][1] - y[5][1])
    for b in (1, 2, 3):
        real = None
        imag = None
        for first in (1, 3, 5, 7):
            cosine, sine = turn(b * first)
            term, other = y[first][0] * cosine, y[first][1] * sine
            real = term if real is None else real + term
            imag = other if imag is None else imag + other
        d[b] = real - imag
        d[8 - b] = -real - imag
    return [s[b] + d[b] for b in range(8)] + [s[b] - d[b] for b in range(8)]


def half_place():
    group = lax.axis_size("lev") // 2
    me = lax.axis_index("lev")
    return me // group, me % group


def block_of(index, share, length):
    blocks = PARTS // 2
    _, own = half_place()
    return lax.rem(index + own * (share * blocks // length), blocks)


def keep_split(table_ref, high_ref, low_ref):
    @pl.when(pl.program_id(0) == 0)
    def _():
        for block in range(table_ref.shape[0]):
            high_ref[block], low_ref[block] = split(table_ref[block])


def forward_kernel(x_ref, solid_ref, table_ref, *rest):
    out_refs, (kept, mixed, high_ref, low_ref) = rest[:-4], rest[-4:]
    rows, levels, length = x_ref.shape
    width = length // PARTS
    share = out_refs[0].shape[1]
    pair = 8 // levels
    keep_split(table_ref, high_ref, low_ref)
    shape = (length // BX, length)
    first = lax.broadcasted_iota(jnp.int32, shape, 0) * BX
    lane = lax.broadcasted_iota(jnp.int32, shape, 1)
    spread = jnp.where((lane >= first) & (lane < first + BX), 1.0, 0.0).astype(bf16)
    keep = (1 - solid_ref[...]).astype(f32)
    keep = jnp.concatenate([keep] * pair, 1).reshape(kept.shape[0], length // BX)
    kept[...] = jnp.dot(keep.astype(bf16), spread, preferred_element_type=f32)

    def group(index, unused):
        mask = kept[pl.ds(pl.multiple_of(index * 8, 8), 8), :]
        for part in range(BY // pair):
            row = index * BY + part * pair
            x = [
                x_ref[pl.ds(row, pair), :, pl.ds(b * width, width)].reshape(8, width)
                * mask[:, b * width : (b + 1) * width]
                for b in range(PARTS)
            ]
            base = pl.multiple_of(row * levels, 8)
            for block, (real, imag) in enumerate(stage(x)):
                mixed[block, pl.ds(base, 8), :width] = real
                mixed[block, pl.ds(base, 8), width:] = imag
        return unused

    lax.fori_loop(0, rows // BY, group, 0)
    for index in range(PARTS // 2):
        block = block_of(index, share, length)
        product = dot3(split(mixed[block]), (high_ref[block], low_ref[block]))
        target, offset = divmod(2 * index * width, share)
        out_refs[target][:, offset : offset + 2 * width] = product


def backward_kernel(*refs):
    x_refs, (table_ref, out_ref, mixed, high_ref, low_ref) = refs[:-5], refs[-5:]
    rows, levels, length = out_ref.shape
    width = length // PARTS
    share = x_refs[0].shape[1]
    pair = 8 // levels
    keep_split(table_ref, high_ref, low_ref)
    for index in range(PARTS // 2):
        block = block_of(index, share, length)
        source, offset = divmod(2 * index * width, share)
        values = split(x_refs[source][:, offset : offset + 2 * width])
        mixed[block] = dot3(values, (high_ref[block], low_ref[block]))

    def group(index, unused):
        row = index * pair
        base = pl.multiple_of(index * 8, 8)
        y = [
            (mixed[block, pl.ds(base, 8), :width], mixed[block, pl.ds(base, 8), width:])
            for block in range(PARTS // 2)
        ]
        for b, value in enumerate(unstage(y)):
            out_ref[pl.ds(row, pair), :, pl.ds(b * width, width)] = value.reshape(pair, levels, width)
        return unused

    lax.fori_loop(0, rows // pair, group, 0, unroll=4)


def jacobi(start, sizes, top):
    lanes = start.shape[1]
    lane = lax.broadcasted_iota(jnp.int32, (1, lanes), 1)
    in_first = lane < sizes[0]
    local = jnp.where(in_first, lane, lane - sizes[0])
    count = jnp.where(in_first, sizes[0], sizes[1])

    def rotate(values, parity):
        is_left = local % 2 == parity
        alone = (lane >= sum(sizes)) | (is_left & (local == count - 1)) | (jnp.logical_not(is_left) & (local == 0))
        partner = jnp.where(is_left, pltpu.roll(values, lanes - 1, 1), pltpu.roll(values, 1, 1))
        head = values[:top]
        head_partner = partner[:top]
        own = jnp.sum(head * head, axis=0, keepdims=True)
        other = jnp.sum(head_partner * head_partner, axis=0, keepdims=True)
        cross = jnp.sum(head * head_partner, axis=0, keepdims=True)
        delta = other - own
        sign = jnp.where((delta > 0) | ((delta == 0) & is_left), 1.0, -1.0)
        bottom = jnp.abs(delta) + jnp.sqrt(delta * delta + 4.0 * cross * cross)
        tangent = 2.0 * cross * sign / jnp.maximum(bottom, 1e-30)
        cosine = 1.0 / jnp.sqrt(1.0 + tangent * tangent)
        sine = cosine * tangent
        angle = jnp.where(alone, 0.0, jnp.abs(cross) * lax.rsqrt(jnp.maximum(own * other, 1e-30)))
        return jnp.where(alone, values, cosine * partner + sine * values), angle

    def sweep(carry):
        values, done, unused = carry
        worst = jnp.zeros((1, lanes), f32)
        for step in range(max(sizes)):
            values, angle = rotate(values, step % 2)
            worst = jnp.maximum(worst, angle)
        return values, done + 1, jnp.max(worst)

    def going(carry):
        return (carry[2] > 1e-4) & (carry[1] < 20)

    return lax.while_loop(going, sweep, (start, jnp.int32(0), jnp.float32(1.0)))[0]


def levels_kernel(
    couplings_ref, eigen_ref, to_high, to_low, from_high, from_low, edge_high, edge_low, jump_high, jump_low,
    ratio_ref, full_ref, weight_ref, *, group,
):
    modes, share = ratio_ref.shape
    all_modes, piece = full_ref.shape
    lanes = 128
    rows = to_high.shape[0]
    chunk = rows // modes
    levels = modes // group
    top = -(-(all_modes + 1) // 8) * 8
    low = -(-all_modes // 8) * 8
    half, own = half_place()
    exact = functools.partial(jnp.dot, precision=highest, preferred_element_type=f32)

    def iota(shape, axis):
        return lax.broadcasted_iota(jnp.int32, shape, axis)

    def spot(condition):
        return jnp.where(condition, 1.0, 0.0)

    row, lane = iota((top, lanes), 0), iota((top, lanes), 1)
    in_first = lane < all_modes
    local = jnp.where(in_first, lane, lane - all_modes)
    used = lane < all_modes + modes
    weights = jnp.zeros((top, lanes), f32)
    for place in range(all_modes + 1):
        weights = jnp.where(in_first & (row == place), couplings_ref[place], weights)
    cut = jnp.where(half == 0, modes, 0)
    for place in range(modes + 1):
        value = couplings_ref[half * modes + place] * jnp.where(cut == place, 2.0, 1.0)
        weights = jnp.where(jnp.logical_not(in_first) & (row == place), value, weights)
    head = jnp.sqrt(weights) * (spot(used & (row == local)) - spot(used & (row == local + 1)))
    tail = spot(used & (row == local))[:low]
    turned = jacobi(jnp.concatenate([head, tail], 0), (all_modes, modes), top)
    head, vectors = turned[:top], turned[top : top + low]
    values = jnp.sum(head * head, axis=0, keepdims=True)

    at, to = iota((rows, low), 0), iota((rows, low), 1)
    section = at // (chunk * levels)
    level = lax.rem(own - section + group, group) * levels + lax.rem(at, levels)
    pick = spot(to == level)
    column = iota((lanes, rows), 1)
    place = spot(iota((lanes, rows), 0) == all_modes + lax.rem(column, modes))
    spread = exact(exact(pick, vectors), place)
    at, to = iota((rows, rows), 0), iota((rows, rows), 1)
    spread = jnp.where(lax.rem(at // levels, chunk) == to // modes, spread, 0.0)
    from_high[...], from_low[...] = split(spread)
    to_high[...], to_low[...] = split(spread.T)

    edge = jnp.where(half == 0, vectors[modes - 1 : modes], vectors[0:1])
    wide, wide_rows = edge_high.shape
    column = iota((lanes, wide_rows), 1)
    place = spot(iota((lanes, wide_rows), 0) == all_modes + lax.rem(column, modes))
    line = exact(jnp.broadcast_to(edge, (8, lanes)), place)[0:1]
    at, to = iota((wide, wide_rows), 0), iota((wide, wide_rows), 1)
    edge_high[...], edge_low[...] = split(jnp.where(at == to // modes, line, 0.0))
    jump = couplings_ref[modes] * (vectors[modes - 1 : modes] + vectors[modes : modes + 1])
    thin, plane_rows = jump_high.shape
    column = iota((lanes, plane_rows), 1)
    place = spot(iota((lanes, plane_rows), 0) == lax.rem(column, all_modes))
    line = exact(jnp.broadcast_to(jump * jump, (8, lanes)), place)[0:1]
    at, to = iota((thin, plane_rows), 0), iota((thin, plane_rows), 1)
    jump_high[...], jump_low[...] = split(jnp.where(at == to // all_modes, line, 0.0))

    def decay(count, first, mine):
        at, to = iota((count, lanes), 0), iota((count, lanes), 1)
        own_values = jnp.sum(jnp.where(to == at + first, values, 0.0), axis=1, keepdims=True)
        sigma = own_values + mine
        return 1.0 / (1.0 + 0.5 * sigma + jnp.sqrt(sigma + 0.25 * sigma * sigma))

    start = pl.multiple_of(own * share, share)
    ratio_ref[...] = decay(modes, all_modes, eigen_ref[:, pl.ds(start, share)])
    full_ref[...] = decay(all_modes, 0, eigen_ref[:, pl.ds(pl.multiple_of(start + half * piece, piece), piece)])
    at, to = iota((modes, lanes), 0), iota((modes, lanes), 1)
    weight = jnp.sum(jnp.where(to == at + all_modes, edge, 0.0), axis=1, keepdims=True)
    weight_ref[...] = jnp.broadcast_to(weight, (modes, share))


def power(value, exponent):
    result = None
    while exponent:
        if exponent % 2:
            result = value if result is None else result * value
        value = value * value
        exponent //= 2
    return result


def rows_place():
    me = lax.axis_index("rows")
    return me // 2, lax.rem(me, 2), lax.axis_size("rows") // 2


def partners():
    pair, place, pairs = rows_place()
    return [2 * pair + 1 - place] + [2 * lax.rem(pair + hop, pairs) + place for hop in range(1, pairs)]


def greet():
    barrier = pltpu.get_barrier_semaphore()
    for partner in partners():
        pl.semaphore_signal(barrier, inc=1, device_id={"rows": partner}, device_id_type=pl.DeviceIdType.MESH)


def exchange(row_count, ratio, ends, mate, total, others, send_sem, recv_sem):
    pair, place, pairs = rows_place()
    targets = partners()
    pl.semaphore_wait(pltpu.get_barrier_semaphore(), pairs)

    def copy(index, source, target):
        return pltpu.make_async_remote_copy(
            src_ref=source,
            dst_ref=target,
            send_sem=send_sem.at[index],
            recv_sem=recv_sem.at[index],
            device_id={"rows": targets[index]},
            device_id_type=pl.DeviceIdType.MESH,
        )

    near = copy(0, ends, mate)
    near.start()
    across = power(ratio, row_count)
    twice = across * across
    closing = 1.0 / (1.0 - power(twice, pairs))
    near.wait()
    is_first = place == 0
    first_f, last_f = jnp.where(is_first, ends[0], mate[0]), jnp.where(is_first, mate[0], ends[0])
    first_b, last_b = jnp.where(is_first, ends[1], mate[1]), jnp.where(is_first, mate[1], ends[1])
    total[0] = last_f + across * first_f
    total[1] = first_b + across * last_b
    far = [copy(hop, total, others.at[hop - 1]) for hop in range(1, pairs)]
    for one in far:
        one.start()
    for one in far:
        one.wait()
    before, after = total[0], total[1]
    for hop in range(pairs - 1, 0, -1):
        before = before * twice + others[hop - 1, 0]
        after = after * twice + others[pairs - hop - 1, 1]
    before, after = before * closing, after * closing
    before = jnp.where(is_first, before, first_f + across * before)
    after = jnp.where(is_first, last_b + across * after, after)
    last = ends[0] + across * before
    above = ratio * (ratio * last + after) / (1.0 - ratio * ratio)
    return before, above


def to_modes_kernel(*refs):
    x_refs = refs[:-12]
    high_ref, low_ref, ratio_ref, modes_ref, edge_ref, scale_ref, ends, mate, total, others, send_sem, recv_sem = refs[-12:]
    modes, share = ratio_ref.shape
    step = pl.program_id(0)

    @pl.when(step == 0)
    def _():
        greet()
        ends[...] = jnp.zeros(ends.shape, f32)
        scale_ref[...] = jnp.ones(scale_ref.shape, f32)

    values = jnp.concatenate([x_ref[...] for x_ref in x_refs], 0)
    modes_ref[...] = dot3((high_ref[...], low_ref[...]), split(values))
    ratio = ratio_ref[...]
    first, last, scale = ends[0], ends[1], scale_ref[...]
    rows = modes_ref.shape[0] // modes
    for row in range(rows):
        current = modes_ref[row * modes : (row + 1) * modes, :]
        first = first * ratio + current
        last = last + scale * current
        scale = scale * ratio
    ends[0] = first
    ends[1] = last
    scale_ref[...] = scale

    @pl.when(step == pl.num_programs(0) - 1)
    def _():
        count = rows * pl.num_programs(0)
        edge_ref[0], edge_ref[1] = exchange(count, ratio_ref[...], ends, mate, total, others, send_sem, recv_sem)


def two_way(rows, ratio_ref, edge_ref, held, chunk, carry, source, finish):
    step = pl.program_id(0)
    steps = pl.num_programs(0) // 2
    modes = ratio_ref.shape[0]
    ratio = ratio_ref[...]

    @pl.when(step == 0)
    def _():
        carry[...] = edge_ref[0]

    @pl.when(step == steps)
    def _():
        carry[...] = edge_ref[1]

    @pl.when(step < steps)
    def _():
        base = pl.multiple_of(step * rows * modes, rows * modes)
        value = carry[...]
        for row in range(rows):
            value = value * ratio + source(row)
            held[pl.ds(base + row * modes, modes), :] = value
        carry[...] = value

    @pl.when(step >= steps)
    def _():
        base = pl.multiple_of((2 * steps - 1 - step) * rows * modes, rows * modes)
        value = carry[...]
        for row in reversed(range(rows)):
            value = (value + held[pl.ds(base + row * modes, modes), :]) * ratio
            chunk[row * modes : (row + 1) * modes, :] = value
        carry[...] = value
        finish(split(chunk[...]))


def interface_kernel(modes_ref, high_ref, low_ref, ratio_ref, edge_ref, keep_ref, send_ref, held, chunk, carry, line):
    modes = ratio_ref.shape[0]
    piece = keep_ref.shape[1]
    half, _ = half_place()

    def finish(values):
        line[...] = dot3((high_ref[...], low_ref[...]), values)
        keep_ref[...] = line[:, pl.ds(pl.multiple_of(half * piece, piece), piece)]
        send_ref[...] = line[:, pl.ds(pl.multiple_of((1 - half) * piece, piece), piece)]

    two_way(
        keep_ref.shape[0], ratio_ref, edge_ref, held, chunk, carry,
        lambda row: modes_ref[row * modes : (row + 1) * modes, :], finish,
    )


def plane_ends(plane_ref, ratio_ref, ends, weight):
    rows = plane_ref.shape[0]
    shape = ratio_ref.shape
    ratio = ratio_ref[...]

    def group(index, carry):
        first, last, scale = carry
        lines = plane_ref[pl.ds(pl.multiple_of(index * BY, BY), BY), :]
        for row in range(BY):
            current = jnp.broadcast_to(lines[row : row + 1], shape)
            first = first * ratio + current
            last = last + scale * current
            scale = scale * ratio
        return first, last, scale

    zero = jnp.zeros(shape, f32)
    first, last, _ = lax.fori_loop(0, rows // BY, group, (zero, zero, jnp.ones(shape, f32)))
    ends[0] = first if weight is None else first * weight
    ends[1] = last if weight is None else last * weight


def sum_kernel(own_ref, other_ref, ratio_ref, plane_ref, edge_ref, ends, *rest):
    greet()
    plane_ref[...] = own_ref[...] + other_ref[...]
    plane_ends(plane_ref, ratio_ref, ends, None)
    edge_ref[0], edge_ref[1] = exchange(plane_ref.shape[0], ratio_ref[...], ends, *rest)


def join_kernel(own_ref, other_ref, ratio_ref, weight_ref, known_ref, plane_ref, edge_ref, ends, *rest):
    greet()
    half, _ = half_place()
    piece = own_ref.shape[1]
    plane_ref[:, pl.ds(pl.multiple_of(half * piece, piece), piece)] = own_ref[...]
    plane_ref[:, pl.ds(pl.multiple_of((1 - half) * piece, piece), piece)] = other_ref[...]
    plane_ends(plane_ref, ratio_ref, ends, weight_ref[...])
    before, above = exchange(plane_ref.shape[0], ratio_ref[...], ends, *rest)
    edge_ref[0] = known_ref[0] + before
    edge_ref[1] = known_ref[1] + above


def couple_kernel(
    plane_ref, again_ref, high_ref, low_ref, ratio_ref, edge_ref, couplings_ref, out_ref, held, chunk, carry
):
    shape = ratio_ref.shape
    strength = couplings_ref[shape[0] // 2]

    def finish(values):
        out_ref[...] = dot3((high_ref[...], low_ref[...]), values) + again_ref[...] * strength

    two_way(
        out_ref.shape[0], ratio_ref, edge_ref, held, chunk, carry,
        lambda row: jnp.broadcast_to(plane_ref[row : row + 1, :], shape), finish,
    )


def from_modes_kernel(modes_ref, plane_ref, weight_ref, high_ref, low_ref, ratio_ref, edge_ref, *rest, group):
    out_refs, (held, chunk, carry, *remote) = rest[:group], rest[group:]
    modes, share = ratio_ref.shape
    rows = plane_ref.shape[0]
    weight = weight_ref[...]
    step = pl.program_id(0)
    steps = pl.num_programs(0) // 2
    half, own = half_place()
    each = out_refs[0].shape[0]
    targets = [half * group + lax.rem(own + group - hop, group) for hop in range(1, group)]

    def copy(hop, index):
        outgoing, send_sem, recv_sem = remote
        place = pl.ds(pl.multiple_of(index * each, each), each)
        return pltpu.make_async_remote_copy(
            src_ref=outgoing.at[hop - 1, place],
            dst_ref=out_refs[hop].at[place],
            send_sem=send_sem.at[hop - 1, index],
            recv_sem=recv_sem.at[hop - 1, index],
            device_id={"lev": targets[hop - 1]},
            device_id_type=pl.DeviceIdType.MESH,
        )

    if group > 1:

        @pl.when(step == 0)
        def _():
            barrier = pltpu.get_barrier_semaphore()
            for target in targets:
                pl.semaphore_signal(barrier, inc=1, device_id={"lev": target}, device_id_type=pl.DeviceIdType.MESH)

        @pl.when(step == steps)
        def _():
            pl.semaphore_wait(pltpu.get_barrier_semaphore(), group - 1)

    def finish(values):
        result = dot3((high_ref[...], low_ref[...]), values)
        out_refs[0][...] = result[:each]
        index = 2 * steps - 1 - step
        for hop in range(1, group):
            remote[0][hop - 1, pl.ds(pl.multiple_of(index * each, each), each), :] = result[hop * each : (hop + 1) * each]
            copy(hop, index).start()

    two_way(
        rows, ratio_ref, edge_ref, held, chunk, carry,
        lambda row: modes_ref[row * modes : (row + 1) * modes, :] + weight * plane_ref[row : row + 1, :], finish,
    )

    if group > 1:

        @pl.when(step == 2 * steps - 1)
        def _():
            def settle(index, unused):
                for hop in range(1, group):
                    copy(hop, index).wait()
                return unused

            lax.fori_loop(0, steps, settle, 0)


def params(collective_id=None, room=VMEM_BYTES):
    if collective_id is None:
        return pltpu.CompilerParams(vmem_limit_bytes=room)
    return pltpu.CompilerParams(vmem_limit_bytes=room, collective_id=collective_id, has_side_effects=True)


def exchange_scratch(shape, row_devices):
    pairs = row_devices // 2
    two = (2,) + shape
    return [pltpu.VMEM(two, f32)] * 3 + [
        pltpu.VMEM((pairs - 1,) + two, f32),
        pltpu.SemaphoreType.DMA((pairs,)),
        pltpu.SemaphoreType.DMA((pairs,)),
    ]


def cost(flops, moved):
    return pl.CostEstimate(flops=int(flops), bytes_accessed=int(moved), transcendentals=0)


def whole(shape):
    return pl.BlockSpec(shape, lambda *index: (0,) * len(shape))


def struct(*shape):
    return jax.ShapeDtypeStruct(shape, f32)


def body(source, solid, couplings):
    row_count, levels, length = source.shape
    lev_devices = lax.axis_size("lev")
    row_devices = lax.axis_size("rows")
    group = lev_devices // 2
    share = length // group
    piece = share // 2
    width = length // PARTS
    half_levels = levels * group
    all_levels = 2 * half_levels
    tile = 64 if row_count % 64 == 0 else BY
    size = source.size

    def passed(value, shift):
        pairs = [
            (side * group + place, side * group + (place + shift) % group) for side in range(2) for place in range(group)
        ]
        return lax.ppermute(value, "lev", pairs)

    def across_halves(value):
        return lax.ppermute(value, "lev", [(place, (place + group) % lev_devices) for place in range(lev_devices)])

    blocks, eigen_x = x_tables(length)
    forward_table = blocks.astype(np.float32)
    backward_table = np.swapaxes(blocks, 1, 2).astype(np.float32)
    groups = tile // BY * 8
    table = whole(blocks.shape)
    part_spec = pl.BlockSpec((tile * levels, share), lambda i: (i, 0))
    field_spec = pl.BlockSpec((tile, levels, length), lambda i: (i, 0, 0))
    mixed = pltpu.VMEM((PARTS // 2, levels * tile, 2 * width), f32)
    halves = [pltpu.VMEM(blocks.shape, bf16)] * 2
    spectral = pl.pallas_call(
        forward_kernel,
        grid=(row_count // tile,),
        in_specs=[field_spec, pl.BlockSpec((tile // BY, levels, length // BX), lambda i: (i, 0, 0)), table],
        out_specs=[part_spec] * group,
        out_shape=[struct(row_count * levels, share)] * group,
        scratch_shapes=[pltpu.VMEM((groups, length), f32), mixed] + halves,
        compiler_params=params(room=ALL_VMEM_BYTES),
        cost_estimate=cost(6 * size * 2 * width, 8 * size),
        name="forward_x",
    )(source, solid, forward_table)
    sections = [spectral[0]] + [passed(spectral[shift], shift) for shift in range(1, group)]

    chunk = max(BY, 256 // half_levels)
    thin = min(row_count, max(BY, 512 // all_levels))
    wide = min(row_count, max(BY, 512 // half_levels))
    rows = chunk * half_levels
    plane_rows = thin * all_levels
    wide_rows = wide * half_levels
    in_smem = pl.BlockSpec(memory_space=pltpu.SMEM)
    built = [(rows, rows)] * 4 + [(wide, wide_rows)] * 2 + [(thin, plane_rows)] * 2
    *matrices, ratio, full_ratio, weight = pl.pallas_call(
        functools.partial(levels_kernel, group=group),
        in_specs=[in_smem, pl.BlockSpec(memory_space=pltpu.VMEM)],
        out_shape=[jax.ShapeDtypeStruct(each, bf16) for each in built]
        + [struct(half_levels, share), struct(all_levels, piece), struct(half_levels, share)],
        compiler_params=params(room=ALL_VMEM_BYTES),
        name="levels",
    )(couplings, eigen_x[None, :])
    to_modes, from_modes, to_edge, to_jump = (matrices[2 * index : 2 * index + 2] for index in range(4))

    steps = row_count // chunk
    plane_steps = row_count // thin
    wide_steps = row_count // wide
    shape = (half_levels, share)
    plane_shape = (all_levels, piece)
    modes_shape = struct(row_count * half_levels, share)
    section_spec = pl.BlockSpec((chunk * levels, share), lambda i: (i, 0))

    def ahead(count):
        return lambda i: (jnp.minimum(i, count - 1), 0)

    def behind(count):
        return lambda i: (jnp.minimum(2 * count - 1 - i, count - 1), 0)

    def scratch(rows, shape):
        return [pltpu.VMEM((row_count * shape[0], shape[1]), f32), pltpu.VMEM((rows, shape[1]), f32), pltpu.VMEM(shape, f32)]

    modes, edge = pl.pallas_call(
        to_modes_kernel,
        grid=(steps,),
        in_specs=[section_spec] * group + [whole((rows, rows))] * 2 + [whole(shape)],
        out_specs=[pl.BlockSpec((rows, share), lambda i: (i, 0)), whole((2,) + shape)],
        out_shape=[modes_shape, struct(2, *shape)],
        scratch_shapes=[pltpu.VMEM(shape, f32)] + exchange_scratch(shape, row_devices),
        compiler_params=params(0, ALL_VMEM_BYTES),
        cost_estimate=cost(6 * size * rows, 8 * size),
        name="to_modes",
    )(*sections, *to_modes, ratio)

    kept, sent = pl.pallas_call(
        interface_kernel,
        grid=(2 * wide_steps,),
        in_specs=[pl.BlockSpec((wide_rows, share), ahead(wide_steps))] + [whole((wide, wide_rows))] * 2 + [whole(shape), whole((2,) + shape)],
        out_specs=[pl.BlockSpec((wide, piece), behind(wide_steps))] * 2,
        out_shape=[struct(row_count, piece)] * 2,
        scratch_shapes=scratch(wide_rows, shape) + [pltpu.VMEM((wide, share), f32)],
        compiler_params=params(),
        cost_estimate=cost(6 * size * chunk, 5 * size),
        name="interface",
    )(modes, *to_edge, ratio, edge)

    plane, plane_edge = pl.pallas_call(
        sum_kernel,
        out_shape=[struct(row_count, piece), struct(2, *plane_shape)],
        scratch_shapes=exchange_scratch(plane_shape, row_devices),
        compiler_params=params(1),
        name="plane_sum",
    )(kept, across_halves(sent), full_ratio)

    moved = pl.pallas_call(
        couple_kernel,
        grid=(2 * plane_steps,),
        in_specs=[
            pl.BlockSpec((thin, piece), ahead(plane_steps)),
            pl.BlockSpec((thin, piece), behind(plane_steps)),
            whole((thin, plane_rows)),
            whole((thin, plane_rows)),
            whole(plane_shape),
            whole((2,) + plane_shape),
            in_smem,
        ],
        out_specs=pl.BlockSpec((thin, piece), behind(plane_steps)),
        out_shape=struct(row_count, piece),
        scratch_shapes=scratch(plane_rows, plane_shape),
        compiler_params=params(),
        cost_estimate=cost(6 * size * thin, 2 * size),
        name="couple",
    )(plane, plane, *to_jump, full_ratio, plane_edge, couplings)

    joined, edge = pl.pallas_call(
        join_kernel,
        out_shape=[struct(row_count, share), struct(2, *shape)],
        scratch_shapes=exchange_scratch(shape, row_devices),
        compiler_params=params(2),
        name="plane_join",
    )(moved, across_halves(moved), ratio, weight, edge)

    outgoing = [
        pltpu.VMEM((group - 1, row_count * levels, share), f32),
        pltpu.SemaphoreType.DMA((group - 1, steps)),
        pltpu.SemaphoreType.DMA((group - 1, steps)),
    ]
    returned = pl.pallas_call(
        functools.partial(from_modes_kernel, group=group),
        grid=(2 * steps,),
        in_specs=[pl.BlockSpec((rows, share), ahead(steps)), pl.BlockSpec((chunk, share), ahead(steps)), whole(shape)]
        + [whole((rows, rows))] * 2
        + [whole(shape), whole((2,) + shape)],
        out_specs=[pl.BlockSpec((chunk * levels, share), behind(steps))] + [pl.BlockSpec(memory_space=pl.ANY)] * (group - 1),
        out_shape=[struct(row_count * levels, share)] * group,
        scratch_shapes=scratch(rows, shape) + (outgoing if group > 1 else []),
        compiler_params=params(3 if group > 1 else None, ALL_VMEM_BYTES),
        cost_estimate=cost(6 * size * rows, 8 * size),
        name="from_modes",
    )(modes, joined, weight, *from_modes, ratio, edge)
    return pl.pallas_call(
        backward_kernel,
        grid=(row_count // tile,),
        in_specs=[part_spec] * group + [table],
        out_specs=field_spec,
        out_shape=struct(*source.shape),
        scratch_shapes=[mixed] + halves,
        compiler_params=params(room=ALL_VMEM_BYTES),
        cost_estimate=cost(6 * size * 2 * width, 8 * size),
        name="backward_x",
    )(*returned, backward_table)


def solution(mesh):
    return jax.shard_map(
        body,
        mesh=mesh,
        in_specs=(P("rows", "lev", None), P("rows", "lev", None), P()),
        out_specs=P("rows", "lev", None),
        check_vma=False,
    )
```

```python
import functools
import math

import numpy as np

import jax
import jax.numpy as jnp
from jax import lax
from jax.experimental import pallas as pl
from jax.experimental.pallas import tpu as pltpu
from jax.sharding import PartitionSpec as P

BY = 8
BX = 64
PARTS = 16
VMEM_BYTES = 48 * 1024 * 1024
ALL_VMEM_BYTES = 60 * 1024 * 1024

f32 = jnp.float32
highest = lax.Precision.HIGHEST
bf16 = jnp.bfloat16


def split(values):
    high = values.astype(bf16)
    low = (values - high.astype(f32)).astype(bf16)
    return high, low


def dot3(left, right):
    dot = functools.partial(jnp.dot, preferred_element_type=f32)
    return dot(left[0], right[0]) + (dot(left[0], right[1]) + dot(left[1], right[0]))


@functools.lru_cache(None)
def x_tables(length):
    width = length // PARTS
    half = PARTS // 2
    place = np.arange(width)
    blocks = np.zeros((half, 2 * width, 2 * width))
    slots = np.zeros((half, 2 * width))
    inner = math.sqrt(2.0 / length)
    edge = math.sqrt(1.0 / length)

    def angle(freq):
        return 2.0 * math.pi * (np.outer(place, freq) % length) / length

    low = PARTS * np.arange(width // 2 + 1)
    weight = np.where((low == 0) | (low == length // 2), edge, inner)
    cosines = np.cos(angle(low)) * weight
    sines = np.sin(angle(low[1:-1])) * inner
    blocks[0, :width, :width] = np.concatenate([cosines, sines], 1)
    slots[0, :width] = np.concatenate([low, low[1:-1]])
    middle = half + PARTS * np.arange(width // 2)
    blocks[0, width:, width:] = np.concatenate([np.cos(angle(middle)), np.sin(angle(middle))], 1) * inner
    slots[0, width:] = np.concatenate([middle, middle])
    for first in range(1, half):
        freq = first + PARTS * np.arange(width)
        turn = angle(freq)
        cosines, sines = np.cos(turn) * inner, np.sin(turn) * inner
        blocks[first] = np.block([[cosines, -sines], [sines, cosines]])
        slots[first] = np.concatenate([freq, freq])
    eigen = 4.0 * np.sin(math.pi * slots.reshape(-1) / length) ** 2
    return blocks, eigen.astype(np.float32)


def turn(index):
    return math.cos(2.0 * math.pi * index / PARTS), math.sin(2.0 * math.pi * index / PARTS)


def stage(x):
    s = [x[b] + x[b + 8] for b in range(8)]
    d = [x[b] - x[b + 8] for b in range(8)]
    out = [None] * 8
    minus = [d[b] - d[8 - b] for b in range(1, 4)]
    plus = [d[b] + d[8 - b] for b in range(1, 4)]
    for first in (1, 3, 5, 7):
        real = d[0]
        imag = d[4] * (-turn(4 * first)[1])
        for b in (1, 2, 3):
            cosine, sine = turn(b * first)
            real = real + minus[b - 1] * cosine
            imag = imag - plus[b - 1] * sine
        out[first] = (real, imag)
    ss = [s[b] + s[b + 4] for b in range(4)]
    sd = [s[b] - s[b + 4] for b in range(4)]
    root = math.sqrt(0.5)
    m = (sd[1] - sd[3]) * root
    p = (sd[1] + sd[3]) * root
    out[2] = (sd[0] + m, -p - sd[2])
    out[6] = (sd[0] - m, sd[2] - p)
    out[4] = (ss[0] - ss[2], ss[3] - ss[1])
    even, odd = ss[0] + ss[2], ss[1] + ss[3]
    out[0] = (even + odd, even - odd)
    return out


def unstage(y):
    root = math.sqrt(0.5)
    even, odd = y[0][0] + y[0][1], y[0][0] - y[0][1]
    ss = [even + y[4][0], odd - y[4][1], even - y[4][0], odd + y[4][1]]
    m = (y[2][0] - y[6][0]) * root
    p = (y[2][1] + y[6][1]) * root
    sd = [y[2][0] + y[6][0], m - p, y[6][1] - y[2][1], -m - p]
    s = [ss[b] + sd[b] for b in range(4)] + [ss[b] - sd[b] for b in range(4)]
    d = [None] * 8
    d[0] = (y[1][0] + y[3][0]) + (y[5][0] + y[7][0])
    d[4] = (y[3][1] - y[1][1]) + (y[7][1] - y[5][1])
    for b in (1, 2, 3):
        real = None
        imag = None
        for first in (1, 3, 5, 7):
            cosine, sine = turn(b * first)
            term, other = y[first][0] * cosine, y[first][1] * sine
            real = term if real is None else real + term
            imag = other if imag is None else imag + other
        d[b] = real - imag
        d[8 - b] = -real - imag
    return [s[b] + d[b] for b in range(8)] + [s[b] - d[b] for b in range(8)]


def half_place():
    group = lax.axis_size("lev") // 2
    me = lax.axis_index("lev")
    return me // group, me % group


def block_of(index, share, length):
    blocks = PARTS // 2
    _, own = half_place()
    return lax.rem(index + own * (share * blocks // length), blocks)


def keep_split(table_ref, high_ref, low_ref):
    @pl.when(pl.program_id(0) == 0)
    def _():
        for block in range(table_ref.shape[0]):
            high_ref[block], low_ref[block] = split(table_ref[block])


def forward_kernel(x_ref, solid_ref, table_ref, *rest):
    out_refs, (kept, mixed, high_ref, low_ref) = rest[:-4], rest[-4:]
    rows, levels, length = x_ref.shape
    width = length // PARTS
    share = out_refs[0].shape[1]
    pair = 8 // levels
    keep_split(table_ref, high_ref, low_ref)
    shape = (length // BX, length)
    first = lax.broadcasted_iota(jnp.int32, shape, 0) * BX
    lane = lax.broadcasted_iota(jnp.int32, shape, 1)
    spread = jnp.where((lane >= first) & (lane < first + BX), 1.0, 0.0).astype(bf16)
    keep = (1 - solid_ref[...]).astype(f32)
    keep = jnp.concatenate([keep] * pair, 1).reshape(kept.shape[0], length // BX)
    kept[...] = jnp.dot(keep.astype(bf16), spread, preferred_element_type=f32)

    def group(index, unused):
        mask = kept[pl.ds(pl.multiple_of(index * 8, 8), 8), :]
        for part in range(BY // pair):
            row = index * BY + part * pair
            x = [
                x_ref[pl.ds(row, pair), :, pl.ds(b * width, width)].reshape(8, width)
                * mask[:, b * width : (b + 1) * width]
                for b in range(PARTS)
            ]
            base = pl.multiple_of(row * levels, 8)
            for block, (real, imag) in enumerate(stage(x)):
                mixed[block, pl.ds(base, 8), :width] = real
                mixed[block, pl.ds(base, 8), width:] = imag
        return unused

    lax.fori_loop(0, rows // BY, group, 0)
    for index in range(PARTS // 2):
        block = block_of(index, share, length)
        product = dot3(split(mixed[block]), (high_ref[block], low_ref[block]))
        target, offset = divmod(2 * index * width, share)
        out_refs[target][:, offset : offset + 2 * width] = product


def backward_kernel(*refs):
    x_refs, (table_ref, out_ref, mixed, high_ref, low_ref) = refs[:-5], refs[-5:]
    rows, levels, length = out_ref.shape
    width = length // PARTS
    share = x_refs[0].shape[1]
    pair = 8 // levels
    keep_split(table_ref, high_ref, low_ref)
    for index in range(PARTS // 2):
        block = block_of(index, share, length)
        source, offset = divmod(2 * index * width, share)
        values = split(x_refs[source][:, offset : offset + 2 * width])
        mixed[block] = dot3(values, (high_ref[block], low_ref[block]))

    def group(index, unused):
        row = index * pair
        base = pl.multiple_of(index * 8, 8)
        y = [
            (mixed[block, pl.ds(base, 8), :width], mixed[block, pl.ds(base, 8), width:])
            for block in range(PARTS // 2)
        ]
        for b, value in enumerate(unstage(y)):
            out_ref[pl.ds(row, pair), :, pl.ds(b * width, width)] = value.reshape(pair, levels, width)
        return unused

    lax.fori_loop(0, rows // pair, group, 0, unroll=4)


def jacobi(start, sizes, top):
    lanes = start.shape[1]
    lane = lax.broadcasted_iota(jnp.int32, (1, lanes), 1)
    in_first = lane < sizes[0]
    local = jnp.where(in_first, lane, lane - sizes[0])
    count = jnp.where(in_first, sizes[0], sizes[1])

    def rotate(values, parity):
        is_left = local % 2 == parity
        alone = (lane >= sum(sizes)) | (is_left & (local == count - 1)) | (jnp.logical_not(is_left) & (local == 0))
        partner = jnp.where(is_left, pltpu.roll(values, lanes - 1, 1), pltpu.roll(values, 1, 1))
        head = values[:top]
        head_partner = partner[:top]
        own = jnp.sum(head * head, axis=0, keepdims=True)
        other = jnp.sum(head_partner * head_partner, axis=0, keepdims=True)
        cross = jnp.sum(head * head_partner, axis=0, keepdims=True)
        delta = other - own
        sign = jnp.where((delta > 0) | ((delta == 0) & is_left), 1.0, -1.0)
        bottom = jnp.abs(delta) + jnp.sqrt(delta * delta + 4.0 * cross * cross)
        tangent = 2.0 * cross * sign / jnp.maximum(bottom, 1e-30)
        cosine = 1.0 / jnp.sqrt(1.0 + tangent * tangent)
        sine = cosine * tangent
        angle = jnp.where(alone, 0.0, jnp.abs(cross) * lax.rsqrt(jnp.maximum(own * other, 1e-30)))
        return jnp.where(alone, values, cosine * partner + sine * values), angle

    def sweep(carry):
        values, done, unused = carry
        worst = jnp.zeros((1, lanes), f32)
        for step in range(max(sizes)):
            values, angle = rotate(values, step % 2)
            worst = jnp.maximum(worst, angle)
        return values, done + 1, jnp.max(worst)

    def going(carry):
        return (carry[2] > 1e-4) & (carry[1] < 20)

    return lax.while_loop(going, sweep, (start, jnp.int32(0), jnp.float32(1.0)))[0]


def levels_kernel(
    couplings_ref, eigen_ref, to_high, to_low, from_high, from_low, edge_high, edge_low, jump_high, jump_low,
    ratio_ref, full_ref, weight_ref, *, group,
):
    modes, share = ratio_ref.shape
    all_modes, piece = full_ref.shape
    lanes = 128
    rows = to_high.shape[0]
    chunk = rows // modes
    levels = modes // group
    top = -(-(all_modes + 1) // 8) * 8
    low = -(-all_modes // 8) * 8
    half, own = half_place()
    exact = functools.partial(jnp.dot, precision=highest, preferred_element_type=f32)

    def iota(shape, axis):
        return lax.broadcasted_iota(jnp.int32, shape, axis)

    def spot(condition):
        return jnp.where(condition, 1.0, 0.0)

    row, lane = iota((top, lanes), 0), iota((top, lanes), 1)
    in_first = lane < all_modes
    local = jnp.where(in_first, lane, lane - all_modes)
    used = lane < all_modes + modes
    weights = jnp.zeros((top, lanes), f32)
    for place in range(all_modes + 1):
        weights = jnp.where(in_first & (row == place), couplings_ref[place], weights)
    cut = jnp.where(half == 0, modes, 0)
    for place in range(modes + 1):
        value = couplings_ref[half * modes + place] * jnp.where(cut == place, 2.0, 1.0)
        weights = jnp.where(jnp.logical_not(in_first) & (row == place), value, weights)
    head = jnp.sqrt(weights) * (spot(used & (row == local)) - spot(used & (row == local + 1)))
    tail = spot(used & (row == local))[:low]
    turned = jacobi(jnp.concatenate([head, tail], 0), (all_modes, modes), top)
    head, vectors = turned[:top], turned[top : top + low]
    values = jnp.sum(head * head, axis=0, keepdims=True)

    at, to = iota((rows, low), 0), iota((rows, low), 1)
    section = at // (chunk * levels)
    level = lax.rem(own - section + group, group) * levels + lax.rem(at, levels)
    pick = spot(to == level)
    column = iota((lanes, rows), 1)
    place = spot(iota((lanes, rows), 0) == all_modes + lax.rem(column, modes))
    spread = exact(exact(pick, vectors), place)
    at, to = iota((rows, rows), 0), iota((rows, rows), 1)
    spread = jnp.where(lax.rem(at // levels, chunk) == to // modes, spread, 0.0)
    from_high[...], from_low[...] = split(spread)
    to_high[...], to_low[...] = split(spread.T)

    edge = jnp.where(half == 0, vectors[modes - 1 : modes], vectors[0:1])
    wide, wide_rows = edge_high.shape
    column = iota((lanes, wide_rows), 1)
    place = spot(iota((lanes, wide_rows), 0) == all_modes + lax.rem(column, modes))
    line = exact(jnp.broadcast_to(edge, (8, lanes)), place)[0:1]
    at, to = iota((wide, wide_rows), 0), iota((wide, wide_rows), 1)
    edge_high[...], edge_low[...] = split(jnp.where(at == to // modes, line, 0.0))
    jump = couplings_ref[modes] * (vectors[modes - 1 : modes] + vectors[modes : modes + 1])
    thin, plane_rows = jump_high.shape
    column = iota((lanes, plane_rows), 1)
    place = spot(iota((lanes, plane_rows), 0) == lax.rem(column, all_modes))
    line = exact(jnp.broadcast_to(jump * jump, (8, lanes)), place)[0:1]
    at, to = iota((thin, plane_rows), 0), iota((thin, plane_rows), 1)
    jump_high[...], jump_low[...] = split(jnp.where(at == to // all_modes, line, 0.0))

    def decay(count, first, mine):
        at, to = iota((count, lanes), 0), iota((count, lanes), 1)
        own_values = jnp.sum(jnp.where(to == at + first, values, 0.0), axis=1, keepdims=True)
        sigma = own_values + mine
        return 1.0 / (1.0 + 0.5 * sigma + jnp.sqrt(sigma + 0.25 * sigma * sigma))

    start = pl.multiple_of(own * share, share)
    ratio_ref[...] = decay(modes, all_modes, eigen_ref[:, pl.ds(start, share)])
    full_ref[...] = decay(all_modes, 0, eigen_ref[:, pl.ds(pl.multiple_of(start + half * piece, piece), piece)])
    at, to = iota((modes, lanes), 0), iota((modes, lanes), 1)
    weight = jnp.sum(jnp.where(to == at + all_modes, edge, 0.0), axis=1, keepdims=True)
    weight_ref[...] = jnp.broadcast_to(weight, (modes, share))


def power(value, exponent):
    result = None
    while exponent:
        if exponent % 2:
            result = value if result is None else result * value
        value = value * value
        exponent //= 2
    return result


def rows_place():
    me = lax.axis_index("rows")
    return me // 2, lax.rem(me, 2), lax.axis_size("rows") // 2


def partners():
    pair, place, pairs = rows_place()
    return [2 * pair + 1 - place] + [2 * lax.rem(pair + hop, pairs) + place for hop in range(1, pairs)]


def greet():
    barrier = pltpu.get_barrier_semaphore()
    for partner in partners():
        pl.semaphore_signal(barrier, inc=1, device_id={"rows": partner}, device_id_type=pl.DeviceIdType.MESH)


def exchange(row_count, ratio, ends, mate, total, others, send_sem, recv_sem):
    pair, place, pairs = rows_place()
    targets = partners()
    pl.semaphore_wait(pltpu.get_barrier_semaphore(), pairs)

    def copy(index, source, target):
        return pltpu.make_async_remote_copy(
            src_ref=source,
            dst_ref=target,
            send_sem=send_sem.at[index],
            recv_sem=recv_sem.at[index],
            device_id={"rows": targets[index]},
            device_id_type=pl.DeviceIdType.MESH,
        )

    near = copy(0, ends, mate)
    near.start()
    across = power(ratio, row_count)
    twice = across * across
    closing = 1.0 / (1.0 - power(twice, pairs))
    near.wait()
    is_first = place == 0
    first_f, last_f = jnp.where(is_first, ends[0], mate[0]), jnp.where(is_first, mate[0], ends[0])
    first_b, last_b = jnp.where(is_first, ends[1], mate[1]), jnp.where(is_first, mate[1], ends[1])
    total[0] = last_f + across * first_f
    total[1] = first_b + across * last_b
    far = [copy(hop, total, others.at[hop - 1]) for hop in range(1, pairs)]
    for one in far:
        one.start()
    for one in far:
        one.wait()
    before, after = total[0], total[1]
    for hop in range(pairs - 1, 0, -1):
        before = before * twice + others[hop - 1, 0]
        after = after * twice + others[pairs - hop - 1, 1]
    before, after = before * closing, after * closing
    before = jnp.where(is_first, before, first_f + across * before)
    after = jnp.where(is_first, last_b + across * after, after)
    last = ends[0] + across * before
    above = ratio * (ratio * last + after) / (1.0 - ratio * ratio)
    return before, above


def to_modes_kernel(*refs):
    x_refs = refs[:-12]
    high_ref, low_ref, ratio_ref, modes_ref, edge_ref, scale_ref, ends, mate, total, others, send_sem, recv_sem = refs[-12:]
    modes, share = ratio_ref.shape
    step = pl.program_id(0)

    @pl.when(step == 0)
    def _():
        greet()
        ends[...] = jnp.zeros(ends.shape, f32)
        scale_ref[...] = jnp.ones(scale_ref.shape, f32)

    block = high_ref.shape[0]
    each = block // len(x_refs)
    for part in range(modes_ref.shape[0] // block):
        values = jnp.concatenate([x_ref[part * each : (part + 1) * each] for x_ref in x_refs], 0)
        modes_ref[part * block : (part + 1) * block] = dot3((high_ref[...], low_ref[...]), split(values))
    ratio = ratio_ref[...]
    first, last, scale = ends[0], ends[1], scale_ref[...]
    rows = modes_ref.shape[0] // modes
    for row in range(rows):
        current = modes_ref[row * modes : (row + 1) * modes, :]
        first = first * ratio + current
        last = last + scale * current
        scale = scale * ratio
    ends[0] = first
    ends[1] = last
    scale_ref[...] = scale

    @pl.when(step == pl.num_programs(0) - 1)
    def _():
        count = rows * pl.num_programs(0)
        edge_ref[0], edge_ref[1] = exchange(count, ratio_ref[...], ends, mate, total, others, send_sem, recv_sem)


def two_way(rows, ratio_ref, edge_ref, held, chunk, carry, source, finish):
    step = pl.program_id(0)
    steps = pl.num_programs(0) // 2
    modes = ratio_ref.shape[0]
    ratio = ratio_ref[...]

    @pl.when(step == 0)
    def _():
        carry[...] = edge_ref[0]

    @pl.when(step == steps)
    def _():
        carry[...] = edge_ref[1]

    @pl.when(step < steps)
    def _():
        base = pl.multiple_of(step * rows * modes, rows * modes)
        value = carry[...]
        for row in range(rows):
            value = value * ratio + source(row)
            held[pl.ds(base + row * modes, modes), :] = value
        carry[...] = value

    @pl.when(step >= steps)
    def _():
        base = pl.multiple_of((2 * steps - 1 - step) * rows * modes, rows * modes)
        value = carry[...]
        for row in reversed(range(rows)):
            value = (value + held[pl.ds(base + row * modes, modes), :]) * ratio
            chunk[row * modes : (row + 1) * modes, :] = value
        carry[...] = value
        finish(split(chunk[...]))


def interface_kernel(modes_ref, high_ref, low_ref, ratio_ref, edge_ref, keep_ref, send_ref, held, chunk, carry, line):
    modes = ratio_ref.shape[0]
    piece = keep_ref.shape[1]
    half, _ = half_place()

    def finish(values):
        line[...] = dot3((high_ref[...], low_ref[...]), values)
        keep_ref[...] = line[:, pl.ds(pl.multiple_of(half * piece, piece), piece)]
        send_ref[...] = line[:, pl.ds(pl.multiple_of((1 - half) * piece, piece), piece)]

    two_way(
        keep_ref.shape[0], ratio_ref, edge_ref, held, chunk, carry,
        lambda row: modes_ref[row * modes : (row + 1) * modes, :], finish,
    )


def plane_ends(plane_ref, ratio_ref, ends, weight):
    rows = plane_ref.shape[0]
    shape = ratio_ref.shape
    ratio = ratio_ref[...]

    def group(index, carry):
        first, last, scale = carry
        lines = plane_ref[pl.ds(pl.multiple_of(index * BY, BY), BY), :]
        for row in range(BY):
            current = jnp.broadcast_to(lines[row : row + 1], shape)
            first = first * ratio + current
            last = last + scale * current
            scale = scale * ratio
        return first, last, scale

    zero = jnp.zeros(shape, f32)
    first, last, _ = lax.fori_loop(0, rows // BY, group, (zero, zero, jnp.ones(shape, f32)))
    ends[0] = first if weight is None else first * weight
    ends[1] = last if weight is None else last * weight


def sum_kernel(own_ref, other_ref, ratio_ref, plane_ref, edge_ref, ends, *rest):
    greet()
    plane_ref[...] = own_ref[...] + other_ref[...]
    plane_ends(plane_ref, ratio_ref, ends, None)
    edge_ref[0], edge_ref[1] = exchange(plane_ref.shape[0], ratio_ref[...], ends, *rest)


def join_kernel(own_ref, other_ref, ratio_ref, weight_ref, known_ref, plane_ref, edge_ref, ends, *rest):
    greet()
    half, _ = half_place()
    piece = own_ref.shape[1]
    plane_ref[:, pl.ds(pl.multiple_of(half * piece, piece), piece)] = own_ref[...]
    plane_ref[:, pl.ds(pl.multiple_of((1 - half) * piece, piece), piece)] = other_ref[...]
    plane_ends(plane_ref, ratio_ref, ends, weight_ref[...])
    before, above = exchange(plane_ref.shape[0], ratio_ref[...], ends, *rest)
    edge_ref[0] = known_ref[0] + before
    edge_ref[1] = known_ref[1] + above


def couple_kernel(
    plane_ref, again_ref, high_ref, low_ref, ratio_ref, edge_ref, couplings_ref, out_ref, held, chunk, carry
):
    shape = ratio_ref.shape
    strength = couplings_ref[shape[0] // 2]

    def finish(values):
        out_ref[...] = dot3((high_ref[...], low_ref[...]), values) + again_ref[...] * strength

    two_way(
        out_ref.shape[0], ratio_ref, edge_ref, held, chunk, carry,
        lambda row: jnp.broadcast_to(plane_ref[row : row + 1, :], shape), finish,
    )


def from_modes_kernel(modes_ref, plane_ref, weight_ref, high_ref, low_ref, ratio_ref, edge_ref, *rest, group):
    out_refs, (held, chunk, carry, *remote) = rest[:group], rest[group:]
    modes, share = ratio_ref.shape
    rows = plane_ref.shape[0]
    weight = weight_ref[...]
    step = pl.program_id(0)
    steps = pl.num_programs(0) // 2
    half, own = half_place()
    each = out_refs[0].shape[0]
    targets = [half * group + lax.rem(own + group - hop, group) for hop in range(1, group)]

    def copy(hop, index):
        outgoing, send_sem, recv_sem = remote
        place = pl.ds(pl.multiple_of(index * each, each), each)
        return pltpu.make_async_remote_copy(
            src_ref=outgoing.at[hop - 1, place],
            dst_ref=out_refs[hop].at[place],
            send_sem=send_sem.at[hop - 1, index],
            recv_sem=recv_sem.at[hop - 1, index],
            device_id={"lev": targets[hop - 1]},
            device_id_type=pl.DeviceIdType.MESH,
        )

    if group > 1:

        @pl.when(step == 0)
        def _():
            barrier = pltpu.get_barrier_semaphore()
            for target in targets:
                pl.semaphore_signal(barrier, inc=1, device_id={"lev": target}, device_id_type=pl.DeviceIdType.MESH)

        @pl.when(step == steps)
        def _():
            pl.semaphore_wait(pltpu.get_barrier_semaphore(), group - 1)

    def finish(values):
        result = dot3((high_ref[...], low_ref[...]), values)
        out_refs[0][...] = result[:each]
        index = 2 * steps - 1 - step
        for hop in range(1, group):
            remote[0][hop - 1, pl.ds(pl.multiple_of(index * each, each), each), :] = result[hop * each : (hop + 1) * each]
            copy(hop, index).start()

    two_way(
        rows, ratio_ref, edge_ref, held, chunk, carry,
        lambda row: modes_ref[row * modes : (row + 1) * modes, :] + weight * plane_ref[row : row + 1, :], finish,
    )

    if group > 1:

        @pl.when(step == 2 * steps - 1)
        def _():
            def settle(index, unused):
                for hop in range(1, group):
                    copy(hop, index).wait()
                return unused

            lax.fori_loop(0, steps, settle, 0)


def params(collective_id=None, room=VMEM_BYTES):
    if collective_id is None:
        return pltpu.CompilerParams(vmem_limit_bytes=room)
    return pltpu.CompilerParams(vmem_limit_bytes=room, collective_id=collective_id, has_side_effects=True)


def exchange_scratch(shape, row_devices):
    pairs = row_devices // 2
    two = (2,) + shape
    return [pltpu.VMEM(two, f32)] * 3 + [
        pltpu.VMEM((pairs - 1,) + two, f32),
        pltpu.SemaphoreType.DMA((pairs,)),
        pltpu.SemaphoreType.DMA((pairs,)),
    ]


def cost(flops, moved):
    return pl.CostEstimate(flops=int(flops), bytes_accessed=int(moved), transcendentals=0)


def whole(shape):
    return pl.BlockSpec(shape, lambda *index: (0,) * len(shape))


def struct(*shape):
    return jax.ShapeDtypeStruct(shape, f32)


def body(source, solid, couplings):
    row_count, levels, length = source.shape
    lev_devices = lax.axis_size("lev")
    row_devices = lax.axis_size("rows")
    group = lev_devices // 2
    share = length // group
    piece = share // 2
    width = length // PARTS
    half_levels = levels * group
    all_levels = 2 * half_levels
    tile = 64 if row_count % 64 == 0 else BY
    size = source.size

    def passed(value, shift):
        pairs = [
            (side * group + place, side * group + (place + shift) % group) for side in range(2) for place in range(group)
        ]
        return lax.ppermute(value, "lev", pairs)

    def across_halves(value):
        return lax.ppermute(value, "lev", [(place, (place + group) % lev_devices) for place in range(lev_devices)])

    blocks, eigen_x = x_tables(length)
    forward_table = blocks.astype(np.float32)
    backward_table = np.swapaxes(blocks, 1, 2).astype(np.float32)
    groups = tile // BY * 8
    table = whole(blocks.shape)
    part_spec = pl.BlockSpec((tile * levels, share), lambda i: (i, 0))
    field_spec = pl.BlockSpec((tile, levels, length), lambda i: (i, 0, 0))
    mixed = pltpu.VMEM((PARTS // 2, levels * tile, 2 * width), f32)
    halves = [pltpu.VMEM(blocks.shape, bf16)] * 2
    spectral = pl.pallas_call(
        forward_kernel,
        grid=(row_count // tile,),
        in_specs=[field_spec, pl.BlockSpec((tile // BY, levels, length // BX), lambda i: (i, 0, 0)), table],
        out_specs=[part_spec] * group,
        out_shape=[struct(row_count * levels, share)] * group,
        scratch_shapes=[pltpu.VMEM((groups, length), f32), mixed] + halves,
        compiler_params=params(room=ALL_VMEM_BYTES),
        cost_estimate=cost(6 * size * 2 * width, 8 * size),
        name="forward_x",
    )(source, solid, forward_table)
    sections = [spectral[0]] + [passed(spectral[shift], shift) for shift in range(1, group)]

    chunk = max(BY, 256 // half_levels)
    thin = min(row_count, max(BY, 512 // all_levels))
    wide = min(row_count, max(BY, 512 // half_levels))
    rows = chunk * half_levels
    plane_rows = thin * all_levels
    wide_rows = wide * half_levels
    in_smem = pl.BlockSpec(memory_space=pltpu.SMEM)
    built = [(rows, rows)] * 4 + [(wide, wide_rows)] * 2 + [(thin, plane_rows)] * 2
    *matrices, ratio, full_ratio, weight = pl.pallas_call(
        functools.partial(levels_kernel, group=group),
        in_specs=[in_smem, pl.BlockSpec(memory_space=pltpu.VMEM)],
        out_shape=[jax.ShapeDtypeStruct(each, bf16) for each in built]
        + [struct(half_levels, share), struct(all_levels, piece), struct(half_levels, share)],
        compiler_params=params(room=ALL_VMEM_BYTES),
        name="levels",
    )(couplings, eigen_x[None, :])
    to_modes, from_modes, to_edge, to_jump = (matrices[2 * index : 2 * index + 2] for index in range(4))

    steps = row_count // chunk
    plane_steps = row_count // thin
    wide_steps = row_count // wide
    shape = (half_levels, share)
    plane_shape = (all_levels, piece)
    modes_shape = struct(row_count * half_levels, share)

    def ahead(count):
        return lambda i: (jnp.minimum(i, count - 1), 0)

    def behind(count):
        return lambda i: (jnp.minimum(2 * count - 1 - i, count - 1), 0)

    def scratch(rows, shape):
        return [pltpu.VMEM((row_count * shape[0], shape[1]), f32), pltpu.VMEM((rows, shape[1]), f32), pltpu.VMEM(shape, f32)]

    double = 2 if steps % 2 == 0 else 1
    modes, edge = pl.pallas_call(
        to_modes_kernel,
        grid=(steps // double,),
        in_specs=[pl.BlockSpec((double * chunk * levels, share), lambda i: (i, 0))] * group + [whole((rows, rows))] * 2 + [whole(shape)],
        out_specs=[pl.BlockSpec((double * rows, share), lambda i: (i, 0)), whole((2,) + shape)],
        out_shape=[modes_shape, struct(2, *shape)],
        scratch_shapes=[pltpu.VMEM(shape, f32)] + exchange_scratch(shape, row_devices),
        compiler_params=params(0, ALL_VMEM_BYTES),
        cost_estimate=cost(6 * size * rows, 8 * size),
        name="to_modes",
    )(*sections, *to_modes, ratio)

    kept, sent = pl.pallas_call(
        interface_kernel,
        grid=(2 * wide_steps,),
        in_specs=[pl.BlockSpec((wide_rows, share), ahead(wide_steps))] + [whole((wide, wide_rows))] * 2 + [whole(shape), whole((2,) + shape)],
        out_specs=[pl.BlockSpec((wide, piece), behind(wide_steps))] * 2,
        out_shape=[struct(row_count, piece)] * 2,
        scratch_shapes=scratch(wide_rows, shape) + [pltpu.VMEM((wide, share), f32)],
        compiler_params=params(),
        cost_estimate=cost(6 * size * chunk, 5 * size),
        name="interface",
    )(modes, *to_edge, ratio, edge)

    plane, plane_edge = pl.pallas_call(
        sum_kernel,
        out_shape=[struct(row_count, piece), struct(2, *plane_shape)],
        scratch_shapes=exchange_scratch(plane_shape, row_devices),
        compiler_params=params(1),
        name="plane_sum",
    )(kept, across_halves(sent), full_ratio)

    moved = pl.pallas_call(
        couple_kernel,
        grid=(2 * plane_steps,),
        in_specs=[
            pl.BlockSpec((thin, piece), ahead(plane_steps)),
            pl.BlockSpec((thin, piece), behind(plane_steps)),
            whole((thin, plane_rows)),
            whole((thin, plane_rows)),
            whole(plane_shape),
            whole((2,) + plane_shape),
            in_smem,
        ],
        out_specs=pl.BlockSpec((thin, piece), behind(plane_steps)),
        out_shape=struct(row_count, piece),
        scratch_shapes=scratch(plane_rows, plane_shape),
        compiler_params=params(),
        cost_estimate=cost(6 * size * thin, 2 * size),
        name="couple",
    )(plane, plane, *to_jump, full_ratio, plane_edge, couplings)

    joined, edge = pl.pallas_call(
        join_kernel,
        out_shape=[struct(row_count, share), struct(2, *shape)],
        scratch_shapes=exchange_scratch(shape, row_devices),
        compiler_params=params(2),
        name="plane_join",
    )(moved, across_halves(moved), ratio, weight, edge)

    outgoing = [
        pltpu.VMEM((group - 1, row_count * levels, share), f32),
        pltpu.SemaphoreType.DMA((group - 1, steps)),
        pltpu.SemaphoreType.DMA((group - 1, steps)),
    ]
    returned = pl.pallas_call(
        functools.partial(from_modes_kernel, group=group),
        grid=(2 * steps,),
        in_specs=[pl.BlockSpec((rows, share), ahead(steps)), pl.BlockSpec((chunk, share), ahead(steps)), whole(shape)]
        + [whole((rows, rows))] * 2
        + [whole(shape), whole((2,) + shape)],
        out_specs=[pl.BlockSpec((chunk * levels, share), behind(steps))] + [pl.BlockSpec(memory_space=pl.ANY)] * (group - 1),
        out_shape=[struct(row_count * levels, share)] * group,
        scratch_shapes=scratch(rows, shape) + (outgoing if group > 1 else []),
        compiler_params=params(3 if group > 1 else None, ALL_VMEM_BYTES),
        cost_estimate=cost(6 * size * rows, 8 * size),
        name="from_modes",
    )(modes, joined, weight, *from_modes, ratio, edge)
    return pl.pallas_call(
        backward_kernel,
        grid=(row_count // tile,),
        in_specs=[part_spec] * group + [table],
        out_specs=field_spec,
        out_shape=struct(*source.shape),
        scratch_shapes=[mixed] + halves,
        compiler_params=params(room=ALL_VMEM_BYTES),
        cost_estimate=cost(6 * size * 2 * width, 8 * size),
        name="backward_x",
    )(*returned, backward_table)


def solution(mesh):
    return jax.shard_map(
        body,
        mesh=mesh,
        in_specs=(P("rows", "lev", None), P("rows", "lev", None), P()),
        out_specs=P("rows", "lev", None),
        check_vma=False,
    )
```
